128 devices in a mesh: ty: 8 (over z_hi, x), tx: 16 (over y, z_lo, core).
Axes of the slice: x: 4, y: 4, z: 4 (z_hi: 2, z_lo: 2; z = z_hi * 2 + z_lo), core: 2. Of those that a mesh axis runs over, the one named last changes fastest.
Arguments:
- object_slab: float32 [2, 2, 4096, 8192], P(None, None, 'ty', 'tx'), may hold values from -4 to 4
- probe_wave: float32 [2, 256, 256], replicated, may hold values from -5 to 5
- frames: float32 [768, 256, 256], P('tx'), may hold values from 0.05 to 8
- scan_tiles: int32 [768], replicated, may hold values from 0 to 127, as said below
- scan_offsets: int32 [768, 2], replicated, may hold values from 0 to 511, as said below
Outputs:
- new_object: float32 [2, 2, 4096, 8192], P(None, None, 'ty', 'tx')
- new_probe: float32 [2, 256, 256], replicated
The draws below stay inside these ranges and needn't reach their ends.
Inputs may be any that keep to these rules, and one draw needn't show every extreme that they name: `scan_tiles`: tiles are numbered row by row: tile row times 16 plus tile column. Every tile is named by at most 8 scan positions, and some tile by exactly 8. Within the frames of one owner (aligned blocks of 48 positions) no tile is named twice. `scan_offsets`: row offsets lie in 0 to 511 and column offsets in 0 to 511; windows may reach past the tile's lower and right edges.
All inputs are finite; a program needn't handle non-finite values.
Results may differ from the reference program's by a relative error of at most 0.0003.
Values sent between devices are 32-bit elements; how exact they have to be, the bound alone decides.
A program may use at most 192 MiB of HBM per device.

```python
import math
import jax
import jax.numpy as jnp
from jax import lax

P_SIZE = 256
S = 2
ITERS = 1
FR_TILE = 6
TR = 512
TC = 512
TILE_CAP = 8
FRAMES = 768
NR = 4096
NC = 8192
N_TY = 8
N_TX = 16


def draw_scan_tiles(key, part):
    key = jax.random.fold_in(key, 17)
    tile_count = N_TY * N_TX
    order_key, share_key = jax.random.split(key)
    shuffled = jax.random.permutation(order_key, tile_count)
    shares = jax.random.randint(share_key, (tile_count // 2,), 2 * FR_TILE - TILE_CAP, TILE_CAP + 1)
    partners = shuffled[1::2]
    inner = ((partners > 0) & (partners < tile_count - 1)).astype(jnp.int32)
    full_pair = jnp.argmax(inner).astype(jnp.int32)
    shares = shares.at[full_pair].set(TILE_CAP)
    counts = jnp.zeros((tile_count,), jnp.int32)
    counts = counts.at[shuffled[0::2]].set(shares).at[shuffled[1::2]].set(2 * FR_TILE - shares)
    running = jnp.cumsum(counts)
    frame_ids = jnp.arange(FRAMES, dtype=jnp.int32)
    owned = FRAMES // N_TX
    places = frame_ids % owned * N_TX + frame_ids // owned
    return jnp.sum((running[None, :] <= places[:, None]).astype(jnp.int32), axis=1).astype(jnp.int32)


def draw_scan_offsets(key, part):
    key = jax.random.fold_in(key, 29)
    first_key, second_key, third_key, fourth_key = jax.random.split(key, 4)
    row_part = jax.random.randint(first_key, (FRAMES,), 0, TR)
    col_part = jax.random.randint(second_key, (FRAMES,), 0, TC)
    row_pick = jax.random.randint(third_key, (), 0, FRAMES)
    col_pick = jax.random.randint(fourth_key, (), 0, FRAMES)
    row_part = row_part.at[row_pick].set(TR - 1).at[(row_pick + 1) % FRAMES].set(0)
    col_part = col_part.at[col_pick].set(TC - 1).at[(col_pick + 1) % FRAMES].set(0)
    return jnp.stack([row_part, col_part], axis=1).astype(jnp.int32)


def level_of(stream_key, extent, pieces, low, largest):
    def one(position, parts):
        heights = jax.random.uniform(jax.random.fold_in(jax.random.fold_in(stream_key, 6), position), (parts,), jnp.float32, low / len(pieces), largest / len(pieces))
        return jnp.repeat(jnp.exp(heights), extent[position] // parts).reshape((-1,) + (1,) * (len(extent) - position - 1))

    gain = one(*pieces[0])
    for cut in pieces[1:]:
        gain = gain * one(*cut)
    return gain


def centred(rng, extent, deviation, most, cuts=(), kind=jnp.bfloat16):
    gain = level_of(rng, extent, cuts, -0.22, 0.18) if cuts else 1.0
    entries = jax.random.normal(rng, extent, jnp.float32) * deviation * gain
    return jnp.minimum(jnp.maximum(entries, -most), most).astype(kind)


def setup_inputs(seed: int = 0) -> dict:
    arg_keys = jax.random.split(jax.random.key(seed), 6)
    object_slab = centred(arg_keys[0], (S, 2, NR, NC), 0.7, 4.0, ((2, 8), (3, 16)), jnp.float32)
    probe_wave = centred(arg_keys[1], (2, P_SIZE, P_SIZE), 1.0, 5.0, (), jnp.float32)
    frames = jnp.clip(jnp.exp(math.log(8.0) - 5.075174 * jax.random.uniform(arg_keys[2], (FRAMES, P_SIZE, P_SIZE), jnp.float32) ** level_of(arg_keys[2], (FRAMES, P_SIZE, P_SIZE), ((0, 16),), -0.2, 0.2)), 0.05, 8.0)
    scan_tiles = draw_scan_tiles(jax.random.fold_in(arg_keys[5], 71), 0)
    scan_offsets = draw_scan_offsets(jax.random.fold_in(arg_keys[5], 71), 0)
    return {"object_slab": object_slab, "probe_wave": probe_wave, "frames": frames, "scan_tiles": scan_tiles, "scan_offsets": scan_offsets}


BACKGROUND = 0.5
FRESNEL = 0.25
OBJECT_RATE = 0.25
PROBE_RATE = 4.0

def kernel_phase(points):
    indices = jnp.arange(points, dtype=jnp.int32)
    frequency = (indices + points // 2) % points - points // 2
    square = (frequency * frequency).astype(jnp.float32)
    return -jnp.pi * FRESNEL / points * (square[:, None] + square[None, :])

def frame_loss(window, probe_now, measured):
    phases = kernel_phase(probe_now.shape[-1])
    kernel = lax.complex(jnp.cos(phases), jnp.sin(phases))
    exit_wave = lax.complex(probe_now[0], probe_now[1]) * lax.complex(window[0, 0], window[0, 1])
    for slice_index in range(1, window.shape[0]):
        spectrum = jnp.fft.fft2(exit_wave, norm='ortho')
        exit_wave = jnp.fft.ifft2(kernel * spectrum, norm='ortho')
        exit_wave = exit_wave * lax.complex(window[slice_index, 0], window[slice_index, 1])
    far_field = jnp.fft.fft2(exit_wave, norm='ortho')
    model_amp = jnp.sqrt(jnp.real(far_field) ** 2 + jnp.imag(far_field) ** 2 + BACKGROUND)
    target = jnp.sqrt(measured + BACKGROUND)
    return jnp.sum((model_amp - target) ** 2)

def reference(object_slab, probe_wave, frames, scan_tiles, scan_offsets):
    points = probe_wave.shape[-1]
    slab_now = object_slab
    probe_now = probe_wave
    for iteration in range(ITERS):
        padded = jnp.pad(slab_now, ((0, 0), (0, 0), (0, points), (0, points)))

        def visit(totals, record):
            grad_slab, grad_probe = totals
            tile_id, offset, measured = record
            row_start = (tile_id // N_TX * TR + offset[0]).astype(jnp.int32)
            col_start = (tile_id % N_TX * TC + offset[1]).astype(jnp.int32)
            anchor = (jnp.int32(0), jnp.int32(0), row_start, col_start)
            window = lax.dynamic_slice(padded, anchor, (S, 2, points, points))
            grad_window, grad_part = jax.grad(frame_loss, argnums=(0, 1))(window, probe_now, measured)
            existing = lax.dynamic_slice(grad_slab, anchor, (S, 2, points, points))
            grad_slab = lax.dynamic_update_slice(grad_slab, existing + grad_window, anchor)
            return ((grad_slab, grad_probe + grad_part), None)
        initial = (jnp.zeros_like(padded), jnp.zeros_like(probe_now))
        (grad_slab, grad_probe), unused = lax.scan(visit, initial, (scan_tiles, scan_offsets, frames))
        slab_now = slab_now - OBJECT_RATE * grad_slab[:, :, :NR, :NC]
        probe_now = probe_now - PROBE_RATE / FRAMES * grad_probe
    return (slab_now, probe_now)
```

```python
import functools
import math

import jax
import jax.numpy as jnp
import ml_dtypes
import numpy as np
from jax import lax
from jax.experimental import pallas as pl
from jax.experimental.pallas import tpu as pltpu
from jax.sharding import PartitionSpec as P

MESH = pl.DeviceIdType.MESH
TILE_CAP = 8
BACKGROUND = 0.5
FRESNEL = 0.25
OBJECT_RATE = 0.25
PROBE_RATE = 4.0
VMEM_LIMIT = 56 * 1024 * 1024


def passed_along(value, axis, steps):
    count = lax.axis_size(axis)
    leading, last = (max(0, -steps), min(count, count - steps))
    return lax.ppermute(value, axis, [(source, source + steps) for source in range(leading, last)])


def real_form(matrix):
    return np.block([[matrix.real, -matrix.imag], [matrix.imag, matrix.real]])


def split_table(table):
    high = table.astype(ml_dtypes.bfloat16)
    low = (table - high.astype(np.float64)).astype(ml_dtypes.bfloat16)
    return high, low


def left_table(table):
    high, low = split_table(table)
    return np.concatenate([high, low, high], axis=1)


def right_table(table):
    high, low = split_table(table)
    return np.concatenate([high, low, high], axis=0)


def half_transforms(points):
    half = points // 2
    places = np.arange(half)
    even = np.exp(-2j * np.pi * ((2 * places[:, None]) * places[None, :] % points) / points)
    odd = np.exp(-2j * np.pi * ((2 * places[:, None] + 1) * places[None, :] % points) / points)
    return even / math.sqrt(points), odd / math.sqrt(points)


def build_tables(points):
    even, odd = half_transforms(points)
    places = np.arange(points)
    frequency = (places + points // 2) % points - points // 2
    phase = np.exp(-1j * np.pi * FRESNEL / points * frequency.astype(np.float64) ** 2)
    spread_even = even.conj().T @ (phase[0::2, None] * even)
    spread_odd = odd.conj().T @ (phase[1::2, None] * odd)
    spread = [real_form(spread_even), real_form(spread_odd)]
    fourier = [real_form(even), real_form(odd)]
    order = np.concatenate([places[0::2], places[1::2]])
    shuffle = (places[:, None] == order[None, :]).astype(ml_dtypes.bfloat16)

    def both(pair):
        ahead = [left_table(t) for t in pair] + [right_table(t.T) for t in pair]
        back = [left_table(t.T) for t in pair] + [right_table(t) for t in pair]
        return ahead, back

    spread_ahead, spread_back = both(spread)
    fourier_ahead, fourier_back = both(fourier)
    return spread_ahead, spread_back, fourier_ahead, fourier_back, np.concatenate([shuffle] * 3, axis=0)


def split(value):
    high = value.astype(jnp.bfloat16)
    low = (value - high.astype(jnp.float32)).astype(jnp.bfloat16)
    return high, low


def left_product(table, value):
    high, low = split(value)
    return jnp.dot(table[...], jnp.concatenate([high, high, low], axis=0), preferred_element_type=jnp.float32)


def right_product(value, table):
    high, low = split(value)
    return jnp.dot(jnp.concatenate([high, high, low], axis=1), table[...], preferred_element_type=jnp.float32)


def halves(value, axis):
    half = value.shape[axis] // 2
    first = lax.slice_in_dim(value, 0, half, axis=axis)
    second = lax.slice_in_dim(value, half, 2 * half, axis=axis)
    return first, second


def apart(real, imag, axis):
    real_a, real_b = halves(real, axis)
    imag_a, imag_b = halves(imag, axis)
    plus = jnp.concatenate([real_a + real_b, imag_a + imag_b], axis=axis)
    minus = jnp.concatenate([real_a - real_b, imag_a - imag_b], axis=axis)
    return plus, minus


def together(plus, minus, axis):
    plus_re, plus_im = halves(plus, axis)
    minus_re, minus_im = halves(minus, axis)
    real = jnp.concatenate([plus_re + minus_re, plus_re - minus_re], axis=axis)
    imag = jnp.concatenate([plus_im + minus_im, plus_im - minus_im], axis=axis)
    return real, imag


def regroup(even, odd, axis):
    even_re, even_im = halves(even, axis)
    odd_re, odd_im = halves(odd, axis)
    return jnp.concatenate([even_re, odd_re], axis=axis), jnp.concatenate([even_im, odd_im], axis=axis)


def spread(real, imag, tables):
    left_even, left_odd, right_even, right_odd = tables
    plus, minus = apart(real, imag, 0)
    real, imag = together(left_product(left_even, plus), left_product(left_odd, minus), 0)
    plus, minus = apart(real, imag, 1)
    return together(right_product(plus, right_even), right_product(minus, right_odd), 1)


def to_frequencies(real, imag, tables):
    left_even, left_odd, right_even, right_odd = tables
    plus, minus = apart(real, imag, 0)
    real, imag = regroup(left_product(left_even, plus), left_product(left_odd, minus), 0)
    plus, minus = apart(real, imag, 1)
    return regroup(right_product(plus, right_even), right_product(minus, right_odd), 1)


def from_frequencies(real, imag, tables):
    left_even, left_odd, right_even, right_odd = tables
    even, odd = regroup(real, imag, 0)
    real, imag = together(left_product(left_even, even), left_product(left_odd, odd), 0)
    even, odd = regroup(real, imag, 1)
    return together(right_product(even, right_even), right_product(odd, right_odd), 1)


def place_of(offsets, slot, points):
    row, column = offsets[2 * slot], offsets[2 * slot + 1]
    top = pl.multiple_of(row // 8 * 8, 8)
    start = pl.multiple_of(column // 128 * 128, 128)
    return pl.ds(top, points + 8), pl.ds(start, points + 128), row - top, column - start


def window_of(canvas, offsets, slot, points):
    rows, columns, down, along = place_of(offsets, slot, points)
    parts = []
    for part in range(2):
        wide = canvas[part, rows, columns]
        wide = pltpu.roll(wide, lax.rem(points + 128 - along, points + 128), 1)[:, :points]
        parts.append(pltpu.roll(wide, lax.rem(points + 8 - down, points + 8), 0)[:points])
    return parts


def add_window(canvas, offsets, slot, points, parts):
    rows, columns, down, along = place_of(offsets, slot, points)
    for part in range(2):
        wide = jnp.concatenate([parts[part], jnp.zeros((8, points), jnp.float32)], axis=0)
        wide = pltpu.roll(wide, down, 0)
        wide = jnp.concatenate([wide, jnp.zeros((points + 8, 128), jnp.float32)], axis=1)
        canvas[part, rows, columns] += pltpu.roll(wide, along, 1)


def gather_canvas(layer, tile, right, lower, corner, canvas, sems):
    rows, cols = tile.shape[2], tile.shape[3]
    points = right.shape[2]
    copies = [
        pltpu.make_async_copy(tile.at[layer], canvas.at[:, pl.ds(0, rows), pl.ds(0, cols)], sems.at[0]),
        pltpu.make_async_copy(right, canvas.at[:, pl.ds(0, rows), pl.ds(cols, points)], sems.at[1]),
        pltpu.make_async_copy(lower, canvas.at[:, pl.ds(rows, points), pl.ds(0, cols)], sems.at[2]),
        pltpu.make_async_copy(corner, canvas.at[:, pl.ds(rows, points), pl.ds(cols, points)], sems.at[3]),
    ]
    for copy in copies:
        copy.start()
    for copy in copies:
        copy.wait()


def spread_out_canvas(canvas, tile, right, lower, sems):
    rows, cols = tile.shape[1], tile.shape[2]
    points = lower.shape[1]
    copies = [
        pltpu.make_async_copy(canvas.at[:, pl.ds(0, rows), pl.ds(0, cols)], tile, sems.at[0]),
        pltpu.make_async_copy(canvas.at[:, :, pl.ds(cols, points)], right, sems.at[1]),
        pltpu.make_async_copy(canvas.at[:, pl.ds(rows, points), pl.ds(0, cols)], lower, sems.at[2]),
    ]
    for copy in copies:
        copy.start()
    for copy in copies:
        copy.wait()


def first_kernel(offsets, count, owners, tile, right, lower, corner, probe, t0, t1, t2, t3, wave, canvas, sems):
    slot = pl.program_id(0)

    @pl.when(slot == 0)
    def _():
        gather_canvas(0, tile, right, lower, corner, canvas, sems)

    @pl.when(slot < count[0])
    def _():
        points = probe.shape[1]
        win_re, win_im = window_of(canvas, offsets, slot, points)
        probe_re, probe_im = probe[0], probe[1]
        real = probe_re * win_re - probe_im * win_im
        imag = probe_re * win_im + probe_im * win_re
        real, imag = spread(real, imag, (t0, t1, t2, t3))
        wave[0, 0] = real
        wave[0, 1] = imag


def second_kernel(offsets, count, owners, tile, right, lower, corner, wave, frame, a0, a1, a2, a3, b0, b1, b2, b3, shuffle, grad_wave,
                  grad_tile, grad_right, grad_lower, canvas, grad, sems, columns):
    slot = pl.program_id(0)

    @pl.when(slot == 0)
    def _():
        grad[...] = jnp.zeros_like(grad)
        gather_canvas(1, tile, right, lower, corner, canvas, sems)

    @pl.when(slot < count[0])
    def _():
        points = wave.shape[2]
        half = points // 2
        win_re, win_im = window_of(canvas, offsets, slot, points)
        wave_re, wave_im = wave[0, 0], wave[0, 1]
        real = wave_re * win_re - wave_im * win_im
        imag = wave_re * win_im + wave_im * win_re
        real, imag = to_frequencies(real, imag, (a0, a1, a2, a3))
        pieces = []
        for side in range(points // 128):
            columns[side] = jnp.sqrt(frame[0, :, pl.ds(side * 128, 128)] + BACKGROUND)
            pieces.append(jnp.concatenate([columns[side, pl.ds(start, half, stride=2), :] for start in range(2)], axis=0))
        target = jnp.concatenate(pieces, axis=1)
        high = target.astype(jnp.bfloat16)
        rest = target - high.astype(jnp.float32)
        middle = rest.astype(jnp.bfloat16)
        low = (rest - middle.astype(jnp.float32)).astype(jnp.bfloat16)
        target = jnp.dot(jnp.concatenate([high, middle, low], axis=1), shuffle[...], preferred_element_type=jnp.float32)
        pull = 2.0 - 2.0 * target * lax.rsqrt(real * real + imag * imag + BACKGROUND)
        real, imag = from_frequencies(pull * real, pull * imag, (b0, b1, b2, b3))
        win_re, win_im = window_of(canvas, offsets, slot, points)
        wave_re, wave_im = wave[0, 0], wave[0, 1]
        grad_wave[0, 0] = win_re * real + win_im * imag
        grad_wave[0, 1] = win_re * imag - win_im * real
        add_window(grad, offsets, slot, points, [wave_re * real + wave_im * imag, wave_re * imag - wave_im * real])

    @pl.when(slot == pl.num_programs(0) - 1)
    def _():
        spread_out_canvas(grad, grad_tile, grad_right, grad_lower, sems)


def third_kernel(offsets, count, owners, tile, right, lower, corner, probe, grad_wave, b0, b1, b2, b3, grad_probe, grad_tile,
                 grad_right, grad_lower, canvas, grad, sems):
    slot = pl.program_id(0)

    @pl.when(slot == 0)
    def _():
        grad[...] = jnp.zeros_like(grad)
        grad_probe[...] = jnp.zeros_like(grad_probe)
        gather_canvas(0, tile, right, lower, corner, canvas, sems)

    @pl.when(slot < count[0])
    def _():
        points = probe.shape[1]
        real, imag = spread(grad_wave[0, 0], grad_wave[0, 1], (b0, b1, b2, b3))
        win_re, win_im = window_of(canvas, offsets, slot, points)
        probe_re, probe_im = probe[0], probe[1]
        grad_probe[0] += win_re * real + win_im * imag
        grad_probe[1] += win_re * imag - win_im * real
        add_window(grad, offsets, slot, points, [probe_re * real + probe_im * imag, probe_re * imag - probe_im * real])

    @pl.when(slot == pl.num_programs(0) - 1)
    def _():
        spread_out_canvas(grad, grad_tile, grad_right, grad_lower, sems)


def whole(array):
    return pl.BlockSpec(array.shape, lambda *_: (0,) * array.ndim)


ANY = pl.BlockSpec(memory_space=pl.ANY)


def per_slot(points):
    return pl.BlockSpec((1, 2, points, points), lambda slot, offsets, count, owners: (jnp.minimum(slot, count[0] - 1), 0, 0, 0))


def call(kernel, scalars, operands, in_specs, out_shapes, out_specs, scratch, flops):
    return pl.pallas_call(
        kernel,
        out_shape=out_shapes,
        grid_spec=pltpu.PrefetchScalarGridSpec(
            num_scalar_prefetch=len(scalars),
            grid=(TILE_CAP,),
            in_specs=in_specs,
            out_specs=out_specs,
            scratch_shapes=scratch,
        ),
        compiler_params=pltpu.CompilerParams(vmem_limit_bytes=VMEM_LIMIT),
        cost_estimate=pl.CostEstimate(flops=flops, bytes_accessed=16 * 1024 * 1024, transcendentals=0),
    )(*scalars, *operands)


def probe_kernel(grad, probe, out, from_row, row_sum, from_column, send_sems, recv_sems):
    down, along = lax.axis_index("ty"), lax.axis_index("tx")
    n_down, n_along = lax.axis_size("ty"), lax.axis_size("tx")
    part = grad.shape[0] // n_along
    piece = part // n_down
    barrier = pltpu.get_barrier_semaphore()
    row_peers = [(down, lax.rem(along + step, n_along)) for step in range(1, n_along)]
    column_peers = [(lax.rem(down + step, n_down), along) for step in range(1, n_down)]
    for peer in row_peers + column_peers:
        pl.semaphore_signal(barrier, inc=1, device_id=peer, device_id_type=MESH)
    pl.semaphore_wait(barrier, n_along + n_down - 2)

    def exchange(index, source, target, peer):
        copy = pltpu.make_async_remote_copy(
            src_ref=source, dst_ref=target, send_sem=send_sems.at[index], recv_sem=recv_sems.at[index],
            device_id=peer, device_id_type=MESH)
        copy.start()
        return copy

    def rows(start, size):
        return pl.ds(pl.multiple_of(start, 8), size)

    copies = [
        exchange(step, grad.at[rows(peer[1] * part, part)], from_row.at[step], peer)
        for step, peer in enumerate(row_peers)
    ]
    total = grad[rows(along * part, part)]
    for step, copy in enumerate(copies):
        copy.wait()
        total = total + from_row[step]
    row_sum[...] = total
    base = len(row_peers)
    copies = [
        exchange(base + step, row_sum.at[rows(peer[0] * piece, piece)], from_column.at[step], peer)
        for step, peer in enumerate(column_peers)
    ]
    total = row_sum[rows(down * piece, piece)]
    for step, copy in enumerate(copies):
        copy.wait()
        total = total + from_column[step]
    mine = rows(along * part + down * piece, piece)
    out[mine] = probe[mine] - total
    base += len(column_peers)
    copies = [exchange(base + step, out.at[mine], out.at[mine], peer) for step, peer in enumerate(column_peers)]
    for copy in copies:
        copy.wait()
    base += len(column_peers)
    mine = rows(along * part, part)
    copies = [exchange(base + step, out.at[mine], out.at[mine], peer) for step, peer in enumerate(row_peers)]
    for copy in copies:
        copy.wait()


def update_probe(grad_probe, probe_wave, scale):
    shape = probe_wave.shape
    flat = (probe_wave.size // 128, 128)
    n_down, n_along = lax.axis_size("ty"), lax.axis_size("tx")
    part = flat[0] // n_along
    piece = part // n_down
    copies = 2 * (n_along + n_down - 2)
    vmem = pl.BlockSpec(memory_space=pltpu.VMEM)
    out = pl.pallas_call(
        probe_kernel,
        out_shape=jax.ShapeDtypeStruct(flat, jnp.float32),
        in_specs=[vmem, vmem],
        out_specs=vmem,
        scratch_shapes=[
            pltpu.VMEM((n_along - 1, part, 128), jnp.float32),
            pltpu.VMEM((part, 128), jnp.float32),
            pltpu.VMEM((n_down - 1, piece, 128), jnp.float32),
            pltpu.SemaphoreType.DMA((copies,)),
            pltpu.SemaphoreType.DMA((copies,)),
        ],
        compiler_params=pltpu.CompilerParams(collective_id=1, has_side_effects=True),
    )((grad_probe * scale).reshape(flat), probe_wave.reshape(flat))
    return out.reshape(shape)


def local(object_slab, probe_wave, frames, scan_tiles, scan_offsets):
    columns = lax.axis_size("tx")
    row_index = lax.axis_index("ty")
    col_index = lax.axis_index("tx")
    owned = frames.shape[0]
    points = probe_wave.shape[-1]
    layers, _, tile_rows, tile_cols = object_slab.shape
    total_frames = owned * columns
    my_tile = row_index * columns + col_index
    by_owner = scan_tiles.reshape(columns, owned)

    mine = lax.dynamic_index_in_dim(by_owner, col_index, 0, keepdims=False)
    wanted = row_index * columns + jnp.arange(columns, dtype=jnp.int32)
    source = jnp.sum((mine[None, :] == wanted[:, None]).astype(jnp.int32) * jnp.arange(owned, dtype=jnp.int32)[None, :], axis=1)

    def pick_kernel(source_ref, frames_ref, out_ref, sems):
        copies = [
            pltpu.make_async_copy(frames_ref.at[source_ref[place]], out_ref.at[place], sems.at[place])
            for place in range(columns)
        ]
        for copy in copies:
            copy.start()
        for copy in copies:
            copy.wait()

    outgoing = pl.pallas_call(
        pick_kernel,
        out_shape=jax.ShapeDtypeStruct((columns, points, points), jnp.float32),
        grid_spec=pltpu.PrefetchScalarGridSpec(
            num_scalar_prefetch=1, grid=(1,), in_specs=[ANY], out_specs=ANY,
            scratch_shapes=[pltpu.SemaphoreType.DMA((columns,))]),
        cost_estimate=pl.CostEstimate(flops=0, bytes_accessed=8 * 1024 * 1024, transcendentals=0),
    )(source, frames)
    arrived = lax.all_to_all(outgoing, "tx", split_axis=0, concat_axis=0, tiled=True)

    matches = by_owner == my_tile
    present = jnp.any(matches, axis=1)
    which = jnp.sum(matches.astype(jnp.int32) * jnp.arange(owned, dtype=jnp.int32)[None, :], axis=1)
    global_ids = jnp.arange(columns, dtype=jnp.int32) * owned + which
    ranks = jnp.cumsum(present.astype(jnp.int32)) - 1
    slot_pick = (present[None, :] & (ranks[None, :] == jnp.arange(TILE_CAP, dtype=jnp.int32)[:, None])).astype(jnp.int32)
    chosen_ids = jnp.sum(slot_pick * global_ids[None, :], axis=1)
    owners = jnp.sum(slot_pick * jnp.arange(columns, dtype=jnp.int32)[None, :], axis=1)
    count = jnp.sum(present.astype(jnp.int32)).reshape(1)
    offsets = scan_offsets[chosen_ids].reshape(-1)
    scalars = (offsets, count, owners)

    halos = []
    for layer in range(layers):
        right = passed_along(object_slab[layer, :, :, :points], "tx", -1)
        lower = passed_along(object_slab[layer, :, :points, :], "ty", -1)
        corner = passed_along(lower[:, :, :points], "tx", -1)
        halos.append((right, lower, corner))

    spread_ahead, spread_back, fourier_ahead, fourier_back, shuffle = build_tables(points)
    slot_spec = pl.BlockSpec((1, 2, points, points), lambda slot, offsets, count, owners: (slot, 0, 0, 0))
    frame_spec = pl.BlockSpec((1, points, points), lambda slot, offsets, count, owners: (owners[slot], 0, 0))
    waves = jax.ShapeDtypeStruct((TILE_CAP, 2, points, points), jnp.float32)
    canvas = pltpu.VMEM((2, tile_rows + points, tile_cols + points), jnp.float32)
    sems = pltpu.SemaphoreType.DMA((4,))
    flops = TILE_CAP * 24 * points**3
    grads = [
        jax.ShapeDtypeStruct((2, tile_rows, tile_cols), jnp.float32),
        jax.ShapeDtypeStruct((2, tile_rows + points, points), jnp.float32),
        jax.ShapeDtypeStruct((2, points, tile_cols), jnp.float32),
    ]

    wave = call(
        first_kernel, scalars, (object_slab, *halos[0], probe_wave, *spread_ahead),
        [ANY] * 4 + [whole(probe_wave)] + [whole(t) for t in spread_ahead],
        waves, slot_spec, [canvas, sems], flops)
    grad_wave, *grad_one = call(
        second_kernel, scalars, (object_slab, *halos[1], wave, arrived, *fourier_ahead, *fourier_back, shuffle),
        [ANY] * 4 + [slot_spec, frame_spec] + [whole(t) for t in (*fourier_ahead, *fourier_back, shuffle)],
        [waves] + grads, [slot_spec] + [ANY] * 3, [canvas, canvas, sems, pltpu.VMEM((points // 128, points, 128), jnp.float32)], 2 * flops)
    grad_probe, *grad_zero = call(
        third_kernel, scalars, (object_slab, *halos[0], probe_wave, grad_wave, *spread_back),
        [ANY] * 4 + [whole(probe_wave), slot_spec] + [whole(t) for t in spread_back],
        [jax.ShapeDtypeStruct(probe_wave.shape, jnp.float32)] + grads,
        [whole(probe_wave)] + [ANY] * 3, [canvas, canvas, sems], flops)

    totals = []
    for tile, right, lower in (grad_zero, grad_one):
        right_back = passed_along(right, "tx", 1)
        lower = lower.at[:, :, :points].add(right_back[:, tile_rows:])
        lower_back = passed_along(lower, "ty", 1)
        tile = tile.at[:, :, :points].add(right_back[:, :tile_rows])
        totals.append(tile.at[:, :points, :].add(lower_back))
    new_probe = update_probe(grad_probe, probe_wave, PROBE_RATE / total_frames)
    return (object_slab - OBJECT_RATE * jnp.stack(totals), new_probe)


def solution(mesh):
    return jax.shard_map(
        local,
        mesh=mesh,
        in_specs=(P(None, None, "ty", "tx"), P(), P("tx", None, None), P(), P()),
        out_specs=(P(None, None, "ty", "tx"), P()),
        check_vma=False,
    )
```

```python
import functools
import math

import jax
import jax.numpy as jnp
import ml_dtypes
import numpy as np
from jax import lax
from jax.experimental import pallas as pl
from jax.experimental.pallas import tpu as pltpu
from jax.sharding import PartitionSpec as P

MESH = pl.DeviceIdType.MESH
TILE_CAP = 8
BACKGROUND = 0.5
FRESNEL = 0.25
OBJECT_RATE = 0.25
PROBE_RATE = 4.0
VMEM_LIMIT = 56 * 1024 * 1024


FRAME_STEPS = ((1, 0, 0), (3, 0, 0), (0, 1, 1), (2, 0, 0), (1, 1, 1), (3, 1, 1), (0, 1, 0), (2, 1, 1), (1, 0, 1), (3, 0, 1), (2, 0, 1),
               (1, 1, 0), (3, 1, 0), (2, 1, 0), (0, 0, 1))


def real_form(matrix):
    return np.block([[matrix.real, -matrix.imag], [matrix.imag, matrix.real]])


def split_table(table):
    high = table.astype(ml_dtypes.bfloat16)
    low = (table - high.astype(np.float64)).astype(ml_dtypes.bfloat16)
    return high, low


def left_table(table):
    high, low = split_table(table)
    return np.concatenate([high, low, high], axis=1)


def right_table(table):
    high, low = split_table(table)
    return np.concatenate([high, low, high], axis=0)


def half_transforms(points):
    half = points // 2
    places = np.arange(half)
    even = np.exp(-2j * np.pi * ((2 * places[:, None]) * places[None, :] % points) / points)
    odd = np.exp(-2j * np.pi * ((2 * places[:, None] + 1) * places[None, :] % points) / points)
    return even / math.sqrt(points), odd / math.sqrt(points)


def build_tables(points):
    even, odd = half_transforms(points)
    places = np.arange(points)
    frequency = (places + points // 2) % points - points // 2
    phase = np.exp(-1j * np.pi * FRESNEL / points * frequency.astype(np.float64) ** 2)
    spread_even = even.conj().T @ (phase[0::2, None] * even)
    spread_odd = odd.conj().T @ (phase[1::2, None] * odd)
    spread = [real_form(spread_even), real_form(spread_odd)]
    fourier = [real_form(even), real_form(odd)]
    order = np.concatenate([places[0::2], places[1::2]])
    shuffle = (places[:, None] == order[None, :]).astype(ml_dtypes.bfloat16)

    def both(pair):
        ahead = [left_table(t) for t in pair] + [right_table(t.T) for t in pair]
        back = [left_table(t.T) for t in pair] + [right_table(t) for t in pair]
        return ahead, back

    spread_ahead, spread_back = both(spread)
    fourier_ahead, fourier_back = both(fourier)
    return spread_ahead, spread_back, fourier_ahead, fourier_back, np.concatenate([shuffle] * 3, axis=0)


def split(value):
    high = value.astype(jnp.bfloat16)
    low = (value - high.astype(jnp.float32)).astype(jnp.bfloat16)
    return high, low


def left_product(table, value):
    high, low = split(value)
    return jnp.dot(table[...], jnp.concatenate([high, high, low], axis=0), preferred_element_type=jnp.float32)


def right_product(value, table):
    high, low = split(value)
    return jnp.dot(jnp.concatenate([high, high, low], axis=1), table[...], preferred_element_type=jnp.float32)


def halves(value, axis):
    half = value.shape[axis] // 2
    first = lax.slice_in_dim(value, 0, half, axis=axis)
    second = lax.slice_in_dim(value, half, 2 * half, axis=axis)
    return first, second


def apart(real, imag, axis):
    real_a, real_b = halves(real, axis)
    imag_a, imag_b = halves(imag, axis)
    plus = jnp.concatenate([real_a + real_b, imag_a + imag_b], axis=axis)
    minus = jnp.concatenate([real_a - real_b, imag_a - imag_b], axis=axis)
    return plus, minus


def together(plus, minus, axis):
    plus_re, plus_im = halves(plus, axis)
    minus_re, minus_im = halves(minus, axis)
    real = jnp.concatenate([plus_re + minus_re, plus_re - minus_re], axis=axis)
    imag = jnp.concatenate([plus_im + minus_im, plus_im - minus_im], axis=axis)
    return real, imag


def regroup(even, odd, axis):
    even_re, even_im = halves(even, axis)
    odd_re, odd_im = halves(odd, axis)
    return jnp.concatenate([even_re, odd_re], axis=axis), jnp.concatenate([even_im, odd_im], axis=axis)


def spread(real, imag, tables):
    left_even, left_odd, right_even, right_odd = tables
    plus, minus = apart(real, imag, 0)
    real, imag = together(left_product(left_even, plus), left_product(left_odd, minus), 0)
    plus, minus = apart(real, imag, 1)
    return together(right_product(plus, right_even), right_product(minus, right_odd), 1)


def to_frequencies(real, imag, tables):
    left_even, left_odd, right_even, right_odd = tables
    plus, minus = apart(real, imag, 0)
    real, imag = regroup(left_product(left_even, plus), left_product(left_odd, minus), 0)
    plus, minus = apart(real, imag, 1)
    return regroup(right_product(plus, right_even), right_product(minus, right_odd), 1)


def from_frequencies(real, imag, tables):
    left_even, left_odd, right_even, right_odd = tables
    even, odd = regroup(real, imag, 0)
    real, imag = together(left_product(left_even, even), left_product(left_odd, odd), 0)
    even, odd = regroup(real, imag, 1)
    return together(right_product(even, right_even), right_product(odd, right_odd), 1)


def place_of(offsets, slot, points):
    row, column = offsets[2 * slot], offsets[2 * slot + 1]
    top = pl.multiple_of(row // 8 * 8, 8)
    start = pl.multiple_of(column // 128 * 128, 128)
    return pl.ds(top, points + 8), pl.ds(start, points + 128), row - top, column - start


def window_of(canvas, offsets, slot, points):
    rows, columns, down, along = place_of(offsets, slot, points)
    parts = []
    for part in range(2):
        wide = canvas[part, rows, columns]
        wide = pltpu.roll(wide, lax.rem(points + 128 - along, points + 128), 1)[:, :points]
        parts.append(pltpu.roll(wide, lax.rem(points + 8 - down, points + 8), 0)[:points])
    return parts


def add_window(canvas, offsets, slot, points, parts):
    rows, columns, down, along = place_of(offsets, slot, points)
    for part in range(2):
        wide = jnp.concatenate([parts[part], jnp.zeros((8, points), jnp.float32)], axis=0)
        wide = pltpu.roll(wide, down, 0)
        wide = jnp.concatenate([wide, jnp.zeros((points + 8, 128), jnp.float32)], axis=1)
        canvas[part, rows, columns] += pltpu.roll(wide, along, 1)


def gather_canvas(layer, tile, right, lower, corner, canvas, sems):
    rows, cols = tile.shape[2], tile.shape[3]
    points = right.shape[3]
    copies = [
        pltpu.make_async_copy(tile.at[layer], canvas.at[:, pl.ds(0, rows), pl.ds(0, cols)], sems.at[0]),
        pltpu.make_async_copy(right.at[layer], canvas.at[:, pl.ds(0, rows), pl.ds(cols, points)], sems.at[1]),
        pltpu.make_async_copy(lower.at[layer], canvas.at[:, pl.ds(rows, points), pl.ds(0, cols)], sems.at[2]),
        pltpu.make_async_copy(corner.at[layer], canvas.at[:, pl.ds(rows, points), pl.ds(cols, points)], sems.at[3]),
    ]
    for copy in copies:
        copy.start()
    for copy in copies:
        copy.wait()

    @pl.when(lax.axis_index("ty") == lax.axis_size("ty") - 1)
    def _():
        canvas[:, pl.ds(rows, points), :] = jnp.zeros((2, points, cols + points), jnp.float32)

    @pl.when(lax.axis_index("tx") == lax.axis_size("tx") - 1)
    def _():
        canvas[:, :, pl.ds(cols, points)] = jnp.zeros((2, rows + points, points), jnp.float32)


def spread_out_canvas(canvas, tile, right, lower, sems):
    rows, cols = tile.shape[1], tile.shape[2]
    points = lower.shape[1]
    copies = [
        pltpu.make_async_copy(canvas.at[:, pl.ds(0, rows), pl.ds(0, cols)], tile, sems.at[0]),
        pltpu.make_async_copy(canvas.at[:, :, pl.ds(cols, points)], right, sems.at[1]),
        pltpu.make_async_copy(canvas.at[:, pl.ds(rows, points), pl.ds(0, cols)], lower, sems.at[2]),
    ]
    for copy in copies:
        copy.start()
    for copy in copies:
        copy.wait()


def first_kernel(offsets, count, owners, tile, right, lower, corner, probe, t0, t1, t2, t3, wave, canvas, sems):
    slot = pl.program_id(0)

    @pl.when(slot == 0)
    def _():
        gather_canvas(0, tile, right, lower, corner, canvas, sems)

    @pl.when(slot < count[0])
    def _():
        points = probe.shape[1]
        win_re, win_im = window_of(canvas, offsets, slot, points)
        probe_re, probe_im = probe[0], probe[1]
        real = probe_re * win_re - probe_im * win_im
        imag = probe_re * win_im + probe_im * win_re
        real, imag = spread(real, imag, (t0, t1, t2, t3))
        wave[0, 0] = real
        wave[0, 1] = imag


def second_kernel(offsets, count, owners, tile, right, lower, corner, wave, frame, a0, a1, a2, a3, b0, b1, b2, b3, shuffle, grad_wave,
                  grad_tile, grad_right, grad_lower, canvas, grad, sems, columns):
    slot = pl.program_id(0)

    @pl.when(slot == 0)
    def _():
        grad[...] = jnp.zeros_like(grad)
        gather_canvas(1, tile, right, lower, corner, canvas, sems)

    @pl.when(slot < count[0])
    def _():
        points = wave.shape[2]
        half = points // 2
        win_re, win_im = window_of(canvas, offsets, slot, points)
        wave_re, wave_im = wave[0, 0], wave[0, 1]
        real = wave_re * win_re - wave_im * win_im
        imag = wave_re * win_im + wave_im * win_re
        real, imag = to_frequencies(real, imag, (a0, a1, a2, a3))
        pieces = []
        for side in range(points // 128):
            columns[side] = jnp.sqrt(frame[0, :, pl.ds(side * 128, 128)] + BACKGROUND)
            pieces.append(jnp.concatenate([columns[side, pl.ds(start, half, stride=2), :] for start in range(2)], axis=0))
        target = jnp.concatenate(pieces, axis=1)
        high = target.astype(jnp.bfloat16)
        rest = target - high.astype(jnp.float32)
        middle = rest.astype(jnp.bfloat16)
        low = (rest - middle.astype(jnp.float32)).astype(jnp.bfloat16)
        target = jnp.dot(jnp.concatenate([high, middle, low], axis=1), shuffle[...], preferred_element_type=jnp.float32)
        pull = 2.0 - 2.0 * target * lax.rsqrt(real * real + imag * imag + BACKGROUND)
        real, imag = from_frequencies(pull * real, pull * imag, (b0, b1, b2, b3))
        win_re, win_im = window_of(canvas, offsets, slot, points)
        wave_re, wave_im = wave[0, 0], wave[0, 1]
        grad_wave[0, 0] = win_re * real + win_im * imag
        grad_wave[0, 1] = win_re * imag - win_im * real
        add_window(grad, offsets, slot, points, [wave_re * real + wave_im * imag, wave_re * imag - wave_im * real])

    @pl.when(slot == pl.num_programs(0) - 1)
    def _():
        spread_out_canvas(grad, grad_tile, grad_right, grad_lower, sems)


def third_kernel(offsets, count, owners, tile, right, lower, corner, probe, grad_wave, b0, b1, b2, b3, grad_probe, grad_tile,
                 grad_right, grad_lower, canvas, grad, sems):
    slot = pl.program_id(0)

    @pl.when(slot == 0)
    def _():
        grad[...] = jnp.zeros_like(grad)
        grad_probe[...] = jnp.zeros_like(grad_probe)
        gather_canvas(0, tile, right, lower, corner, canvas, sems)

    @pl.when(slot < count[0])
    def _():
        points = probe.shape[1]
        real, imag = spread(grad_wave[0, 0], grad_wave[0, 1], (b0, b1, b2, b3))
        win_re, win_im = window_of(canvas, offsets, slot, points)
        probe_re, probe_im = probe[0], probe[1]
        grad_probe[0] += win_re * real + win_im * imag
        grad_probe[1] += win_re * imag - win_im * real
        add_window(grad, offsets, slot, points, [probe_re * real + probe_im * imag, probe_re * imag - probe_im * real])

    @pl.when(slot == pl.num_programs(0) - 1)
    def _():
        spread_out_canvas(grad, grad_tile, grad_right, grad_lower, sems)


def whole(array):
    return pl.BlockSpec(array.shape, lambda *_: (0,) * array.ndim)


ANY = pl.BlockSpec(memory_space=pl.ANY)


def per_slot(points):
    return pl.BlockSpec((1, 2, points, points), lambda slot, offsets, count, owners: (jnp.minimum(slot, count[0] - 1), 0, 0, 0))


def call(kernel, scalars, operands, in_specs, out_shapes, out_specs, scratch, flops):
    return pl.pallas_call(
        kernel,
        out_shape=out_shapes,
        grid_spec=pltpu.PrefetchScalarGridSpec(
            num_scalar_prefetch=len(scalars),
            grid=(TILE_CAP,),
            in_specs=in_specs,
            out_specs=out_specs,
            scratch_shapes=scratch,
        ),
        compiler_params=pltpu.CompilerParams(vmem_limit_bytes=VMEM_LIMIT),
        cost_estimate=pl.CostEstimate(flops=flops, bytes_accessed=16 * 1024 * 1024, transcendentals=0),
    )(*scalars, *operands)


def remote(source, target, send_sem, recv_sem, peer):
    return pltpu.make_async_remote_copy(
        src_ref=source, dst_ref=target, send_sem=send_sem, recv_sem=recv_sem, device_id=peer, device_id_type=MESH)


def when(condition, action):
    pl.when(condition)(lambda: action())


def greet(peers):
    barrier = pltpu.get_barrier_semaphore()
    for peer in peers:
        pl.semaphore_signal(barrier, inc=1, device_id=peer, device_id_type=MESH)
    pl.semaphore_wait(barrier, len(peers))


def around(down, along, n_down, n_along):
    row = [(down, lax.rem(along + step, n_along)) for step in range(1, n_along)]
    column = [(lax.rem(down + step, n_down), along) for step in range(1, n_down)]
    return row, column


def frame_peer(down, along, n_down, n_along, step, ahead):
    step_y, step_z, step_core = step
    if not ahead:
        step_y = -step_y % (n_along // 4)
    place_y, place_z, core = along // 4, lax.rem(along // 2, 2), lax.rem(along, 2)
    other = step_z * jnp.maximum(step_core, core)
    place_y = lax.rem(place_y + step_y, n_along // 4)
    place_z = lax.rem(place_z + step_z, 2)
    core = lax.rem(core + step_core, 2)
    return (lax.rem(down + other * (n_down // 2), n_down), place_y * 4 + place_z * 2 + core), other


def fetch_kernel(source, frames, slab, right, lower, corner, arrived, held, picked, lower_relay, right_relay, held_sem, own_sem,
                 send_sems, recv_sems):
    down, along = lax.axis_index("ty"), lax.axis_index("tx")
    n_down, n_along = lax.axis_size("ty"), lax.axis_size("tx")
    layers, points, rows, cols = right.shape[0], right.shape[3], right.shape[2], lower.shape[3]
    half = n_down // 2
    load = pltpu.make_async_copy(frames, held, held_sem)
    load.start()
    ring = lambda by_down, by_along: (lax.rem(down + by_down + n_down, n_down), lax.rem(along + by_along + n_along, n_along))
    greet([frame_peer(down, along, n_down, n_along, step, False)[0] for step in FRAME_STEPS]
          + [ring(by, 0) for by in (1, -1, half, 3, -3)] + [ring(0, by) for by in (1, -1, 3, -3, 4, -4)])
    above, left = ring(-1, 0), ring(0, -1)
    not_top, not_bottom = down > 0, down < n_down - 1
    not_first, not_last = along > 0, along < n_along - 1
    wraps, passes = down == half, down == 0
    crosses, carries = lax.rem(along, 4) == 0, lax.rem(along, 4) == 3
    crossed = carries & not_last
    across = crosses & not_first
    base = n_along - 1
    index = iter(range(base, base + 20))

    def copy(source_ref, target, peer, at=None):
        at = next(index) if at is None else at
        return remote(source_ref, target, send_sems.at[at], recv_sems.at[at], peer)

    first, last = 0, layers - 1
    side = [slab.at[layer, :, :, pl.ds(0, points)] for layer in range(layers)]
    edge = [lower.at[layer, :, :, pl.ds(0, points)] for layer in range(layers)]
    rest, start = pl.ds(points, cols - points), pl.ds(0, points)
    lowers, others, hops, forwards, rights, corners = [], [], [], [], [], []
    for layer in range(layers):
        lowers.append(copy(slab.at[layer, :, pl.ds(0, points), start], lower.at[layer, :, :, start], above))
        at = next(index)
        others.append(copy(slab.at[layer, :, pl.ds(0, points), rest], lower.at[layer, :, :, rest], above, at))
        hops.append(copy(slab.at[layer, :, pl.ds(0, points), rest], lower_relay.at[layer], ring(half, 0)))
        forwards.append(copy(lower_relay.at[layer], lower.at[layer, :, :, rest], ring(3, 0), at))
        rights.append(copy(side[layer], right.at[layer], left))
        corners.append(copy(edge[layer], corner.at[layer], left))
    at_right, at_corner = base + 5 * last + 3, base + 5 * last + 4
    right_hop = copy(side[last], right_relay.at[:, pl.ds(0, rows), :], ring(0, 3))
    right_forward = copy(right_relay.at[:, pl.ds(0, rows), :], right.at[last], ring(0, -4), at_right)
    corner_hop = copy(edge[last], right_relay.at[:, pl.ds(rows, points), :], ring(0, 3))
    corner_forward = copy(right_relay.at[:, pl.ds(rows, points), :], corner.at[last], ring(0, -4), at_corner)

    for layer in range(layers):
        when(not_top, lowers[layer].start)
        when(not_top & ~wraps, others[layer].start)
        when(wraps, hops[layer].start)
    when(across, right_hop.start)
    when(not_first & ~crosses, rights[last].start)
    when(not_first, rights[first].start)
    load.wait()
    sends = []
    for step, offset in enumerate(FRAME_STEPS):
        peer, other = frame_peer(down, along, n_down, n_along, offset, True)
        picked[step] = held[source[other * n_along + peer[1]]]
        send = remote(picked.at[step], arrived.at[along], send_sems.at[step], recv_sems.at[step], peer)
        send.start()
        sends.append(send)
    picked[n_along - 1] = held[source[along]]
    own = pltpu.make_async_copy(picked.at[n_along - 1], arrived.at[along], own_sem)
    own.start()
    relays = along >= 4
    when(carries & relays, right_hop.wait_recv)
    when(carries & relays, right_forward.start)
    for layer in range(layers):
        when(passes, hops[layer].wait_recv)
        when(passes, forwards[layer].start)
        when(not_bottom, lowers[layer].wait_recv)
        if layer == last:
            when(not_bottom & across, corner_hop.start)
            when(not_bottom & not_first & ~crosses, corners[layer].start)
            when(not_bottom & carries & relays, corner_hop.wait_recv)
            when(not_bottom & carries & relays, corner_forward.start)
        else:
            when(not_bottom & not_first, corners[layer].start)
    for layer in range(layers):
        when(not_bottom, others[layer].wait_recv)
        when(not_last, rights[layer].wait_recv)
        when(not_bottom & not_last, corners[layer].wait_recv)
        when(not_top, lowers[layer].wait_send)
        when(not_top & ~wraps, others[layer].wait_send)
        when(wraps, hops[layer].wait_send)
        when(passes, forwards[layer].wait_send)
        if layer == last:
            when(across, right_hop.wait_send)
            when(not_first & ~crosses, rights[layer].wait_send)
            when(carries & relays, right_forward.wait_send)
            when(not_bottom & across, corner_hop.wait_send)
            when(not_bottom & not_first & ~crosses, corners[layer].wait_send)
            when(not_bottom & carries & relays, corner_forward.wait_send)
        else:
            when(not_first, rights[layer].wait_send)
            when(not_bottom & not_first, corners[layer].wait_send)
    for send in sends:
        send.wait()
    own.wait()


def fetch(source, frames, object_slab, points):
    layers, _, rows, cols = object_slab.shape
    n_along = lax.axis_size("tx")
    copies = n_along - 1 + 5 * layers + 2
    shape = lambda *dims: jax.ShapeDtypeStruct(dims, jnp.float32)
    return pl.pallas_call(
        fetch_kernel,
        out_shape=[shape(layers, 2, rows, points), shape(layers, 2, points, cols), shape(layers, 2, points, points),
                   shape(n_along, points, points)],
        in_specs=[pl.BlockSpec(memory_space=pltpu.SMEM), ANY, ANY],
        out_specs=[ANY] * 4,
        scratch_shapes=[
            pltpu.VMEM(frames.shape, jnp.float32),
            pltpu.VMEM((n_along, points, points), jnp.float32),
            pltpu.VMEM((layers, 2, points, cols - points), jnp.float32),
            pltpu.VMEM((2, rows + points, points), jnp.float32),
            pltpu.SemaphoreType.DMA,
            pltpu.SemaphoreType.DMA,
            pltpu.SemaphoreType.DMA((copies,)),
            pltpu.SemaphoreType.DMA((copies,)),
        ],
        compiler_params=pltpu.CompilerParams(collective_id=0, has_side_effects=True, vmem_limit_bytes=VMEM_LIMIT),
    )(source, frames, object_slab)


def return_kernel(right_0, right_1, lower_0, lower_1, grad_probe, probe, right_in, lower_in, probe_out,
                  corner_in, held, relay, from_row, row_sum, from_column, load_sems, send_sems, recv_sems):
    down, along = lax.axis_index("ty"), lax.axis_index("tx")
    n_down, n_along = lax.axis_size("ty"), lax.axis_size("tx")
    rights, lowers = (right_0, right_1), (lower_0, lower_1)
    layers, points, rows, cols = len(rights), right_in.shape[3], right_in.shape[2], lower_in.shape[3]
    loads = [
        pltpu.make_async_copy(lowers[layer].at[:, :, pl.ds(0, points)], held.at[layer], load_sems.at[layer])
        for layer in range(layers)
    ]
    for load in loads:
        load.start()
    row_peers, column_peers = around(down, along, n_down, n_along)
    greet(row_peers + column_peers)
    part = grad_probe.shape[0] // n_along
    piece = part // n_down
    below, after = (lax.rem(down + 1, n_down), along), (down, lax.rem(along + 1, n_along))
    not_top, not_bottom = down > 0, down < n_down - 1
    not_first, not_last = along > 0, along < n_along - 1

    def exchange(index, source, target, peer):
        copy = remote(source, target, send_sems.at[index], recv_sems.at[index], peer)
        copy.start()
        return copy

    def aligned(start, size):
        return pl.ds(pl.multiple_of(start, 8), size)

    row_copies = [
        exchange(step, grad_probe.at[aligned(peer[1] * part, part)], from_row.at[step], peer) for step, peer in enumerate(row_peers)
    ]
    base = 2 * (n_along + n_down - 2)
    corners, sides, firsts, seconds, hops, forwards = [], [], [], [], [], []
    half = n_down // 2
    wraps, passes = down == half - 1, down == n_down - 1
    over, down_three = (lax.rem(down + half, n_down), along), (lax.rem(down + n_down - 3, n_down), along)
    for layer in range(layers):
        at = base + 5 * layer
        corners.append(remote(rights[layer].at[:, pl.ds(rows, points), :], corner_in.at[layer], send_sems.at[at], recv_sems.at[at], after))
        sides.append(remote(rights[layer].at[:, pl.ds(0, rows), :], right_in.at[layer], send_sems.at[at + 1], recv_sems.at[at + 1], after))
        rest = pl.ds(points, cols - points)
        firsts.append(remote(lowers[layer].at[:, :, rest], lower_in.at[layer, :, :, rest], send_sems.at[at + 2], recv_sems.at[at + 2], below))
        seconds.append(remote(held.at[layer], lower_in.at[layer, :, :, pl.ds(0, points)], send_sems.at[at + 3], recv_sems.at[at + 3], below))
        hops.append(remote(lowers[layer].at[:, :, rest], relay.at[layer], send_sems.at[at + 4], recv_sems.at[at + 4], over))
        forwards.append(remote(relay.at[layer], lower_in.at[layer, :, :, rest], send_sems.at[at + 2], recv_sems.at[at + 2], down_three))
    for layer in range(layers):
        when(not_bottom & not_last, corners[layer].start)

    total = grad_probe[aligned(along * part, part)]
    for step, copy in enumerate(row_copies):
        copy.wait()
        total = total + from_row[step]
    row_sum[...] = total
    at = n_along - 1
    copies = [
        exchange(at + step, row_sum.at[aligned(peer[0] * piece, piece)], from_column.at[step], peer)
        for step, peer in enumerate(column_peers)
    ]
    total = row_sum[aligned(down * piece, piece)]
    for step, copy in enumerate(copies):
        copy.wait()
        total = total + from_column[step]
    mine = aligned(along * part + down * piece, piece)
    probe_out[mine] = probe[mine] - total
    at += n_down - 1
    copies = [exchange(at + step, probe_out.at[mine], probe_out.at[mine], peer) for step, peer in enumerate(column_peers)]
    for layer in range(layers):
        when(not_bottom & ~wraps, firsts[layer].start)
        when(wraps, hops[layer].start)
    for copy in copies:
        copy.wait()
    at += n_down - 1
    mine = aligned(along * part, part)
    row_copies = [exchange(at + step, probe_out.at[mine], probe_out.at[mine], peer) for step, peer in enumerate(row_peers)]

    for layer in range(layers):
        loads[layer].wait()
        when(not_bottom & not_first, corners[layer].wait_recv)

        @pl.when(not_bottom & not_first)
        def _():
            held[layer] += corner_in[layer]

        when(not_bottom, seconds[layer].start)
        when(not_last, sides[layer].start)
    for layer in range(layers):
        when(passes, hops[layer].wait_recv)
        when(passes, forwards[layer].start)
    for copy in row_copies:
        copy.wait()
    for layer in range(layers):
        when(not_bottom & not_last, corners[layer].wait_send)
        when(not_last, sides[layer].wait_send)
        when(not_first, sides[layer].wait_recv)
        when(not_bottom & ~wraps, firsts[layer].wait_send)
        when(not_top, firsts[layer].wait_recv)
        when(wraps, hops[layer].wait_send)
        when(passes, forwards[layer].wait_send)
        when(not_bottom, seconds[layer].wait_send)
        when(not_top, seconds[layer].wait_recv)


def send_back(rights, lowers, grad_probe, probe_wave, scale, rows):
    flat = (probe_wave.size // 128, 128)
    n_down, n_along = lax.axis_size("ty"), lax.axis_size("tx")
    part = flat[0] // n_along
    piece = part // n_down
    layers = len(rights)
    points = rights[0].shape[2]
    cols = lowers[0].shape[2]
    copies = 2 * (n_along + n_down - 2) + 5 * layers
    vmem = pl.BlockSpec(memory_space=pltpu.VMEM)
    shape = lambda *dims: jax.ShapeDtypeStruct(dims, jnp.float32)
    right_in, lower_in, probe = pl.pallas_call(
        return_kernel,
        out_shape=[shape(layers, 2, rows, points), shape(layers, 2, points, cols), shape(*flat)],
        in_specs=[ANY] * (2 * layers) + [vmem, vmem],
        out_specs=[ANY, ANY, vmem],
        scratch_shapes=[
            pltpu.VMEM((layers, 2, points, points), jnp.float32),
            pltpu.VMEM((layers, 2, points, points), jnp.float32),
            pltpu.VMEM((layers, 2, points, cols - points), jnp.float32),
            pltpu.VMEM((n_along - 1, part, 128), jnp.float32),
            pltpu.VMEM((part, 128), jnp.float32),
            pltpu.VMEM((n_down - 1, piece, 128), jnp.float32),
            pltpu.SemaphoreType.DMA((layers,)),
            pltpu.SemaphoreType.DMA((copies,)),
            pltpu.SemaphoreType.DMA((copies,)),
        ],
        compiler_params=pltpu.CompilerParams(collective_id=1, has_side_effects=True, vmem_limit_bytes=VMEM_LIMIT),
    )(*rights, *lowers, (grad_probe * scale).reshape(flat), probe_wave.reshape(flat))
    return right_in, lower_in, probe.reshape(probe_wave.shape)


def local(object_slab, probe_wave, frames, scan_tiles, scan_offsets):
    columns = lax.axis_size("tx")
    row_index = lax.axis_index("ty")
    col_index = lax.axis_index("tx")
    owned = frames.shape[0]
    points = probe_wave.shape[-1]
    layers, _, tile_rows, tile_cols = object_slab.shape
    total_frames = owned * columns
    my_tile = row_index * columns + col_index
    by_owner = scan_tiles.reshape(columns, owned)

    mine = lax.dynamic_index_in_dim(by_owner, col_index, 0, keepdims=False)
    other_row = lax.rem(row_index + lax.axis_size("ty") // 2, lax.axis_size("ty"))
    places = jnp.arange(columns, dtype=jnp.int32)
    wanted = jnp.concatenate([row_index * columns + places, other_row * columns + places])
    source = jnp.sum((mine[None, :] == wanted[:, None]).astype(jnp.int32) * jnp.arange(owned, dtype=jnp.int32)[None, :], axis=1)

    right, lower, corner, arrived = fetch(source, frames, object_slab, points)

    matches = by_owner == my_tile
    present = jnp.any(matches, axis=1)
    which = jnp.sum(matches.astype(jnp.int32) * jnp.arange(owned, dtype=jnp.int32)[None, :], axis=1)
    global_ids = jnp.arange(columns, dtype=jnp.int32) * owned + which
    ranks = jnp.cumsum(present.astype(jnp.int32)) - 1
    slot_pick = (present[None, :] & (ranks[None, :] == jnp.arange(TILE_CAP, dtype=jnp.int32)[:, None])).astype(jnp.int32)
    chosen_ids = jnp.sum(slot_pick * global_ids[None, :], axis=1)
    owners = jnp.sum(slot_pick * jnp.arange(columns, dtype=jnp.int32)[None, :], axis=1)
    count = jnp.sum(present.astype(jnp.int32)).reshape(1)
    offsets = scan_offsets[chosen_ids].reshape(-1)
    scalars = (offsets, count, owners)

    spread_ahead, spread_back, fourier_ahead, fourier_back, shuffle = build_tables(points)
    slot_spec = pl.BlockSpec((1, 2, points, points), lambda slot, offsets, count, owners: (slot, 0, 0, 0))
    frame_spec = pl.BlockSpec((1, points, points), lambda slot, offsets, count, owners: (owners[slot], 0, 0))
    waves = jax.ShapeDtypeStruct((TILE_CAP, 2, points, points), jnp.float32)
    canvas = pltpu.VMEM((2, tile_rows + points, tile_cols + points), jnp.float32)
    sems = pltpu.SemaphoreType.DMA((4,))
    flops = TILE_CAP * 24 * points**3
    grads = [
        jax.ShapeDtypeStruct((2, tile_rows, tile_cols), jnp.float32),
        jax.ShapeDtypeStruct((2, tile_rows + points, points), jnp.float32),
        jax.ShapeDtypeStruct((2, points, tile_cols), jnp.float32),
    ]

    wave = call(
        first_kernel, scalars, (object_slab, right, lower, corner, probe_wave, *spread_ahead),
        [ANY] * 4 + [whole(probe_wave)] + [whole(t) for t in spread_ahead],
        waves, slot_spec, [canvas, sems], flops)
    grad_wave, *grad_one = call(
        second_kernel, scalars, (object_slab, right, lower, corner, wave, arrived, *fourier_ahead, *fourier_back, shuffle),
        [ANY] * 4 + [slot_spec, frame_spec] + [whole(t) for t in (*fourier_ahead, *fourier_back, shuffle)],
        [waves] + grads, [slot_spec] + [ANY] * 3, [canvas, canvas, sems, pltpu.VMEM((points // 128, points, 128), jnp.float32)], 2 * flops)
    grad_probe, *grad_zero = call(
        third_kernel, scalars, (object_slab, right, lower, corner, probe_wave, grad_wave, *spread_back),
        [ANY] * 4 + [whole(probe_wave), slot_spec] + [whole(t) for t in spread_back],
        [jax.ShapeDtypeStruct(probe_wave.shape, jnp.float32)] + grads,
        [whole(probe_wave)] + [ANY] * 3, [canvas, canvas, sems], flops)

    right_back, lower_back, new_probe = send_back(
        [grad_zero[1], grad_one[1]], [grad_zero[2], grad_one[2]], grad_probe, probe_wave, PROBE_RATE / total_frames, tile_rows)
    right_back = jnp.where(col_index > 0, right_back, 0.0)
    lower_back = jnp.where(row_index > 0, lower_back, 0.0)
    total = jnp.stack([grad_zero[0], grad_one[0]])
    total = total + jnp.pad(right_back, ((0, 0), (0, 0), (0, 0), (0, tile_cols - points)))
    total = total + jnp.pad(lower_back, ((0, 0), (0, 0), (0, tile_rows - points), (0, 0)))
    return (object_slab - OBJECT_RATE * total, new_probe)


def solution(mesh):
    return jax.shard_map(
        local,
        mesh=mesh,
        in_specs=(P(None, None, "ty", "tx"), P(), P("tx", None, None), P(), P()),
        out_specs=(P(None, None, "ty", "tx"), P()),
        check_vma=False,
    )
```

```python
import functools
import math

import jax
import jax.numpy as jnp
import ml_dtypes
import numpy as np
from jax import lax
from jax.experimental import pallas as pl
from jax.experimental.pallas import tpu as pltpu
from jax.sharding import PartitionSpec as P

MESH = pl.DeviceIdType.MESH
TILE_CAP = 8
HOPS = 4
BACKGROUND = 0.5
FRESNEL = 0.25
OBJECT_RATE = 0.25
PROBE_RATE = 4.0
VMEM_LIMIT = 56 * 1024 * 1024


FRAME_STEPS = ((1, 0, 0), (3, 0, 0), (0, 1, 1), (2, 0, 0), (1, 1, 1), (3, 1, 1), (0, 1, 0), (2, 1, 1), (1, 0, 1), (3, 0, 1), (2, 0, 1),
               (1, 1, 0), (3, 1, 0), (2, 1, 0), (0, 0, 1))


def real_form(matrix):
    return np.block([[matrix.real, -matrix.imag], [matrix.imag, matrix.real]])


def split_table(table):
    high = table.astype(ml_dtypes.bfloat16)
    low = (table - high.astype(np.float64)).astype(ml_dtypes.bfloat16)
    return high, low


def left_table(table):
    return np.concatenate(split_table(table), axis=1)


def right_table(table):
    return np.concatenate(split_table(table), axis=0)


def half_transforms(points):
    half = points // 2
    places = np.arange(half)
    even = np.exp(-2j * np.pi * ((2 * places[:, None]) * places[None, :] % points) / points)
    odd = np.exp(-2j * np.pi * ((2 * places[:, None] + 1) * places[None, :] % points) / points)
    return even / math.sqrt(points), odd / math.sqrt(points)


def build_tables(points):
    even, odd = half_transforms(points)
    places = np.arange(points)
    frequency = (places + points // 2) % points - points // 2
    phase = np.exp(-1j * np.pi * FRESNEL / points * frequency.astype(np.float64) ** 2)
    spread_even = even.conj().T @ (phase[0::2, None] * even)
    spread_odd = odd.conj().T @ (phase[1::2, None] * odd)
    spread = [real_form(spread_even), real_form(spread_odd)]
    fourier = [real_form(even), real_form(odd)]
    order = np.concatenate([places[0::2], places[1::2]])
    shuffle = (places[:, None] == order[None, :]).astype(ml_dtypes.bfloat16)

    groups = [spread, [table.T for table in spread], fourier, [table.T for table in fourier]]
    left = np.stack([left_table(table) for group in groups for table in group])
    right = np.stack([right_table(table.T) for group in groups for table in group])
    return left, right, shuffle


def split(value):
    high = value.astype(jnp.bfloat16)
    low = (value - high.astype(jnp.float32)).astype(jnp.bfloat16)
    return high, low


def left_product(table, value):
    high, low = split(value)
    size = value.shape[0]
    table = jnp.concatenate([table[...], table[:, :size]], axis=1)
    return jnp.dot(table, jnp.concatenate([high, high, low], axis=0), preferred_element_type=jnp.float32)


def right_product(value, table):
    high, low = split(value)
    size = value.shape[1]
    table = jnp.concatenate([table[...], table[:size, :]], axis=0)
    return jnp.dot(jnp.concatenate([high, high, low], axis=1), table, preferred_element_type=jnp.float32)


def halves(value, axis):
    half = value.shape[axis] // 2
    first = lax.slice_in_dim(value, 0, half, axis=axis)
    second = lax.slice_in_dim(value, half, 2 * half, axis=axis)
    return first, second


def apart(real, imag, axis):
    real_a, real_b = halves(real, axis)
    imag_a, imag_b = halves(imag, axis)
    plus = jnp.concatenate([real_a + real_b, imag_a + imag_b], axis=axis)
    minus = jnp.concatenate([real_a - real_b, imag_a - imag_b], axis=axis)
    return plus, minus


def together(plus, minus, axis):
    plus_re, plus_im = halves(plus, axis)
    minus_re, minus_im = halves(minus, axis)
    real = jnp.concatenate([plus_re + minus_re, plus_re - minus_re], axis=axis)
    imag = jnp.concatenate([plus_im + minus_im, plus_im - minus_im], axis=axis)
    return real, imag


def regroup(even, odd, axis):
    even_re, even_im = halves(even, axis)
    odd_re, odd_im = halves(odd, axis)
    return jnp.concatenate([even_re, odd_re], axis=axis), jnp.concatenate([even_im, odd_im], axis=axis)


def spread(real, imag, tables):
    left_even, left_odd, right_even, right_odd = tables
    plus, minus = apart(real, imag, 0)
    real, imag = together(left_product(left_even, plus), left_product(left_odd, minus), 0)
    plus, minus = apart(real, imag, 1)
    return together(right_product(plus, right_even), right_product(minus, right_odd), 1)


def to_frequencies(real, imag, tables):
    left_even, left_odd, right_even, right_odd = tables
    plus, minus = apart(real, imag, 0)
    real, imag = regroup(left_product(left_even, plus), left_product(left_odd, minus), 0)
    plus, minus = apart(real, imag, 1)
    return regroup(right_product(plus, right_even), right_product(minus, right_odd), 1)


def from_frequencies(real, imag, tables):
    left_even, left_odd, right_even, right_odd = tables
    even, odd = regroup(real, imag, 0)
    real, imag = together(left_product(left_even, even), left_product(left_odd, odd), 0)
    even, odd = regroup(real, imag, 1)
    return together(right_product(even, right_even), right_product(odd, right_odd), 1)


def place_of(row, column, points):
    return pl.ds(row, points), column // 128, lax.rem(column, 128)


def window_of(canvas, layer, place, points):
    rows, first, along = place
    before = lax.broadcasted_iota(jnp.int32, (points, 128), 1) < 128 - along
    parts = []
    for part in range(2):
        turned = [
            pltpu.roll(canvas[layer, part, first + step, rows, :], lax.rem(128 - along, 128), 1)
            for step in range(points // 128 + 1)
        ]
        parts.append(jnp.concatenate([jnp.where(before, one, other) for one, other in zip(turned, turned[1:])], axis=1))
    return parts


def add_window(canvas, layer, place, points, parts):
    rows, first, along = place
    inside = lax.broadcasted_iota(jnp.int32, (points, 128), 1) >= along
    for part in range(2):
        turned = [pltpu.roll(parts[part][:, at:at + 128], along, 1) for at in range(0, points, 128)]
        none = jnp.zeros((points, 128), jnp.float32)
        for step, (one, other) in enumerate(zip(turned + [none], [none] + turned)):
            canvas[layer, part, first + step, rows, :] += jnp.where(inside, one, other)


def times(a, b):
    return a[0] * b[0] - a[1] * b[1], a[0] * b[1] + a[1] * b[0]


def times_conjugate(a, b):
    return a[0] * b[0] + a[1] * b[1], a[0] * b[1] - a[1] * b[0]


def gradient_kernel(offsets, count, owners, slab, right, lower, corner, arrived, probe, left_all, right_all, shuffle_all, moved,
                    grad_right, grad_lower, grad_probe, canvas, grad, frame, columns, left_held, right_held, shuffle, load_sems,
                    table_sems, frame_sems, out_sems):
    table_loads = [
        pltpu.make_async_copy(source, target, table_sems.at[at])
        for at, (source, target) in enumerate(((left_all, left_held), (right_all, right_held), (shuffle_all, shuffle)))
    ]
    spread_ahead, spread_back, fourier_ahead, fourier_back = (
        [left_held.at[at], left_held.at[at + 1], right_held.at[at], right_held.at[at + 1]] for at in range(0, 8, 2))
    layers, rows, cols = slab.shape[0], slab.shape[2], slab.shape[3]
    points = probe.shape[1]
    half = points // 2
    own_lanes, more_lanes = cols // 128, points // 128
    own, beside = pl.ds(0, rows), pl.ds(rows, points)

    def lanes(number):
        return pl.ds(128 * number, 128)

    def frame_copy(slot):
        return pltpu.make_async_copy(arrived.at[owners[slot]], frame.at[lax.rem(slot, 2)], frame_sems.at[lax.rem(slot, 2)])

    pairs = []
    for layer in range(layers):
        for number in range(own_lanes):
            pairs.append((slab.at[layer, :, :, lanes(number)], canvas.at[layer, :, number, own, :]))
            pairs.append((lower.at[layer, :, :, lanes(number)], canvas.at[layer, :, number, beside, :]))
        for number in range(more_lanes):
            pairs.append((right.at[layer, :, :, lanes(number)], canvas.at[layer, :, own_lanes + number, own, :]))
            pairs.append((corner.at[layer, :, :, lanes(number)], canvas.at[layer, :, own_lanes + number, beside, :]))
    loads = [pltpu.make_async_copy(source, target, load_sems.at[at]) for at, (source, target) in enumerate(pairs)]
    for load in loads + table_loads:
        load.start()

    @pl.when(count[0] > 0)
    def _():
        frame_copy(0).start()

    grad[...] = jnp.zeros_like(grad)
    grad_probe[...] = jnp.zeros_like(grad_probe)
    for load in loads + table_loads:
        load.wait()

    @pl.when(lax.axis_index("ty") == lax.axis_size("ty") - 1)
    def _():
        canvas[:, :, :, beside, :] = jnp.zeros((layers, 2, own_lanes + more_lanes, points, 128), jnp.float32)

    @pl.when(lax.axis_index("tx") == lax.axis_size("tx") - 1)
    def _():
        canvas[:, :, pl.ds(own_lanes, more_lanes)] = jnp.zeros((layers, 2, more_lanes, rows + points, 128), jnp.float32)

    def visit(slot, carry):
        place = place_of(offsets[2 * slot], offsets[2 * slot + 1], points)
        frame_copy(slot).wait()

        @pl.when(slot + 1 < count[0])
        def _():
            frame_copy(slot + 1).start()

        probe_wave = (probe[0], probe[1])
        windows = [window_of(canvas, layer, place, points) for layer in range(layers)]
        wave = spread(*times(probe_wave, windows[0]), spread_ahead)
        real, imag = to_frequencies(*times(wave, windows[1]), fourier_ahead)
        pieces = []
        for side in range(points // 128):
            columns[side] = jnp.sqrt(frame[lax.rem(slot, 2), :, pl.ds(side * 128, 128)] + BACKGROUND)
            pieces.append(jnp.concatenate([columns[side, pl.ds(start, half, stride=2), :] for start in range(2)], axis=0))
        target = jnp.concatenate(pieces, axis=1)
        high = target.astype(jnp.bfloat16)
        rest = target - high.astype(jnp.float32)
        middle = rest.astype(jnp.bfloat16)
        low = (rest - middle.astype(jnp.float32)).astype(jnp.bfloat16)
        target = jnp.dot(
            jnp.concatenate([high, middle, low], axis=1), jnp.concatenate([shuffle[...]] * 3, axis=0),
            preferred_element_type=jnp.float32)
        pull = 2.0 - 2.0 * target * lax.rsqrt(real * real + imag * imag + BACKGROUND)
        back = from_frequencies(pull * real, pull * imag, fourier_back)
        add_window(grad, 1, place, points, times_conjugate(wave, back))
        back = times_conjugate(windows[1], back)
        back = spread(*back, spread_back)
        add_window(grad, 0, place, points, times_conjugate(probe_wave, back))
        more = times_conjugate(windows[0], back)
        grad_probe[0] += more[0]
        grad_probe[1] += more[1]
        return carry

    lax.fori_loop(0, count[0], visit, 0)
    writes = [
        pltpu.make_async_copy(grad.at[:, :, own_lanes + number], grad_right.at[:, :, :, lanes(number)], out_sems.at[number])
        for number in range(more_lanes)
    ]
    writes += [
        pltpu.make_async_copy(grad.at[:, :, number, beside, :], grad_lower.at[:, :, :, lanes(number)], out_sems.at[more_lanes + number])
        for number in range(own_lanes)
    ]
    for write in writes:
        write.start()
    for number in range(own_lanes):
        canvas[:, :, number, :rows, :] -= OBJECT_RATE * grad[:, :, number, :rows, :]
        writes.append(pltpu.make_async_copy(
            canvas.at[:, :, number, own, :], moved.at[:, :, :, lanes(number)], out_sems.at[more_lanes + own_lanes + number]))
        writes[-1].start()
    for write in writes:
        write.wait()


ANY = pl.BlockSpec(memory_space=pl.ANY)
WHOLE = pl.BlockSpec(memory_space=pltpu.VMEM)


def gradients(scalars, object_slab, right, lower, corner, arrived, probe_wave):
    layers, _, rows, cols = object_slab.shape
    points = probe_wave.shape[-1]
    tables = build_tables(points)
    shape = lambda *dims: jax.ShapeDtypeStruct(dims, jnp.float32)
    canvas = pltpu.VMEM((layers, 2, (cols + points) // 128, rows + points, 128), jnp.float32)
    lanes = (cols + points) // 128
    return pl.pallas_call(
        gradient_kernel,
        out_shape=[shape(*object_slab.shape), shape(layers, 2, rows + points, points), shape(layers, 2, points, cols),
                   shape(*probe_wave.shape)],
        grid_spec=pltpu.PrefetchScalarGridSpec(
            num_scalar_prefetch=len(scalars),
            grid=(1,),
            in_specs=[ANY] * 5 + [WHOLE] + [ANY] * len(tables),
            out_specs=[ANY] * 3 + [WHOLE],
            scratch_shapes=[
                canvas, canvas,
                pltpu.VMEM((2, points, points), jnp.float32),
                pltpu.VMEM((points // 128, points, 128), jnp.float32),
                *[pltpu.VMEM(table.shape, jnp.bfloat16) for table in tables],
                pltpu.SemaphoreType.DMA((2 * layers * lanes,)),
                pltpu.SemaphoreType.DMA((len(tables),)),
                pltpu.SemaphoreType.DMA((2,)),
                pltpu.SemaphoreType.DMA((lanes + cols // 128,)),
            ]),
        compiler_params=pltpu.CompilerParams(vmem_limit_bytes=VMEM_LIMIT),
        cost_estimate=pl.CostEstimate(flops=TILE_CAP * 96 * points**3, bytes_accessed=32 * 1024 * 1024, transcendentals=0),
    )(*scalars, object_slab, right, lower, corner, arrived, probe_wave, *tables)


def finish_kernel(moved, right, lower, out):
    points = right.shape[3]
    out[...] = moved[...]

    @pl.when(lax.axis_index("tx") > 0)
    def _():
        out[0, 0, :, :points] -= OBJECT_RATE * right[0, 0]

    @pl.when(lax.axis_index("ty") > 0)
    def _():
        out[0, 0, :points, :] -= OBJECT_RATE * lower[0, 0]


def finish(moved, right, lower):
    plane = lambda array: pl.BlockSpec((1, 1) + array.shape[2:], lambda layer, part: (layer, part, 0, 0))
    return pl.pallas_call(
        finish_kernel,
        out_shape=jax.ShapeDtypeStruct(moved.shape, moved.dtype),
        grid=moved.shape[:2],
        in_specs=[plane(moved), plane(right), plane(lower)],
        out_specs=plane(moved),
        compiler_params=pltpu.CompilerParams(vmem_limit_bytes=VMEM_LIMIT),
        cost_estimate=pl.CostEstimate(flops=3 * moved.size, bytes_accessed=12 * moved.size, transcendentals=0),
    )(moved, right, lower)


def remote(source, target, send_sem, recv_sem, peer):
    return pltpu.make_async_remote_copy(
        src_ref=source, dst_ref=target, send_sem=send_sem, recv_sem=recv_sem, device_id=peer, device_id_type=MESH)


def when(condition, action):
    pl.when(condition)(lambda: action())


def greet(peers):
    barrier = pltpu.get_barrier_semaphore()
    for peer in peers:
        pl.semaphore_signal(barrier, inc=1, device_id=peer, device_id_type=MESH)
    pl.semaphore_wait(barrier, len(peers))


def around(down, along, n_down, n_along):
    row = [(down, lax.rem(along + step, n_along)) for step in range(1, n_along)]
    column = [(lax.rem(down + step, n_down), along) for step in range(1, n_down)]
    return row, column


def frame_peer(down, along, n_down, n_along, step, ahead):
    step_y, step_z, step_core = step
    if not ahead:
        step_y = -step_y % (n_along // 4)
    place_y, place_z, core = along // 4, lax.rem(along // 2, 2), lax.rem(along, 2)
    other = step_z * jnp.maximum(step_core, core)
    place_y = lax.rem(place_y + step_y, n_along // 4)
    place_z = lax.rem(place_z + step_z, 2)
    core = lax.rem(core + step_core, 2)
    return (lax.rem(down + other * (n_down // 2), n_down), place_y * 4 + place_z * 2 + core), other


def fetch_kernel(source, frames, slab, right, lower, corner, arrived, held, picked, lower_relay, right_relay, held_sem, own_sem,
                 send_sems, recv_sems):
    down, along = lax.axis_index("ty"), lax.axis_index("tx")
    n_down, n_along = lax.axis_size("ty"), lax.axis_size("tx")
    layers, points, rows, cols = right.shape[0], right.shape[3], right.shape[2], lower.shape[3]
    half = n_down // 2
    load = pltpu.make_async_copy(frames, held, held_sem)
    load.start()
    ring = lambda by_down, by_along: (lax.rem(down + by_down + n_down, n_down), lax.rem(along + by_along + n_along, n_along))
    greet([frame_peer(down, along, n_down, n_along, step, False)[0] for step in FRAME_STEPS]
          + [ring(by, 0) for by in (1, -1, half, 3, -3)] + [ring(0, by) for by in (1, -1, 3, -3, 4, -4)])
    above, left = ring(-1, 0), ring(0, -1)
    not_top, not_bottom = down > 0, down < n_down - 1
    not_first, not_last = along > 0, along < n_along - 1
    wraps, passes = down == half, down == 0
    crosses, carries = lax.rem(along, 4) == 0, lax.rem(along, 4) == 3
    crossed = carries & not_last
    across = crosses & not_first
    base = n_along - 1
    index = iter(range(base, base + 64))

    def copy(source_ref, target, peer, at=None):
        at = next(index) if at is None else at
        return remote(source_ref, target, send_sems.at[at], recv_sems.at[at], peer)

    first, last = 0, layers - 1
    side = [slab.at[layer, :, :, pl.ds(0, points)] for layer in range(layers)]
    edge = [lower.at[layer, :, :, pl.ds(0, points)] for layer in range(layers)]
    rest, start = pl.ds(points, cols - points), pl.ds(0, points)
    lowers, others, hops, forwards, rights, corners = [], [], [], [], [], []
    for layer in range(layers):
        lowers.append(copy(slab.at[layer, :, pl.ds(0, points), start], lower.at[layer, :, :, start], above))
        at = next(index)
        others.append(copy(slab.at[layer, :, pl.ds(0, points), rest], lower.at[layer, :, :, rest], above, at))
        chunk = points // HOPS
        for number in range(HOPS):
            here = pl.ds(number * chunk, chunk)
            hop_at = next(index)
            hops.append(copy(slab.at[layer, :, here, rest], lower_relay.at[layer, :, here, :], ring(half, 0), hop_at))
            forwards.append(remote(
                lower_relay.at[layer, :, here, :], lower.at[layer, :, here, rest], send_sems.at[hop_at], recv_sems.at[at], ring(3, 0)))
        rights.append(copy(side[layer], right.at[layer], left))
        corners.append(copy(edge[layer], corner.at[layer], left))
    per_layer = 4 + HOPS
    at_right, at_corner = base + per_layer * layers - 2, base + per_layer * layers - 1
    right_hop = copy(side[last], right_relay.at[:, pl.ds(0, rows), :], ring(0, 3))
    right_forward = copy(right_relay.at[:, pl.ds(0, rows), :], right.at[last], ring(0, -4), at_right)
    corner_hop = copy(edge[last], right_relay.at[:, pl.ds(rows, points), :], ring(0, 3))
    corner_forward = copy(right_relay.at[:, pl.ds(rows, points), :], corner.at[last], ring(0, -4), at_corner)

    for layer in range(layers):
        when(not_top, lowers[layer].start)
        when(not_top & ~wraps, others[layer].start)
    when(across, right_hop.start)
    when(not_first & ~crosses, rights[last].start)
    when(not_first, rights[first].start)
    load.wait()
    sends = []
    for step, offset in enumerate(FRAME_STEPS):
        peer, other = frame_peer(down, along, n_down, n_along, offset, True)
        picked[step] = held[source[other * n_along + peer[1]]]
        send = remote(picked.at[step], arrived.at[along], send_sems.at[step], recv_sems.at[step], peer)
        send.start()
        sends.append(send)
    for hop in hops:
        when(wraps, hop.start)
    picked[n_along - 1] = held[source[along]]
    own = pltpu.make_async_copy(picked.at[n_along - 1], arrived.at[along], own_sem)
    own.start()
    relays = along >= 4
    for hop, forward in zip(hops, forwards):
        when(passes, hop.wait_recv)
        when(passes, forward.start)
    when(carries & relays, right_hop.wait_recv)
    when(carries & relays, right_forward.start)
    for layer in range(layers):
        when(not_bottom, lowers[layer].wait_recv)
        if layer == last:
            when(not_bottom & across, corner_hop.start)
            when(not_bottom & not_first & ~crosses, corners[layer].start)
            when(not_bottom & carries & relays, corner_hop.wait_recv)
            when(not_bottom & carries & relays, corner_forward.start)
        else:
            when(not_bottom & not_first, corners[layer].start)
    for layer in range(layers):
        when(not_bottom, others[layer].wait_recv)
        when(not_last, rights[layer].wait_recv)
        when(not_bottom & not_last, corners[layer].wait_recv)
        when(not_top, lowers[layer].wait_send)
        when(not_top & ~wraps, others[layer].wait_send)
        if layer == last:
            when(across, right_hop.wait_send)
            when(not_first & ~crosses, rights[layer].wait_send)
            when(carries & relays, right_forward.wait_send)
            when(not_bottom & across, corner_hop.wait_send)
            when(not_bottom & not_first & ~crosses, corners[layer].wait_send)
            when(not_bottom & carries & relays, corner_forward.wait_send)
        else:
            when(not_first, rights[layer].wait_send)
            when(not_bottom & not_first, corners[layer].wait_send)
    for hop, forward in zip(hops, forwards):
        when(wraps, hop.wait_send)
        when(passes, forward.wait_send)
    for send in sends:
        send.wait()
    own.wait()


def fetch(source, frames, object_slab, points):
    layers, _, rows, cols = object_slab.shape
    n_along = lax.axis_size("tx")
    copies = n_along - 1 + (4 + HOPS) * layers + 2
    shape = lambda *dims: jax.ShapeDtypeStruct(dims, jnp.float32)
    return pl.pallas_call(
        fetch_kernel,
        out_shape=[shape(layers, 2, rows, points), shape(layers, 2, points, cols), shape(layers, 2, points, points),
                   shape(n_along, points, points)],
        in_specs=[pl.BlockSpec(memory_space=pltpu.SMEM), ANY, ANY],
        out_specs=[ANY] * 4,
        scratch_shapes=[
            pltpu.VMEM(frames.shape, jnp.float32),
            pltpu.VMEM((n_along, points, points), jnp.float32),
            pltpu.VMEM((layers, 2, points, cols - points), jnp.float32),
            pltpu.VMEM((2, rows + points, points), jnp.float32),
            pltpu.SemaphoreType.DMA,
            pltpu.SemaphoreType.DMA,
            pltpu.SemaphoreType.DMA((copies,)),
            pltpu.SemaphoreType.DMA((copies,)),
        ],
        compiler_params=pltpu.CompilerParams(collective_id=0, has_side_effects=True, vmem_limit_bytes=VMEM_LIMIT),
    )(source, frames, object_slab)


def return_kernel(scale, all_right, all_lower, grad_probe, probe, right_in, lower_in, probe_out,
                  corner_in, held, relay, from_row, row_sum, from_column, load_sems, send_sems, recv_sems):
    down, along = lax.axis_index("ty"), lax.axis_index("tx")
    n_down, n_along = lax.axis_size("ty"), lax.axis_size("tx")
    rights, lowers = ([ref.at[layer] for layer in range(ref.shape[0])] for ref in (all_right, all_lower))
    layers, points, rows, cols = len(rights), right_in.shape[3], right_in.shape[2], lower_in.shape[3]
    loads = [
        pltpu.make_async_copy(lowers[layer].at[:, :, pl.ds(0, points)], held.at[layer], load_sems.at[layer])
        for layer in range(layers)
    ]
    for load in loads:
        load.start()
    row_peers, column_peers = around(down, along, n_down, n_along)
    greet(row_peers + column_peers)
    part = grad_probe.shape[0] // n_along

    def piece_of(number, start):
        return pl.ds(pl.multiple_of(start + number // 2 * 8, 8), 8), pl.ds(pl.multiple_of(lax.rem(number, 2) * 128, 128), 128)

    below, after = (lax.rem(down + 1, n_down), along), (down, lax.rem(along + 1, n_along))
    not_top, not_bottom = down > 0, down < n_down - 1
    not_first, not_last = along > 0, along < n_along - 1

    def exchange(index, source, target, peer):
        copy = remote(source, target, send_sems.at[index], recv_sems.at[index], peer)
        copy.start()
        return copy

    def aligned(start, size):
        return pl.ds(pl.multiple_of(start, 8), size)

    row_copies = [
        exchange(step, grad_probe.at[aligned(peer[1] * part, part)], from_row.at[step], peer) for step, peer in enumerate(row_peers)
    ]
    base = 2 * (n_along + n_down - 2)
    corners, sides, firsts, seconds, hops, forwards = [], [], [], [], [], []
    half = n_down // 2
    wraps, passes = down == half - 1, down == n_down - 1
    over, down_three = (lax.rem(down + half, n_down), along), (lax.rem(down + n_down - 3, n_down), along)
    for layer in range(layers):
        at = base + 4 * layer
        corners.append(remote(rights[layer].at[:, pl.ds(rows, points), :], corner_in.at[layer], send_sems.at[at], recv_sems.at[at], after))
        sides.append(remote(rights[layer].at[:, pl.ds(0, rows), :], right_in.at[layer], send_sems.at[at + 1], recv_sems.at[at + 1], after))
        rest = pl.ds(points, cols - points)
        firsts.append(remote(lowers[layer].at[:, :, rest], lower_in.at[layer, :, :, rest], send_sems.at[at + 2], recv_sems.at[at + 2], below))
        seconds.append(remote(held.at[layer], lower_in.at[layer, :, :, pl.ds(0, points)], send_sems.at[at + 3], recv_sems.at[at + 3], below))
        chunk = points // HOPS
        hops.append([])
        forwards.append([])
        for number in range(HOPS):
            here = pl.ds(number * chunk, chunk)
            hop_at = base + 4 * layers + HOPS * layer + number
            hops[-1].append(remote(
                lowers[layer].at[:, here, rest], relay.at[layer, :, here, :], send_sems.at[hop_at], recv_sems.at[hop_at], over))
            forwards[-1].append(remote(
                relay.at[layer, :, here, :], lower_in.at[layer, :, here, rest], send_sems.at[hop_at], recv_sems.at[at + 2], down_three))
    for layer in range(layers):
        when(not_bottom & not_last, corners[layer].start)

    total = grad_probe[aligned(along * part, part)]
    for step, copy in enumerate(row_copies):
        copy.wait()
        total = total + from_row[step]
    row_sum[...] = total
    at = n_along - 1
    copies = [
        exchange(at + step, row_sum.at[piece_of(peer[0], 0)], from_column.at[step], peer)
        for step, peer in enumerate(column_peers)
    ]
    total = row_sum[piece_of(down, 0)]
    for step, copy in enumerate(copies):
        copy.wait()
        total = total + from_column[step]
    mine = piece_of(down, along * part)
    probe_out[mine] = probe[mine] - scale * total
    at += n_down - 1
    copies = [exchange(at + step, probe_out.at[mine], probe_out.at[mine], peer) for step, peer in enumerate(column_peers)]
    for layer in range(layers):
        for hop in hops[layer]:
            when(wraps, hop.start)
    for layer in range(layers):
        when(not_bottom & ~wraps, firsts[layer].start)
    for copy in copies:
        copy.wait()
    at += n_down - 1
    mine = aligned(along * part, part)
    row_copies = [exchange(at + step, probe_out.at[mine], probe_out.at[mine], peer) for step, peer in enumerate(row_peers)]
    for layer in range(layers):
        when(not_last, sides[layer].start)

    for layer in range(layers):
        loads[layer].wait()
        when(not_bottom & not_first, corners[layer].wait_recv)

        @pl.when(not_bottom & not_first)
        def _():
            held[layer] += corner_in[layer]

        when(not_bottom, seconds[layer].start)
    for layer in range(layers):
        for hop, forward in zip(hops[layer], forwards[layer]):
            when(passes, hop.wait_recv)
            when(passes, forward.start)
    for copy in row_copies:
        copy.wait()
    for layer in range(layers):
        when(not_bottom & not_last, corners[layer].wait_send)
        when(not_last, sides[layer].wait_send)
        when(not_first, sides[layer].wait_recv)
        when(not_bottom & ~wraps, firsts[layer].wait_send)
        when(not_top, firsts[layer].wait_recv)
        for hop, forward in zip(hops[layer], forwards[layer]):
            when(wraps, hop.wait_send)
            when(passes, forward.wait_send)
        when(not_bottom, seconds[layer].wait_send)
        when(not_top, seconds[layer].wait_recv)


def send_back(grad_right, grad_lower, grad_probe, probe_wave, scale, rows):
    layers, _, points, cols = grad_lower.shape
    flat = (2 * points, points)
    n_down, n_along = lax.axis_size("ty"), lax.axis_size("tx")
    part = flat[0] // n_along
    copies = 2 * (n_along + n_down - 2) + (4 + HOPS) * layers
    shape = lambda *dims: jax.ShapeDtypeStruct(dims, jnp.float32)
    right_in, lower_in, probe = pl.pallas_call(
        functools.partial(return_kernel, scale),
        out_shape=[shape(layers, 2, rows, points), shape(layers, 2, points, cols), shape(*flat)],
        in_specs=[ANY, ANY, WHOLE, WHOLE],
        out_specs=[ANY, ANY, WHOLE],
        scratch_shapes=[
            pltpu.VMEM((layers, 2, points, points), jnp.float32),
            pltpu.VMEM((layers, 2, points, points), jnp.float32),
            pltpu.VMEM((layers, 2, points, cols - points), jnp.float32),
            pltpu.VMEM((n_along - 1, part, points), jnp.float32),
            pltpu.VMEM((part, points), jnp.float32),
            pltpu.VMEM((n_down - 1, 8, 128), jnp.float32),
            pltpu.SemaphoreType.DMA((layers,)),
            pltpu.SemaphoreType.DMA((copies,)),
            pltpu.SemaphoreType.DMA((copies,)),
        ],
        compiler_params=pltpu.CompilerParams(collective_id=1, has_side_effects=True, vmem_limit_bytes=VMEM_LIMIT),
    )(grad_right, grad_lower, grad_probe.reshape(flat), probe_wave.reshape(flat))
    return right_in, lower_in, probe.reshape(probe_wave.shape)


def local(object_slab, probe_wave, frames, scan_tiles, scan_offsets):
    columns = lax.axis_size("tx")
    row_index = lax.axis_index("ty")
    col_index = lax.axis_index("tx")
    owned = frames.shape[0]
    points = probe_wave.shape[-1]
    layers, _, tile_rows, tile_cols = object_slab.shape
    total_frames = owned * columns
    my_tile = row_index * columns + col_index
    by_owner = scan_tiles.reshape(columns, owned)

    mine = lax.dynamic_index_in_dim(by_owner, col_index, 0, keepdims=False)
    other_row = lax.rem(row_index + lax.axis_size("ty") // 2, lax.axis_size("ty"))
    places = jnp.arange(columns, dtype=jnp.int32)
    wanted = jnp.concatenate([row_index * columns + places, other_row * columns + places])
    source = jnp.sum((mine[None, :] == wanted[:, None]).astype(jnp.int32) * jnp.arange(owned, dtype=jnp.int32)[None, :], axis=1)

    right, lower, corner, arrived = fetch(source, frames, object_slab, points)

    matches = by_owner == my_tile
    present = jnp.any(matches, axis=1)
    which = jnp.sum(matches.astype(jnp.int32) * jnp.arange(owned, dtype=jnp.int32)[None, :], axis=1)
    global_ids = jnp.arange(columns, dtype=jnp.int32) * owned + which
    ranks = jnp.cumsum(present.astype(jnp.int32)) - 1
    slot_pick = (present[None, :] & (ranks[None, :] == jnp.arange(TILE_CAP, dtype=jnp.int32)[:, None])).astype(jnp.int32)
    chosen_ids = jnp.sum(slot_pick * global_ids[None, :], axis=1)
    owners = jnp.sum(slot_pick * jnp.arange(columns, dtype=jnp.int32)[None, :], axis=1)
    count = jnp.sum(present.astype(jnp.int32)).reshape(1)
    offsets = scan_offsets[chosen_ids].reshape(-1)
    scalars = (offsets, count, owners)

    moved, grad_right, grad_lower, grad_probe = gradients(scalars, object_slab, right, lower, corner, arrived, probe_wave)
    right_back, lower_back, new_probe = send_back(
        grad_right, grad_lower, grad_probe, probe_wave, PROBE_RATE / total_frames, object_slab.shape[2])
    return finish(moved, right_back, lower_back), new_probe


def solution(mesh):
    return jax.shard_map(
        local,
        mesh=mesh,
        in_specs=(P(None, None, "ty", "tx"), P(), P("tx", None, None), P(), P()),
        out_specs=(P(None, None, "ty", "tx"), P()),
        check_vma=False,
    )
```

```python
import functools
import math

import jax
import jax.numpy as jnp
import ml_dtypes
import numpy as np
from jax import lax
from jax.experimental import pallas as pl
from jax.experimental.pallas import tpu as pltpu
from jax.sharding import PartitionSpec as P

MESH = pl.DeviceIdType.MESH
TILE_CAP = 8
HOPS = 4
BACKGROUND = 0.5
FRESNEL = 0.25
OBJECT_RATE = 0.25
PROBE_RATE = 4.0
VMEM_LIMIT = 56 * 1024 * 1024


FRAME_STEPS = ((1, 0, 0), (3, 0, 0), (0, 1, 1), (2, 0, 0), (1, 1, 1), (3, 1, 1), (0, 1, 0), (2, 1, 1), (1, 0, 1), (3, 0, 1), (2, 0, 1),
               (1, 1, 0), (3, 1, 0), (2, 1, 0), (0, 0, 1))


def real_form(matrix):
    return np.block([[matrix.real, -matrix.imag], [matrix.imag, matrix.real]])


def split_table(table):
    high = table.astype(ml_dtypes.bfloat16)
    low = (table - high.astype(np.float64)).astype(ml_dtypes.bfloat16)
    return high, low


def left_table(table):
    return np.concatenate(split_table(table), axis=1)


def right_table(table):
    return np.concatenate(split_table(table), axis=0)


def half_transforms(points):
    half = points // 2
    places = np.arange(half)
    even = np.exp(-2j * np.pi * ((2 * places[:, None]) * places[None, :] % points) / points)
    odd = np.exp(-2j * np.pi * ((2 * places[:, None] + 1) * places[None, :] % points) / points)
    return even / math.sqrt(points), odd / math.sqrt(points)


def build_tables(points):
    even, odd = half_transforms(points)
    places = np.arange(points)
    frequency = (places + points // 2) % points - points // 2
    phase = np.exp(-1j * np.pi * FRESNEL / points * frequency.astype(np.float64) ** 2)
    spread_even = even.conj().T @ (phase[0::2, None] * even)
    spread_odd = odd.conj().T @ (phase[1::2, None] * odd)
    spread = [real_form(spread_even), real_form(spread_odd)]
    fourier = [real_form(even), real_form(odd)]
    order = np.concatenate([places[0::2], places[1::2]])
    shuffle = (places[:, None] == order[None, :]).astype(ml_dtypes.bfloat16)

    groups = [spread, [table.T for table in spread], fourier, [table.T for table in fourier]]
    left = np.stack([left_table(table) for group in groups for table in group])
    right = np.stack([right_table(table.T) for group in groups for table in group])
    return left, right, shuffle


def split(value):
    high = value.astype(jnp.bfloat16)
    low = (value - high.astype(jnp.float32)).astype(jnp.bfloat16)
    return high, low


def left_product(table, value):
    high, low = split(value)
    size = value.shape[0]
    table = jnp.concatenate([table[...], table[:, :size]], axis=1)
    return jnp.dot(table, jnp.concatenate([high, high, low], axis=0), preferred_element_type=jnp.float32)


def right_product(value, table):
    high, low = split(value)
    size = value.shape[1]
    table = jnp.concatenate([table[...], table[:size, :]], axis=0)
    return jnp.dot(jnp.concatenate([high, high, low], axis=1), table, preferred_element_type=jnp.float32)


def halves(value, axis):
    half = value.shape[axis] // 2
    first = lax.slice_in_dim(value, 0, half, axis=axis)
    second = lax.slice_in_dim(value, half, 2 * half, axis=axis)
    return first, second


def apart(real, imag, axis):
    real_a, real_b = halves(real, axis)
    imag_a, imag_b = halves(imag, axis)
    plus = jnp.concatenate([real_a + real_b, imag_a + imag_b], axis=axis)
    minus = jnp.concatenate([real_a - real_b, imag_a - imag_b], axis=axis)
    return plus, minus


def together(plus, minus, axis):
    plus_re, plus_im = halves(plus, axis)
    minus_re, minus_im = halves(minus, axis)
    real = jnp.concatenate([plus_re + minus_re, plus_re - minus_re], axis=axis)
    imag = jnp.concatenate([plus_im + minus_im, plus_im - minus_im], axis=axis)
    return real, imag


def regroup(even, odd, axis):
    even_re, even_im = halves(even, axis)
    odd_re, odd_im = halves(odd, axis)
    return jnp.concatenate([even_re, odd_re], axis=axis), jnp.concatenate([even_im, odd_im], axis=axis)


def spread(real, imag, tables):
    left_even, left_odd, right_even, right_odd = tables
    plus, minus = apart(real, imag, 0)
    real, imag = together(left_product(left_even, plus), left_product(left_odd, minus), 0)
    plus, minus = apart(real, imag, 1)
    return together(right_product(plus, right_even), right_product(minus, right_odd), 1)


def to_frequencies(real, imag, tables):
    left_even, left_odd, right_even, right_odd = tables
    plus, minus = apart(real, imag, 0)
    real, imag = regroup(left_product(left_even, plus), left_product(left_odd, minus), 0)
    plus, minus = apart(real, imag, 1)
    return regroup(right_product(plus, right_even), right_product(minus, right_odd), 1)


def from_frequencies(real, imag, tables):
    left_even, left_odd, right_even, right_odd = tables
    even, odd = regroup(real, imag, 0)
    real, imag = together(left_product(left_even, even), left_product(left_odd, odd), 0)
    even, odd = regroup(real, imag, 1)
    return together(right_product(even, right_even), right_product(odd, right_odd), 1)


def place_of(row, column, points):
    return pl.ds(row, points), column // 128, lax.rem(column, 128)


def window_of(canvas, layer, place, points):
    rows, first, along = place
    before = lax.broadcasted_iota(jnp.int32, (points, 128), 1) < 128 - along
    parts = []
    for part in range(2):
        turned = [
            pltpu.roll(canvas[layer, part, first + step, rows, :], lax.rem(128 - along, 128), 1)
            for step in range(points // 128 + 1)
        ]
        parts.append(jnp.concatenate([jnp.where(before, one, other) for one, other in zip(turned, turned[1:])], axis=1))
    return parts


def add_window(canvas, layer, place, points, parts):
    rows, first, along = place
    inside = lax.broadcasted_iota(jnp.int32, (points, 128), 1) >= along
    for part in range(2):
        turned = [pltpu.roll(parts[part][:, at:at + 128], along, 1) for at in range(0, points, 128)]
        none = jnp.zeros((points, 128), jnp.float32)
        for step, (one, other) in enumerate(zip(turned + [none], [none] + turned)):
            canvas[layer, part, first + step, rows, :] += jnp.where(inside, one, other)


def times(a, b):
    return a[0] * b[0] - a[1] * b[1], a[0] * b[1] + a[1] * b[0]


def times_conjugate(a, b):
    return a[0] * b[0] + a[1] * b[1], a[0] * b[1] - a[1] * b[0]


def gradient_kernel(offsets, count, owners, slab, right, lower, corner, arrived, probe, left_all, right_all, shuffle_all, moved,
                    grad_right, grad_lower, grad_probe, canvas, grad, frame, columns, left_held, right_held, shuffle, load_sems,
                    table_sems, frame_sems, out_sems):
    table_loads = [
        pltpu.make_async_copy(source, target, table_sems.at[at])
        for at, (source, target) in enumerate(((left_all, left_held), (right_all, right_held), (shuffle_all, shuffle)))
    ]
    spread_ahead, spread_back, fourier_ahead, fourier_back = (
        [left_held.at[at], left_held.at[at + 1], right_held.at[at], right_held.at[at + 1]] for at in range(0, 8, 2))
    layers, rows, cols = slab.shape[0], slab.shape[2], slab.shape[3]
    points = probe.shape[1]
    half = points // 2
    own_lanes, more_lanes = cols // 128, points // 128
    own, beside = pl.ds(0, rows), pl.ds(rows, points)

    def lanes(number):
        return pl.ds(128 * number, 128)

    def frame_copy(slot):
        return pltpu.make_async_copy(arrived.at[owners[slot]], frame.at[lax.rem(slot, 2)], frame_sems.at[lax.rem(slot, 2)])

    pairs = []
    for layer in range(layers):
        for number in range(own_lanes):
            pairs.append((slab.at[layer, :, :, lanes(number)], canvas.at[layer, :, number, own, :]))
            pairs.append((lower.at[layer, :, :, lanes(number)], canvas.at[layer, :, number, beside, :]))
        for number in range(more_lanes):
            pairs.append((right.at[layer, :, :, lanes(number)], canvas.at[layer, :, own_lanes + number, own, :]))
            pairs.append((corner.at[layer, :, :, lanes(number)], canvas.at[layer, :, own_lanes + number, beside, :]))
    loads = [pltpu.make_async_copy(source, target, load_sems.at[at]) for at, (source, target) in enumerate(pairs)]
    for load in loads + table_loads:
        load.start()

    @pl.when(count[0] > 0)
    def _():
        frame_copy(0).start()

    grad[...] = jnp.zeros_like(grad)
    grad_probe[...] = jnp.zeros_like(grad_probe)
    for load in loads + table_loads:
        load.wait()

    @pl.when(lax.axis_index("ty") == lax.axis_size("ty") - 1)
    def _():
        canvas[:, :, :, beside, :] = jnp.zeros((layers, 2, own_lanes + more_lanes, points, 128), jnp.float32)

    @pl.when(lax.axis_index("tx") == lax.axis_size("tx") - 1)
    def _():
        canvas[:, :, pl.ds(own_lanes, more_lanes)] = jnp.zeros((layers, 2, more_lanes, rows + points, 128), jnp.float32)

    def visit(slot, carry):
        place = place_of(offsets[2 * slot], offsets[2 * slot + 1], points)
        frame_copy(slot).wait()

        @pl.when(slot + 1 < count[0])
        def _():
            frame_copy(slot + 1).start()

        probe_wave = (probe[0], probe[1])
        windows = [window_of(canvas, layer, place, points) for layer in range(layers)]
        wave = spread(*times(probe_wave, windows[0]), spread_ahead)
        real, imag = to_frequencies(*times(wave, windows[1]), fourier_ahead)
        pieces = []
        for side in range(points // 128):
            columns[side] = jnp.sqrt(frame[lax.rem(slot, 2), :, pl.ds(side * 128, 128)] + BACKGROUND)
            pieces.append(jnp.concatenate([columns[side, pl.ds(start, half, stride=2), :] for start in range(2)], axis=0))
        target = jnp.concatenate(pieces, axis=1)
        high = target.astype(jnp.bfloat16)
        rest = target - high.astype(jnp.float32)
        middle = rest.astype(jnp.bfloat16)
        low = (rest - middle.astype(jnp.float32)).astype(jnp.bfloat16)
        target = jnp.dot(
            jnp.concatenate([high, middle, low], axis=1), jnp.concatenate([shuffle[...]] * 3, axis=0),
            preferred_element_type=jnp.float32)
        pull = 2.0 - 2.0 * target * lax.rsqrt(real * real + imag * imag + BACKGROUND)
        back = from_frequencies(pull * real, pull * imag, fourier_back)
        add_window(grad, 1, place, points, times_conjugate(wave, back))
        back = times_conjugate(windows[1], back)
        back = spread(*back, spread_back)
        add_window(grad, 0, place, points, times_conjugate(probe_wave, back))
        more = times_conjugate(windows[0], back)
        grad_probe[0] += more[0]
        grad_probe[1] += more[1]
        return carry

    lax.fori_loop(0, count[0], visit, 0)
    writes = [
        pltpu.make_async_copy(grad.at[:, :, own_lanes + number], grad_right.at[:, :, :, lanes(number)], out_sems.at[number])
        for number in range(more_lanes)
    ]
    writes += [
        pltpu.make_async_copy(grad.at[:, :, number, beside, :], grad_lower.at[:, :, :, lanes(number)], out_sems.at[more_lanes + number])
        for number in range(own_lanes)
    ]
    for write in writes:
        write.start()
    for number in range(own_lanes):
        canvas[:, :, number, :rows, :] -= OBJECT_RATE * grad[:, :, number, :rows, :]
        writes.append(pltpu.make_async_copy(
            canvas.at[:, :, number, own, :], moved.at[:, :, :, lanes(number)], out_sems.at[more_lanes + own_lanes + number]))
        writes[-1].start()
    for write in writes:
        write.wait()


ANY = pl.BlockSpec(memory_space=pl.ANY)
WHOLE = pl.BlockSpec(memory_space=pltpu.VMEM)


def gradients(scalars, object_slab, right, lower, corner, arrived, probe_wave):
    layers, _, rows, cols = object_slab.shape
    points = probe_wave.shape[-1]
    tables = build_tables(points)
    shape = lambda *dims: jax.ShapeDtypeStruct(dims, jnp.float32)
    canvas = pltpu.VMEM((layers, 2, (cols + points) // 128, rows + points, 128), jnp.float32)
    lanes = (cols + points) // 128
    return pl.pallas_call(
        gradient_kernel,
        out_shape=[shape(*object_slab.shape), shape(layers, 2, rows + points, points), shape(layers, 2, points, cols),
                   shape(*probe_wave.shape)],
        grid_spec=pltpu.PrefetchScalarGridSpec(
            num_scalar_prefetch=len(scalars),
            grid=(1,),
            in_specs=[ANY] * 5 + [WHOLE] + [ANY] * len(tables),
            out_specs=[ANY] * 3 + [WHOLE],
            scratch_shapes=[
                canvas, canvas,
                pltpu.VMEM((2, points, points), jnp.float32),
                pltpu.VMEM((points // 128, points, 128), jnp.float32),
                *[pltpu.VMEM(table.shape, jnp.bfloat16) for table in tables],
                pltpu.SemaphoreType.DMA((2 * layers * lanes,)),
                pltpu.SemaphoreType.DMA((len(tables),)),
                pltpu.SemaphoreType.DMA((2,)),
                pltpu.SemaphoreType.DMA((lanes + cols // 128,)),
            ]),
        compiler_params=pltpu.CompilerParams(vmem_limit_bytes=VMEM_LIMIT),
        cost_estimate=pl.CostEstimate(flops=TILE_CAP * 96 * points**3, bytes_accessed=32 * 1024 * 1024, transcendentals=0),
    )(*scalars, object_slab, right, lower, corner, arrived, probe_wave, *tables)


def finish_kernel(moved, right, lower, out):
    points = right.shape[3]
    out[...] = moved[...]

    @pl.when(lax.axis_index("tx") > 0)
    def _():
        out[0, 0, :, :points] -= OBJECT_RATE * right[0, 0]

    @pl.when(lax.axis_index("ty") > 0)
    def _():
        out[0, 0, :points, :] -= OBJECT_RATE * lower[0, 0]


def finish(moved, right, lower):
    plane = lambda array: pl.BlockSpec((1, 1) + array.shape[2:], lambda layer, part: (layer, part, 0, 0))
    return pl.pallas_call(
        finish_kernel,
        out_shape=jax.ShapeDtypeStruct(moved.shape, moved.dtype),
        grid=moved.shape[:2],
        in_specs=[plane(moved), plane(right), plane(lower)],
        out_specs=plane(moved),
        compiler_params=pltpu.CompilerParams(vmem_limit_bytes=VMEM_LIMIT),
        cost_estimate=pl.CostEstimate(flops=3 * moved.size, bytes_accessed=12 * moved.size, transcendentals=0),
    )(moved, right, lower)


def remote(source, target, send_sem, recv_sem, peer):
    return pltpu.make_async_remote_copy(
        src_ref=source, dst_ref=target, send_sem=send_sem, recv_sem=recv_sem, device_id=peer, device_id_type=MESH)


def when(condition, action):
    pl.when(condition)(lambda: action())


def greet(peers):
    barrier = pltpu.get_barrier_semaphore()
    for peer in peers:
        pl.semaphore_signal(barrier, inc=1, device_id=peer, device_id_type=MESH)
    pl.semaphore_wait(barrier, len(peers))


def detours(n_down, forward):
    half = n_down // 2
    paths = ((half - 1, n_down - 1, half), (half - 1, n_down - 2, half + 1, half), (half - 1, half - 2, half + 1, half))
    return paths if forward else [tuple(n_down - 1 - place for place in path) for path in paths]


def detour(path, along, sources, targets, relay, send_sems, recv_sems, at):
    hops = len(path) - 1
    route = []
    for number, (source, target) in enumerate(zip(sources, targets)):
        route.append([
            remote(
                source if hop == 0 else relay.at[number], target if hop == hops - 1 else relay.at[number],
                send_sems.at[at + number * hops + hop], recv_sems.at[at + number * hops + hop], (jnp.int32(path[hop + 1]), along))
            for hop in range(hops)
        ])
    return route


def set_off(route, path, down):
    for copies in route:
        when(down == path[0], copies[0].start)


def pass_on(routes, paths, down):
    for number in range(len(routes[0])):
        for route, path in zip(routes, paths):
            for hop in range(1, len(path) - 1):
                when(down == path[hop], route[number][hop - 1].wait_recv)
                when(down == path[hop], route[number][hop].start)


def arrive(routes, paths, down):
    for route, path in zip(routes, paths):
        for copies in route:
            when(down == path[-1], copies[-1].wait_recv)


def settle(routes, paths, down):
    for route, path in zip(routes, paths):
        for copies in route:
            for hop, copy in enumerate(copies):
                when(down == path[hop], copy.wait_send)


def around(down, along, n_down, n_along):
    row = [(down, lax.rem(along + step, n_along)) for step in range(1, n_along)]
    column = [(lax.rem(down + step, n_down), along) for step in range(1, n_down)]
    return row, column


def frame_peer(down, along, n_down, n_along, step, ahead):
    step_y, step_z, step_core = step
    if not ahead:
        step_y = -step_y % (n_along // 4)
    place_y, place_z, core = along // 4, lax.rem(along // 2, 2), lax.rem(along, 2)
    other = step_z * jnp.maximum(step_core, core)
    place_y = lax.rem(place_y + step_y, n_along // 4)
    place_z = lax.rem(place_z + step_z, 2)
    core = lax.rem(core + step_core, 2)
    return (lax.rem(down + other * (n_down // 2), n_down), place_y * 4 + place_z * 2 + core), other


def fetch_kernel(source, frames, slab, right, lower, corner, arrived, held, picked, lower_relay, right_relay, held_sem, own_sem,
                 send_sems, recv_sems):
    down, along = lax.axis_index("ty"), lax.axis_index("tx")
    n_down, n_along = lax.axis_size("ty"), lax.axis_size("tx")
    layers, points, rows, cols = right.shape[0], right.shape[3], right.shape[2], lower.shape[3]
    half = n_down // 2
    load = pltpu.make_async_copy(frames, held, held_sem)
    load.start()
    ring = lambda by_down, by_along: (lax.rem(down + by_down + n_down, n_down), lax.rem(along + by_along + n_along, n_along))
    greet([frame_peer(down, along, n_down, n_along, step, False)[0] for step in FRAME_STEPS]
          + [ring(by, 0) for by in (1, -1, half, 3, -3)] + [ring(0, by) for by in (1, -1, 3, -3, 4, -4)])
    above, left = ring(-1, 0), ring(0, -1)
    not_top, not_bottom = down > 0, down < n_down - 1
    not_first, not_last = along > 0, along < n_along - 1
    paths = detours(n_down, False)
    wraps, joins = down == half, down == half - 1
    crosses, carries = lax.rem(along, 4) == 0, lax.rem(along, 4) == 3
    crossed = carries & not_last
    across = crosses & not_first
    base = n_along - 1
    index = iter(range(base, base + 64))

    def copy(source_ref, target, peer, at=None):
        at = next(index) if at is None else at
        return remote(source_ref, target, send_sems.at[at], recv_sems.at[at], peer)

    first, last = 0, layers - 1
    side = [slab.at[layer, :, :, pl.ds(0, points)] for layer in range(layers)]
    edge = [lower.at[layer, :, :, pl.ds(0, points)] for layer in range(layers)]
    rest, start = pl.ds(points, cols - points), pl.ds(0, points)
    lowers, others, rights, corners = [], [], [], []
    for layer in range(layers):
        lowers.append(copy(slab.at[layer, :, pl.ds(0, points), start], lower.at[layer, :, :, start], above))
        others.append(copy(slab.at[layer, :, pl.ds(0, points), rest], lower.at[layer, :, :, rest], above))
        rights.append(copy(side[layer], right.at[layer], left))
        corners.append(copy(edge[layer], corner.at[layer], left))
    at_right, at_corner = base + 4 * last + 2, base + 4 * last + 3
    right_hop = copy(side[last], right_relay.at[:, pl.ds(0, rows), :], ring(0, 3))
    right_forward = copy(right_relay.at[:, pl.ds(0, rows), :], right.at[last], ring(0, -4), at_right)
    corner_hop = copy(edge[last], right_relay.at[:, pl.ds(rows, points), :], ring(0, 3))
    corner_forward = copy(right_relay.at[:, pl.ds(rows, points), :], corner.at[last], ring(0, -4), at_corner)

    chunk = points // HOPS
    routes = []
    at = base + 4 * layers + 2
    for number, (path, layer, lanes) in enumerate(zip(paths, (last, first, last), (start, rest, rest))):
        pieces = [pl.ds(piece * chunk, chunk) for piece in range(HOPS)]
        routes.append(detour(
            path, along, [slab.at[layer, :, piece, lanes] for piece in pieces], [lower.at[layer, :, piece, lanes] for piece in pieces],
            lower_relay.at[number], send_sems, recv_sems, at))
        at += HOPS * (len(path) - 1)
    ahead = (lowers[first], lowers[last], others[first], others[last])
    when(not_top, lowers[first].start)
    for go in ahead[1:]:
        when(not_top & ~wraps, go.start)
    when(across, right_hop.start)
    when(not_first & ~crosses, rights[last].start)
    when(not_first, rights[first].start)
    load.wait()
    sends = []
    for step, offset in enumerate(FRAME_STEPS):
        peer, other = frame_peer(down, along, n_down, n_along, offset, True)
        picked[step] = held[source[other * n_along + peer[1]]]
        send = remote(picked.at[step], arrived.at[along], send_sems.at[step], recv_sems.at[step], peer)
        send.start()
        sends.append(send)
    for route, path in zip(routes, paths):
        set_off(route, path, down)
    picked[n_along - 1] = held[source[along]]
    own = pltpu.make_async_copy(picked.at[n_along - 1], arrived.at[along], own_sem)
    own.start()
    relays = along >= 4
    when(carries & relays, right_hop.wait_recv)
    when(carries & relays, right_forward.start)
    pass_on(routes, paths, down)
    for layer in range(layers):
        if layer == last:
            arrive(routes[:1], paths[:1], down)
            when(not_bottom & ~joins, lowers[layer].wait_recv)
        else:
            when(not_bottom, lowers[layer].wait_recv)
        if layer == last:
            when(not_bottom & across, corner_hop.start)
            when(not_bottom & not_first & ~crosses, corners[layer].start)
            when(not_bottom & carries & relays, corner_hop.wait_recv)
            when(not_bottom & carries & relays, corner_forward.start)
        else:
            when(not_bottom & not_first, corners[layer].start)
    when(not_top, lowers[first].wait_send)
    for go in ahead[1:]:
        when(not_top & ~wraps, go.wait_send)
    for layer in range(layers):
        when(not_bottom & ~joins, others[layer].wait_recv)
        when(not_last, rights[layer].wait_recv)
        when(not_bottom & not_last, corners[layer].wait_recv)
        if layer == last:
            when(across, right_hop.wait_send)
            when(not_first & ~crosses, rights[layer].wait_send)
            when(carries & relays, right_forward.wait_send)
            when(not_bottom & across, corner_hop.wait_send)
            when(not_bottom & not_first & ~crosses, corners[layer].wait_send)
            when(not_bottom & carries & relays, corner_forward.wait_send)
        else:
            when(not_first, rights[layer].wait_send)
            when(not_bottom & not_first, corners[layer].wait_send)
    arrive(routes[1:], paths[1:], down)
    settle(routes, paths, down)
    for send in sends:
        send.wait()
    own.wait()


def fetch(source, frames, object_slab, points):
    layers, _, rows, cols = object_slab.shape
    n_along = lax.axis_size("tx")
    copies = n_along - 1 + 4 * layers + 2 + 8 * HOPS
    shape = lambda *dims: jax.ShapeDtypeStruct(dims, jnp.float32)
    return pl.pallas_call(
        fetch_kernel,
        out_shape=[shape(layers, 2, rows, points), shape(layers, 2, points, cols), shape(layers, 2, points, points),
                   shape(n_along, points, points)],
        in_specs=[pl.BlockSpec(memory_space=pltpu.SMEM), ANY, ANY],
        out_specs=[ANY] * 4,
        scratch_shapes=[
            pltpu.VMEM(frames.shape, jnp.float32),
            pltpu.VMEM((n_along, points, points), jnp.float32),
            pltpu.VMEM((3, HOPS, 2, points // HOPS, points), jnp.float32),
            pltpu.VMEM((2, rows + points, points), jnp.float32),
            pltpu.SemaphoreType.DMA,
            pltpu.SemaphoreType.DMA,
            pltpu.SemaphoreType.DMA((copies,)),
            pltpu.SemaphoreType.DMA((copies,)),
        ],
        compiler_params=pltpu.CompilerParams(collective_id=0, has_side_effects=True, vmem_limit_bytes=VMEM_LIMIT),
    )(source, frames, object_slab)


def return_kernel(scale, all_right, all_lower, grad_probe, probe, right_in, lower_in, probe_out,
                  corner_in, held, relay, from_row, row_sum, from_column, load_sems, send_sems, recv_sems):
    down, along = lax.axis_index("ty"), lax.axis_index("tx")
    n_down, n_along = lax.axis_size("ty"), lax.axis_size("tx")
    rights, lowers = ([ref.at[layer] for layer in range(ref.shape[0])] for ref in (all_right, all_lower))
    layers, points, rows, cols = len(rights), right_in.shape[3], right_in.shape[2], lower_in.shape[3]
    loads = [
        pltpu.make_async_copy(lowers[layer].at[:, :, pl.ds(0, points)], held.at[layer], load_sems.at[layer])
        for layer in range(layers)
    ]
    for load in loads:
        load.start()
    row_peers, column_peers = around(down, along, n_down, n_along)
    greet(row_peers + column_peers)
    part = grad_probe.shape[0] // n_along

    def piece_of(number, start):
        return pl.ds(pl.multiple_of(start + number // 2 * 8, 8), 8), pl.ds(pl.multiple_of(lax.rem(number, 2) * 128, 128), 128)

    below, after = (lax.rem(down + 1, n_down), along), (down, lax.rem(along + 1, n_along))
    not_top, not_bottom = down > 0, down < n_down - 1
    not_first, not_last = along > 0, along < n_along - 1

    def exchange(index, source, target, peer):
        copy = remote(source, target, send_sems.at[index], recv_sems.at[index], peer)
        copy.start()
        return copy

    def aligned(start, size):
        return pl.ds(pl.multiple_of(start, 8), size)

    row_copies = [
        exchange(step, grad_probe.at[aligned(peer[1] * part, part)], from_row.at[step], peer) for step, peer in enumerate(row_peers)
    ]
    base = 2 * (n_along + n_down - 2)
    corners, sides, firsts, seconds = [], [], [], []
    half = n_down // 2
    paths = detours(n_down, True)
    wraps, joins = down == half - 1, down == half
    start, rest = pl.ds(0, points), pl.ds(points, cols - points)
    for layer in range(layers):
        at = base + 4 * layer
        corners.append(remote(rights[layer].at[:, pl.ds(rows, points), :], corner_in.at[layer], send_sems.at[at], recv_sems.at[at], after))
        sides.append(remote(rights[layer].at[:, pl.ds(0, rows), :], right_in.at[layer], send_sems.at[at + 1], recv_sems.at[at + 1], after))
        firsts.append(remote(lowers[layer].at[:, :, rest], lower_in.at[layer, :, :, rest], send_sems.at[at + 2], recv_sems.at[at + 2], below))
        seconds.append(remote(held.at[layer], lower_in.at[layer, :, :, start], send_sems.at[at + 3], recv_sems.at[at + 3], below))
    first, last = 0, layers - 1
    chunk = points // HOPS
    pieces = [pl.ds(piece * chunk, chunk) for piece in range(HOPS)]
    routes = []
    at = base + 4 * layers
    for number, (path, layer) in enumerate(zip(paths, (last, first, last))):
        if number == 0:
            sources, lanes = [held.at[layer, :, piece, :] for piece in pieces], start
        else:
            sources, lanes = [lowers[layer].at[:, piece, rest] for piece in pieces], rest
        routes.append(detour(
            path, along, sources, [lower_in.at[layer, :, piece, lanes] for piece in pieces], relay.at[number], send_sems, recv_sems, at))
        at += HOPS * (len(path) - 1)
    for layer in range(layers):
        when(not_bottom & not_last, corners[layer].start)

    when(not_bottom & ~wraps, firsts[0].start)
    total = grad_probe[aligned(along * part, part)]
    for step, copy in enumerate(row_copies):
        copy.wait()
        total = total + from_row[step]
    row_sum[...] = total
    at = n_along - 1
    copies = [
        exchange(at + step, row_sum.at[piece_of(peer[0], 0)], from_column.at[step], peer)
        for step, peer in enumerate(column_peers)
    ]
    total = row_sum[piece_of(down, 0)]
    for step, copy in enumerate(copies):
        copy.wait()
        total = total + from_column[step]
    mine = piece_of(down, along * part)
    probe_out[mine] = probe[mine] - scale * total
    at += n_down - 1
    copies = [exchange(at + step, probe_out.at[mine], probe_out.at[mine], peer) for step, peer in enumerate(column_peers)]
    for layer in range(1, layers):
        when(not_bottom & ~wraps, firsts[layer].start)
    for copy in copies:
        copy.wait()
    at += n_down - 1
    mine = aligned(along * part, part)
    row_copies = [exchange(at + step, probe_out.at[mine], probe_out.at[mine], peer) for step, peer in enumerate(row_peers)]
    for route, path in zip(routes[1:], paths[1:]):
        set_off(route, path, down)
    for layer in range(layers):
        when(not_last, sides[layer].start)

    for layer in range(layers):
        loads[layer].wait()
        when(not_bottom & not_first, corners[layer].wait_recv)

        @pl.when(not_bottom & not_first)
        def _():
            held[layer] += corner_in[layer]

        if layer == last:
            set_off(routes[0], paths[0], down)
            when(not_bottom & ~wraps, seconds[layer].start)
        else:
            when(not_bottom, seconds[layer].start)
    pass_on(routes[1:], paths[1:], down)
    pass_on(routes[:1], paths[:1], down)
    for copy in row_copies:
        copy.wait()
    for layer in range(layers):
        when(not_bottom & not_last, corners[layer].wait_send)
        when(not_last, sides[layer].wait_send)
        when(not_first, sides[layer].wait_recv)
        when(not_bottom & ~wraps, firsts[layer].wait_send)
        when(not_top & ~joins, firsts[layer].wait_recv)
        if layer == last:
            when(not_bottom & ~wraps, seconds[layer].wait_send)
            when(not_top & ~joins, seconds[layer].wait_recv)
        else:
            when(not_bottom, seconds[layer].wait_send)
            when(not_top, seconds[layer].wait_recv)
    arrive(routes, paths, down)
    settle(routes, paths, down)


def send_back(grad_right, grad_lower, grad_probe, probe_wave, scale, rows):
    layers, _, points, cols = grad_lower.shape
    flat = (2 * points, points)
    n_down, n_along = lax.axis_size("ty"), lax.axis_size("tx")
    part = flat[0] // n_along
    copies = 2 * (n_along + n_down - 2) + 4 * layers + 8 * HOPS
    shape = lambda *dims: jax.ShapeDtypeStruct(dims, jnp.float32)
    right_in, lower_in, probe = pl.pallas_call(
        functools.partial(return_kernel, scale),
        out_shape=[shape(layers, 2, rows, points), shape(layers, 2, points, cols), shape(*flat)],
        in_specs=[ANY, ANY, WHOLE, WHOLE],
        out_specs=[ANY, ANY, WHOLE],
        scratch_shapes=[
            pltpu.VMEM((layers, 2, points, points), jnp.float32),
            pltpu.VMEM((layers, 2, points, points), jnp.float32),
            pltpu.VMEM((3, HOPS, 2, points // HOPS, points), jnp.float32),
            pltpu.VMEM((n_along - 1, part, points), jnp.float32),
            pltpu.VMEM((part, points), jnp.float32),
            pltpu.VMEM((n_down - 1, 8, 128), jnp.float32),
            pltpu.SemaphoreType.DMA((layers,)),
            pltpu.SemaphoreType.DMA((copies,)),
            pltpu.SemaphoreType.DMA((copies,)),
        ],
        compiler_params=pltpu.CompilerParams(collective_id=1, has_side_effects=True, vmem_limit_bytes=VMEM_LIMIT),
    )(grad_right, grad_lower, grad_probe.reshape(flat), probe_wave.reshape(flat))
    return right_in, lower_in, probe.reshape(probe_wave.shape)


def local(object_slab, probe_wave, frames, scan_tiles, scan_offsets):
    columns = lax.axis_size("tx")
    row_index = lax.axis_index("ty")
    col_index = lax.axis_index("tx")
    owned = frames.shape[0]
    points = probe_wave.shape[-1]
    layers, _, tile_rows, tile_cols = object_slab.shape
    total_frames = owned * columns
    my_tile = row_index * columns + col_index
    by_owner = scan_tiles.reshape(columns, owned)

    mine = lax.dynamic_index_in_dim(by_owner, col_index, 0, keepdims=False)
    other_row = lax.rem(row_index + lax.axis_size("ty") // 2, lax.axis_size("ty"))
    places = jnp.arange(columns, dtype=jnp.int32)
    wanted = jnp.concatenate([row_index * columns + places, other_row * columns + places])
    source = jnp.sum((mine[None, :] == wanted[:, None]).astype(jnp.int32) * jnp.arange(owned, dtype=jnp.int32)[None, :], axis=1)

    right, lower, corner, arrived = fetch(source, frames, object_slab, points)

    matches = by_owner == my_tile
    present = jnp.any(matches, axis=1)
    which = jnp.sum(matches.astype(jnp.int32) * jnp.arange(owned, dtype=jnp.int32)[None, :], axis=1)
    global_ids = jnp.arange(columns, dtype=jnp.int32) * owned + which
    ranks = jnp.cumsum(present.astype(jnp.int32)) - 1
    slot_pick = (present[None, :] & (ranks[None, :] == jnp.arange(TILE_CAP, dtype=jnp.int32)[:, None])).astype(jnp.int32)
    chosen_ids = jnp.sum(slot_pick * global_ids[None, :], axis=1)
    owners = jnp.sum(slot_pick * jnp.arange(columns, dtype=jnp.int32)[None, :], axis=1)
    count = jnp.sum(present.astype(jnp.int32)).reshape(1)
    offsets = scan_offsets[chosen_ids].reshape(-1)
    scalars = (offsets, count, owners)

    moved, grad_right, grad_lower, grad_probe = gradients(scalars, object_slab, right, lower, corner, arrived, probe_wave)
    right_back, lower_back, new_probe = send_back(
        grad_right, grad_lower, grad_probe, probe_wave, PROBE_RATE / total_frames, object_slab.shape[2])
    return finish(moved, right_back, lower_back), new_probe


def solution(mesh):
    return jax.shard_map(
        local,
        mesh=mesh,
        in_specs=(P(None, None, "ty", "tx"), P(), P("tx", None, None), P(), P()),
        out_specs=(P(None, None, "ty", "tx"), P()),
        check_vma=False,
    )
```

```python
import functools
import math

import jax
import jax.numpy as jnp
import ml_dtypes
import numpy as np
from jax import lax
from jax.experimental import pallas as pl
from jax.experimental.pallas import tpu as pltpu
from jax.sharding import PartitionSpec as P

MESH = pl.DeviceIdType.MESH
TILE_CAP = 8
HOPS = 4
PAIR = 2
EARLY_FRAMES = (12, 14)
BACKGROUND = 0.5
FRESNEL = 0.25
OBJECT_RATE = 0.25
PROBE_RATE = 4.0
VMEM_LIMIT = 56 * 1024 * 1024


FRAME_STEPS = ((1, 0, 0), (3, 0, 0), (0, 1, 1), (2, 0, 0), (1, 1, 1), (3, 1, 1), (0, 1, 0), (2, 1, 1), (1, 0, 1), (3, 0, 1), (2, 0, 1),
               (1, 1, 0), (3, 1, 0), (2, 1, 0), (0, 0, 1))


def real_form(matrix):
    return np.block([[matrix.real, -matrix.imag], [matrix.imag, matrix.real]])


def split_table(table):
    high = table.astype(ml_dtypes.bfloat16)
    low = (table - high.astype(np.float64)).astype(ml_dtypes.bfloat16)
    return high, low


def left_table(table):
    return np.concatenate(split_table(table), axis=1)


def half_transforms(points):
    half = points // 2
    places = np.arange(half)
    even = np.exp(-2j * np.pi * ((2 * places[:, None]) * places[None, :] % points) / points)
    odd = np.exp(-2j * np.pi * ((2 * places[:, None] + 1) * places[None, :] % points) / points)
    return even / math.sqrt(points), odd / math.sqrt(points)


def build_tables(points):
    even, odd = half_transforms(points)
    places = np.arange(points)
    frequency = (places + points // 2) % points - points // 2
    phase = np.exp(-1j * np.pi * FRESNEL / points * frequency.astype(np.float64) ** 2)
    spread_even = even.conj().T @ (phase[0::2, None] * even)
    spread_odd = odd.conj().T @ (phase[1::2, None] * odd)
    spread = [real_form(spread_even), real_form(spread_odd)]
    fourier = [real_form(even), real_form(odd)]
    order = np.concatenate([places[0::2], places[1::2]])
    shuffle = (places[:, None] == order[None, :]).astype(ml_dtypes.bfloat16)

    groups = [spread, [table.T for table in spread], fourier, [table.T for table in fourier]]
    return np.stack([left_table(table) for group in groups for table in group]), shuffle


def split(value):
    high = value.astype(jnp.bfloat16)
    low = (value - high.astype(jnp.float32)).astype(jnp.bfloat16)
    return high, low


def left_product(table, value):
    high, low = split(value)
    size = value.shape[0]
    table = jnp.concatenate([table[...], table[:, :size]], axis=1)
    return jnp.dot(table, jnp.concatenate([high, high, low], axis=0), preferred_element_type=jnp.float32)


def right_product(value, table):
    high, low = split(value)
    size = value.shape[1]
    table = jnp.concatenate([table[:, :size], table[:, size:], table[:, :size]], axis=0)
    return jnp.dot(jnp.concatenate([high, high, low], axis=1), table, preferred_element_type=jnp.float32)


def halves(value, axis):
    half = value.shape[axis] // 2
    first = lax.slice_in_dim(value, 0, half, axis=axis)
    second = lax.slice_in_dim(value, half, 2 * half, axis=axis)
    return first, second


def apart(real, imag, axis):
    real_a, real_b = halves(real, axis)
    imag_a, imag_b = halves(imag, axis)
    plus = jnp.concatenate([real_a + real_b, imag_a + imag_b], axis=axis)
    minus = jnp.concatenate([real_a - real_b, imag_a - imag_b], axis=axis)
    return plus, minus


def together(plus, minus, axis):
    plus_re, plus_im = halves(plus, axis)
    minus_re, minus_im = halves(minus, axis)
    real = jnp.concatenate([plus_re + minus_re, plus_re - minus_re], axis=axis)
    imag = jnp.concatenate([plus_im + minus_im, plus_im - minus_im], axis=axis)
    return real, imag


def regroup(even, odd, axis):
    even_re, even_im = halves(even, axis)
    odd_re, odd_im = halves(odd, axis)
    return jnp.concatenate([even_re, odd_re], axis=axis), jnp.concatenate([even_im, odd_im], axis=axis)


def spread(real, imag, tables):
    left_even, left_odd, right_even, right_odd = tables
    plus, minus = apart(real, imag, 0)
    real, imag = together(left_product(left_even, plus), left_product(left_odd, minus), 0)
    plus, minus = apart(real, imag, 1)
    return together(right_product(plus, right_even), right_product(minus, right_odd), 1)


def to_frequencies(real, imag, tables):
    left_even, left_odd, right_even, right_odd = tables
    plus, minus = apart(real, imag, 0)
    real, imag = regroup(left_product(left_even, plus), left_product(left_odd, minus), 0)
    plus, minus = apart(real, imag, 1)
    return regroup(right_product(plus, right_even), right_product(minus, right_odd), 1)


def from_frequencies(real, imag, tables):
    left_even, left_odd, right_even, right_odd = tables
    even, odd = regroup(real, imag, 0)
    real, imag = together(left_product(left_even, even), left_product(left_odd, odd), 0)
    even, odd = regroup(real, imag, 1)
    return together(right_product(even, right_even), right_product(odd, right_odd), 1)


def place_of(row, column, points):
    return pl.ds(row, points), column // 128, lax.rem(column, 128)


def window_of(canvas, layer, place, points):
    rows, first, along = place
    before = lax.broadcasted_iota(jnp.int32, (points, 128), 1) < 128 - along
    parts = []
    for part in range(2):
        turned = [
            pltpu.roll(canvas[layer, part, first + step, rows, :], lax.rem(128 - along, 128), 1)
            for step in range(points // 128 + 1)
        ]
        parts.append(jnp.concatenate([jnp.where(before, one, other) for one, other in zip(turned, turned[1:])], axis=1))
    return parts


def add_window(canvas, layer, place, points, parts):
    rows, first, along = place
    inside = lax.broadcasted_iota(jnp.int32, (points, 128), 1) >= along
    for part in range(2):
        turned = [pltpu.roll(parts[part][:, at:at + 128], along, 1) for at in range(0, points, 128)]
        none = jnp.zeros((points, 128), jnp.float32)
        for step, (one, other) in enumerate(zip(turned + [none], [none] + turned)):
            canvas[layer, part, first + step, rows, :] += jnp.where(inside, one, other)


def times(a, b):
    return a[0] * b[0] - a[1] * b[1], a[0] * b[1] + a[1] * b[0]


def times_conjugate(a, b):
    return a[0] * b[0] + a[1] * b[1], a[0] * b[1] - a[1] * b[0]


def gradient_kernel(row_offsets, column_offsets, count, owners, slab, right, lower, corner, arrived, probe, tables_all, shuffle_all, moved,
                    grad_right, grad_lower, grad_probe, canvas, grad, frame, columns, tables, shuffle, load_sems,
                    table_sems, frame_sems, out_sems):
    table_loads = [
        pltpu.make_async_copy(source, target, table_sems.at[at])
        for at, (source, target) in enumerate(((tables_all, tables), (shuffle_all, shuffle)))
    ]
    spread_ahead, spread_back, fourier_ahead, fourier_back = (
        [tables.at[at] for at in order] for order in ((0, 1, 2, 3), (2, 3, 0, 1), (4, 5, 6, 7), (6, 7, 4, 5)))
    layers, rows, cols = slab.shape[0], slab.shape[2], slab.shape[3]
    points = probe.shape[1]
    half = points // 2
    own_lanes, more_lanes = cols // 128, points // 128
    own, beside = pl.ds(0, rows), pl.ds(rows, points)

    def lanes(number):
        return pl.ds(128 * number, 128)

    pairs = (count[0] + PAIR - 1) // PAIR

    def frame_copies(pair):
        side = lax.rem(pair, 2)
        return [
            pltpu.make_async_copy(arrived.at[owners[PAIR * pair + at]], frame.at[side, at], frame_sems.at[side, at])
            for at in range(PAIR)
        ]

    parts = []
    for layer in range(layers):
        for number in range(own_lanes):
            parts.append((slab.at[layer, :, :, lanes(number)], canvas.at[layer, :, number, own, :]))
            parts.append((lower.at[layer, :, :, lanes(number)], canvas.at[layer, :, number, beside, :]))
        for number in range(more_lanes):
            parts.append((right.at[layer, :, :, lanes(number)], canvas.at[layer, :, own_lanes + number, own, :]))
            parts.append((corner.at[layer, :, :, lanes(number)], canvas.at[layer, :, own_lanes + number, beside, :]))
    loads = [pltpu.make_async_copy(source, target, load_sems.at[at]) for at, (source, target) in enumerate(parts)]
    for load in loads + table_loads:
        load.start()

    @pl.when(count[0] > 0)
    def _():
        for copy in frame_copies(0):
            copy.start()

    grad[...] = jnp.zeros_like(grad)
    grad_probe[...] = jnp.zeros_like(grad_probe)
    for load in loads + table_loads:
        load.wait()

    @pl.when(lax.axis_index("ty") == lax.axis_size("ty") - 1)
    def _():
        canvas[:, :, :, beside, :] = jnp.zeros((layers, 2, own_lanes + more_lanes, points, 128), jnp.float32)

    @pl.when(lax.axis_index("tx") == lax.axis_size("tx") - 1)
    def _():
        canvas[:, :, pl.ds(own_lanes, more_lanes)] = jnp.zeros((layers, 2, more_lanes, rows + points, 128), jnp.float32)

    def visit(pair, carry):
        slots = [PAIR * pair + at for at in range(PAIR)]
        places = [place_of(row_offsets[slot], column_offsets[slot], points) for slot in slots]
        for copy in frame_copies(pair):
            copy.wait()

        @pl.when(pair + 1 < pairs)
        def _():
            for copy in frame_copies(pair + 1):
                copy.start()

        probe_wave = (probe[0], probe[1])
        windows = [[window_of(canvas, layer, place, points) for layer in range(layers)] for place in places]
        waves = [spread(*times(probe_wave, window[0]), spread_ahead) for window in windows]
        fars = [to_frequencies(*times(wave, window[1]), fourier_ahead) for wave, window in zip(waves, windows)]
        backs = []
        for at, (real, imag) in enumerate(fars):
            pieces = []
            for side in range(points // 128):
                columns[at, side] = jnp.sqrt(frame[lax.rem(pair, 2), at, :, pl.ds(side * 128, 128)] + BACKGROUND)
                pieces.append(jnp.concatenate([columns[at, side, pl.ds(start, half, stride=2), :] for start in range(2)], axis=0))
            target = jnp.concatenate(pieces, axis=1)
            high = target.astype(jnp.bfloat16)
            rest = target - high.astype(jnp.float32)
            middle = rest.astype(jnp.bfloat16)
            low = (rest - middle.astype(jnp.float32)).astype(jnp.bfloat16)
            target = jnp.dot(
                jnp.concatenate([high, middle, low], axis=1), jnp.concatenate([shuffle[...]] * 3, axis=0),
                preferred_element_type=jnp.float32)
            pull = 2.0 - 2.0 * target * lax.rsqrt(real * real + imag * imag + BACKGROUND)
            pull = pull * (slots[at] < count[0]).astype(jnp.float32)
            backs.append((pull * real, pull * imag))
        backs = [from_frequencies(*back, fourier_back) for back in backs]
        for place, wave, back in zip(places, waves, backs):
            add_window(grad, 1, place, points, times_conjugate(wave, back))
        backs = [spread(*times_conjugate(window[1], back), spread_back) for window, back in zip(windows, backs)]
        for place, back in zip(places, backs):
            add_window(grad, 0, place, points, times_conjugate(probe_wave, back))
        more = [times_conjugate(window[0], back) for window, back in zip(windows, backs)]
        for part in range(2):
            grad_probe[part] += sum(one[part] for one in more)
        return carry

    lax.fori_loop(0, pairs, visit, 0)
    writes = [
        pltpu.make_async_copy(grad.at[:, :, own_lanes + number], grad_right.at[:, :, :, lanes(number)], out_sems.at[number])
        for number in range(more_lanes)
    ]
    writes += [
        pltpu.make_async_copy(grad.at[:, :, number, beside, :], grad_lower.at[:, :, :, lanes(number)], out_sems.at[more_lanes + number])
        for number in range(own_lanes)
    ]
    for write in writes:
        write.start()
    for number in range(own_lanes):
        canvas[:, :, number, :rows, :] -= OBJECT_RATE * grad[:, :, number, :rows, :]
        writes.append(pltpu.make_async_copy(
            canvas.at[:, :, number, own, :], moved.at[:, :, :, lanes(number)], out_sems.at[more_lanes + own_lanes + number]))
        writes[-1].start()
    for write in writes:
        write.wait()


ANY = pl.BlockSpec(memory_space=pl.ANY)
WHOLE = pl.BlockSpec(memory_space=pltpu.VMEM)


def gradients(scalars, object_slab, right, lower, corner, arrived, probe_wave):
    layers, _, rows, cols = object_slab.shape
    points = probe_wave.shape[-1]
    tables = build_tables(points)
    shape = lambda *dims: jax.ShapeDtypeStruct(dims, jnp.float32)
    canvas = pltpu.VMEM((layers, 2, (cols + points) // 128, rows + points, 128), jnp.float32)
    lanes = (cols + points) // 128
    return pl.pallas_call(
        gradient_kernel,
        out_shape=[shape(*object_slab.shape), shape(layers, 2, rows + points, points), shape(layers, 2, points, cols),
                   shape(*probe_wave.shape)],
        grid_spec=pltpu.PrefetchScalarGridSpec(
            num_scalar_prefetch=len(scalars),
            grid=(1,),
            in_specs=[ANY] * 5 + [WHOLE] + [ANY] * len(tables),
            out_specs=[ANY] * 3 + [WHOLE],
            scratch_shapes=[
                canvas, canvas,
                pltpu.VMEM((2, PAIR, points, points), jnp.float32),
                pltpu.VMEM((PAIR, points // 128, points, 128), jnp.float32),
                *[pltpu.VMEM(table.shape, jnp.bfloat16) for table in tables],
                pltpu.SemaphoreType.DMA((2 * layers * lanes,)),
                pltpu.SemaphoreType.DMA((len(tables),)),
                pltpu.SemaphoreType.DMA((2, PAIR)),
                pltpu.SemaphoreType.DMA((lanes + cols // 128,)),
            ]),
        compiler_params=pltpu.CompilerParams(vmem_limit_bytes=VMEM_LIMIT),
        cost_estimate=pl.CostEstimate(flops=TILE_CAP * 96 * points**3, bytes_accessed=32 * 1024 * 1024, transcendentals=0),
    )(*scalars, object_slab, right, lower, corner, arrived, probe_wave, *tables)


def finish_kernel(moved, right, lower, out):
    points = right.shape[3]
    out[...] = moved[...]

    @pl.when(lax.axis_index("tx") > 0)
    def _():
        out[0, 0, :, :points] -= OBJECT_RATE * right[0, 0]

    @pl.when(lax.axis_index("ty") > 0)
    def _():
        out[0, 0, :points, :] -= OBJECT_RATE * lower[0, 0]


def finish(moved, right, lower):
    plane = lambda array: pl.BlockSpec((1, 1) + array.shape[2:], lambda layer, part: (layer, part, 0, 0))
    return pl.pallas_call(
        finish_kernel,
        out_shape=jax.ShapeDtypeStruct(moved.shape, moved.dtype),
        grid=moved.shape[:2],
        in_specs=[plane(moved), plane(right), plane(lower)],
        out_specs=plane(moved),
        compiler_params=pltpu.CompilerParams(vmem_limit_bytes=VMEM_LIMIT),
        cost_estimate=pl.CostEstimate(flops=3 * moved.size, bytes_accessed=12 * moved.size, transcendentals=0),
    )(moved, right, lower)


def remote(source, target, send_sem, recv_sem, peer):
    return pltpu.make_async_remote_copy(
        src_ref=source, dst_ref=target, send_sem=send_sem, recv_sem=recv_sem, device_id=peer, device_id_type=MESH)


def when(condition, action):
    pl.when(condition)(lambda: action())


def greet(peers):
    barrier = pltpu.get_barrier_semaphore()
    for peer in peers:
        pl.semaphore_signal(barrier, inc=1, device_id=peer, device_id_type=MESH)
    pl.semaphore_wait(barrier, len(peers))


def detours(n_down, forward):
    half = n_down // 2
    paths = ((half - 1, n_down - 1, half), (half - 1, n_down - 2, half + 1, half), (half - 1, half - 2, half + 1, half))
    return paths if forward else [tuple(n_down - 1 - place for place in path) for path in paths]


def detour(path, along, sources, targets, relay, send_sems, recv_sems, at):
    hops = len(path) - 1
    route = []
    for number, (source, target) in enumerate(zip(sources, targets)):
        route.append([
            remote(
                source if hop == 0 else relay.at[number], target if hop == hops - 1 else relay.at[number],
                send_sems.at[at + number * hops + hop], recv_sems.at[at + number * hops + hop], (jnp.int32(path[hop + 1]), along))
            for hop in range(hops)
        ])
    return route


def set_off(route, path, down):
    for copies in route:
        when(down == path[0], copies[0].start)


def pass_on(routes, paths, down):
    for number in range(len(routes[0])):
        for route, path in zip(routes, paths):
            for hop in range(1, len(path) - 1):
                when(down == path[hop], route[number][hop - 1].wait_recv)
                when(down == path[hop], route[number][hop].start)


def arrive(routes, paths, down):
    for route, path in zip(routes, paths):
        for copies in route:
            when(down == path[-1], copies[-1].wait_recv)


def settle(routes, paths, down):
    for route, path in zip(routes, paths):
        for copies in route:
            for hop, copy in enumerate(copies):
                when(down == path[hop], copy.wait_send)


def around(down, along, n_down, n_along):
    row = [(down, lax.rem(along + step, n_along)) for step in range(1, n_along)]
    column = [(lax.rem(down + step, n_down), along) for step in range(1, n_down)]
    return row, column


def frame_peer(down, along, n_down, n_along, step, ahead):
    step_y, step_z, step_core = step
    if not ahead:
        step_y = -step_y % (n_along // 4)
    place_y, place_z, core = along // 4, lax.rem(along // 2, 2), lax.rem(along, 2)
    other = step_z * jnp.maximum(step_core, core)
    place_y = lax.rem(place_y + step_y, n_along // 4)
    place_z = lax.rem(place_z + step_z, 2)
    core = lax.rem(core + step_core, 2)
    return (lax.rem(down + other * (n_down // 2), n_down), place_y * 4 + place_z * 2 + core), other


def fetch_kernel(source, frames, slab, right, lower, corner, arrived, held, picked, lower_relay, right_relay, held_sem, own_sem,
                 send_sems, recv_sems):
    down, along = lax.axis_index("ty"), lax.axis_index("tx")
    n_down, n_along = lax.axis_size("ty"), lax.axis_size("tx")
    layers, points, rows, cols = right.shape[0], right.shape[3], right.shape[2], lower.shape[3]
    half = n_down // 2
    load = pltpu.make_async_copy(frames, held, held_sem)
    load.start()
    ring = lambda by_down, by_along: (lax.rem(down + by_down + n_down, n_down), lax.rem(along + by_along + n_along, n_along))
    greet([frame_peer(down, along, n_down, n_along, step, False)[0] for step in FRAME_STEPS]
          + [ring(by, 0) for by in (1, -1, half, 3, -3)] + [ring(0, by) for by in (1, -1, 3, -3, 4, -4)])
    above, left = ring(-1, 0), ring(0, -1)
    not_top, not_bottom = down > 0, down < n_down - 1
    not_first, not_last = along > 0, along < n_along - 1
    paths = detours(n_down, False)
    wraps, joins = down == half, down == half - 1
    crosses, carries = lax.rem(along, 4) == 0, lax.rem(along, 4) == 3
    crossed = carries & not_last
    across = crosses & not_first
    base = n_along - 1
    index = iter(range(base, base + 64))

    def copy(source_ref, target, peer, at=None):
        at = next(index) if at is None else at
        return remote(source_ref, target, send_sems.at[at], recv_sems.at[at], peer)

    first, last = 0, layers - 1
    side = [slab.at[layer, :, :, pl.ds(0, points)] for layer in range(layers)]
    edge = [lower.at[layer, :, :, pl.ds(0, points)] for layer in range(layers)]
    rest, start = pl.ds(points, cols - points), pl.ds(0, points)
    lowers, others, rights, corners = [], [], [], []
    for layer in range(layers):
        lowers.append(copy(slab.at[layer, :, pl.ds(0, points), start], lower.at[layer, :, :, start], above))
        others.append(copy(slab.at[layer, :, pl.ds(0, points), rest], lower.at[layer, :, :, rest], above))
        rights.append(copy(side[layer], right.at[layer], left))
        corners.append(copy(edge[layer], corner.at[layer], left))
    at_right, at_corner = base + 4 * last + 2, base + 4 * last + 3
    right_hop = copy(side[last], right_relay.at[:, pl.ds(0, rows), :], ring(0, 3))
    right_forward = copy(right_relay.at[:, pl.ds(0, rows), :], right.at[last], ring(0, -4), at_right)
    corner_hop = copy(edge[last], right_relay.at[:, pl.ds(rows, points), :], ring(0, 3))
    corner_forward = copy(right_relay.at[:, pl.ds(rows, points), :], corner.at[last], ring(0, -4), at_corner)

    chunk = points // HOPS
    routes = []
    at = base + 4 * layers + 2
    for number, (path, layer, lanes) in enumerate(zip(paths, (last, first, last), (start, rest, rest))):
        pieces = [pl.ds(piece * chunk, chunk) for piece in range(HOPS)]
        routes.append(detour(
            path, along, [slab.at[layer, :, piece, lanes] for piece in pieces], [lower.at[layer, :, piece, lanes] for piece in pieces],
            lower_relay.at[number], send_sems, recv_sems, at))
        at += HOPS * (len(path) - 1)
    ahead = (lowers[first], lowers[last], others[first], others[last])
    when(not_top, lowers[first].start)
    for go in ahead[1:]:
        when(not_top & ~wraps, go.start)
    when(across, right_hop.start)
    when(not_first & ~crosses, rights[last].start)
    when(not_first, rights[first].start)
    load.wait()
    sends = []

    def send_frames(steps):
        for step in steps:
            peer, other = frame_peer(down, along, n_down, n_along, FRAME_STEPS[step], True)
            picked[step] = held[source[other * n_along + peer[1]]]
            send = remote(picked.at[step], arrived.at[along], send_sems.at[step], recv_sems.at[step], peer)
            send.start()
            sends.append(send)

    send_frames(range(EARLY_FRAMES[0]))
    for route, path in zip(routes, paths):
        set_off(route, path, down)
    picked[n_along - 1] = held[source[along]]
    own = pltpu.make_async_copy(picked.at[n_along - 1], arrived.at[along], own_sem)
    own.start()
    relays = along >= 4
    when(carries & relays, right_hop.wait_recv)
    when(carries & relays, right_forward.start)
    pass_on(routes, paths, down)
    for layer in range(layers):
        if layer == last:
            arrive(routes[:1], paths[:1], down)
            when(not_bottom & ~joins, lowers[layer].wait_recv)
        else:
            when(not_bottom, lowers[layer].wait_recv)
        if layer == last:
            when(not_bottom & across, corner_hop.start)
            when(not_bottom & not_first & ~crosses, corners[layer].start)
            when(not_bottom & carries & relays, corner_hop.wait_recv)
            when(not_bottom & carries & relays, corner_forward.start)
        else:
            when(not_bottom & not_first, corners[layer].start)
            send_frames(range(EARLY_FRAMES[0], EARLY_FRAMES[1]))
    send_frames(range(EARLY_FRAMES[1], len(FRAME_STEPS)))
    when(not_top, lowers[first].wait_send)
    for go in ahead[1:]:
        when(not_top & ~wraps, go.wait_send)
    for layer in range(layers):
        when(not_bottom & ~joins, others[layer].wait_recv)
        when(not_last, rights[layer].wait_recv)
        when(not_bottom & not_last, corners[layer].wait_recv)
        if layer == last:
            when(across, right_hop.wait_send)
            when(not_first & ~crosses, rights[layer].wait_send)
            when(carries & relays, right_forward.wait_send)
            when(not_bottom & across, corner_hop.wait_send)
            when(not_bottom & not_first & ~crosses, corners[layer].wait_send)
            when(not_bottom & carries & relays, corner_forward.wait_send)
        else:
            when(not_first, rights[layer].wait_send)
            when(not_bottom & not_first, corners[layer].wait_send)
    arrive(routes[1:], paths[1:], down)
    settle(routes, paths, down)
    for send in sends:
        send.wait()
    own.wait()


def fetch(source, frames, object_slab, points):
    layers, _, rows, cols = object_slab.shape
    n_along = lax.axis_size("tx")
    copies = n_along - 1 + 4 * layers + 2 + 8 * HOPS
    shape = lambda *dims: jax.ShapeDtypeStruct(dims, jnp.float32)
    return pl.pallas_call(
        fetch_kernel,
        out_shape=[shape(layers, 2, rows, points), shape(layers, 2, points, cols), shape(layers, 2, points, points),
                   shape(n_along, points, points)],
        in_specs=[pl.BlockSpec(memory_space=pltpu.SMEM), ANY, ANY],
        out_specs=[ANY] * 4,
        scratch_shapes=[
            pltpu.VMEM(frames.shape, jnp.float32),
            pltpu.VMEM((n_along, points, points), jnp.float32),
            pltpu.VMEM((3, HOPS, 2, points // HOPS, points), jnp.float32),
            pltpu.VMEM((2, rows + points, points), jnp.float32),
            pltpu.SemaphoreType.DMA,
            pltpu.SemaphoreType.DMA,
            pltpu.SemaphoreType.DMA((copies,)),
            pltpu.SemaphoreType.DMA((copies,)),
        ],
        compiler_params=pltpu.CompilerParams(collective_id=0, has_side_effects=True, vmem_limit_bytes=VMEM_LIMIT),
    )(source, frames, object_slab)


def return_kernel(scale, all_right, all_lower, grad_probe, probe, right_in, lower_in, probe_out,
                  corner_in, held, relay, from_row, row_sum, from_column, load_sems, send_sems, recv_sems):
    down, along = lax.axis_index("ty"), lax.axis_index("tx")
    n_down, n_along = lax.axis_size("ty"), lax.axis_size("tx")
    rights, lowers = ([ref.at[layer] for layer in range(ref.shape[0])] for ref in (all_right, all_lower))
    layers, points, rows, cols = len(rights), right_in.shape[3], right_in.shape[2], lower_in.shape[3]
    loads = [
        pltpu.make_async_copy(lowers[layer].at[:, :, pl.ds(0, points)], held.at[layer], load_sems.at[layer])
        for layer in range(layers)
    ]
    for load in loads:
        load.start()
    row_peers, column_peers = around(down, along, n_down, n_along)
    greet(row_peers + column_peers)
    part = grad_probe.shape[0] // n_along

    def piece_of(number, start):
        return pl.ds(pl.multiple_of(start + number // 2 * 8, 8), 8), pl.ds(pl.multiple_of(lax.rem(number, 2) * 128, 128), 128)

    below, after = (lax.rem(down + 1, n_down), along), (down, lax.rem(along + 1, n_along))
    not_top, not_bottom = down > 0, down < n_down - 1
    not_first, not_last = along > 0, along < n_along - 1

    def exchange(index, source, target, peer):
        copy = remote(source, target, send_sems.at[index], recv_sems.at[index], peer)
        copy.start()
        return copy

    def aligned(start, size):
        return pl.ds(pl.multiple_of(start, 8), size)

    row_copies = [
        exchange(step, grad_probe.at[aligned(peer[1] * part, part)], from_row.at[step], peer) for step, peer in enumerate(row_peers)
    ]
    base = 2 * (n_along + n_down - 2)
    corners, sides, firsts, seconds = [], [], [], []
    half = n_down // 2
    paths = detours(n_down, True)
    wraps, joins = down == half - 1, down == half
    start, rest = pl.ds(0, points), pl.ds(points, cols - points)
    for layer in range(layers):
        at = base + 4 * layer
        corners.append(remote(rights[layer].at[:, pl.ds(rows, points), :], corner_in.at[layer], send_sems.at[at], recv_sems.at[at], after))
        sides.append(remote(rights[layer].at[:, pl.ds(0, rows), :], right_in.at[layer], send_sems.at[at + 1], recv_sems.at[at + 1], after))
        firsts.append(remote(lowers[layer].at[:, :, rest], lower_in.at[layer, :, :, rest], send_sems.at[at + 2], recv_sems.at[at + 2], below))
        seconds.append(remote(held.at[layer], lower_in.at[layer, :, :, start], send_sems.at[at + 3], recv_sems.at[at + 3], below))
    first, last = 0, layers - 1
    chunk = points // HOPS
    pieces = [pl.ds(piece * chunk, chunk) for piece in range(HOPS)]
    routes = []
    at = base + 4 * layers
    for number, (path, layer) in enumerate(zip(paths, (last, first, last))):
        if number == 0:
            sources, lanes = [held.at[layer, :, piece, :] for piece in pieces], start
        else:
            sources, lanes = [lowers[layer].at[:, piece, rest] for piece in pieces], rest
        routes.append(detour(
            path, along, sources, [lower_in.at[layer, :, piece, lanes] for piece in pieces], relay.at[number], send_sems, recv_sems, at))
        at += HOPS * (len(path) - 1)
    for layer in range(layers):
        when(not_bottom & not_last, corners[layer].start)

    when(not_bottom & ~wraps, firsts[0].start)
    total = grad_probe[aligned(along * part, part)]
    for step, copy in enumerate(row_copies):
        copy.wait()
        total = total + from_row[step]
    row_sum[...] = total
    at = n_along - 1
    copies = [
        exchange(at + step, row_sum.at[piece_of(peer[0], 0)], from_column.at[step], peer)
        for step, peer in enumerate(column_peers)
    ]
    total = row_sum[piece_of(down, 0)]
    for step, copy in enumerate(copies):
        copy.wait()
        total = total + from_column[step]
    mine = piece_of(down, along * part)
    probe_out[mine] = probe[mine] - scale * total
    at += n_down - 1
    copies = [exchange(at + step, probe_out.at[mine], probe_out.at[mine], peer) for step, peer in enumerate(column_peers)]
    for layer in range(1, layers):
        when(not_bottom & ~wraps, firsts[layer].start)
    for copy in copies:
        copy.wait()
    at += n_down - 1
    mine = aligned(along * part, part)
    row_copies = [exchange(at + step, probe_out.at[mine], probe_out.at[mine], peer) for step, peer in enumerate(row_peers)]
    for route, path in zip(routes[1:], paths[1:]):
        set_off(route, path, down)
    for layer in range(layers):
        when(not_last, sides[layer].start)

    for layer in range(layers):
        loads[layer].wait()
        when(not_bottom & not_first, corners[layer].wait_recv)

        @pl.when(not_bottom & not_first)
        def _():
            held[layer] += corner_in[layer]

        if layer == last:
            set_off(routes[0], paths[0], down)
            when(not_bottom & ~wraps, seconds[layer].start)
        else:
            when(not_bottom, seconds[layer].start)
    pass_on(routes[1:], paths[1:], down)
    pass_on(routes[:1], paths[:1], down)
    for copy in row_copies:
        copy.wait()
    for layer in range(layers):
        when(not_bottom & not_last, corners[layer].wait_send)
        when(not_last, sides[layer].wait_send)
        when(not_first, sides[layer].wait_recv)
        when(not_bottom & ~wraps, firsts[layer].wait_send)
        when(not_top & ~joins, firsts[layer].wait_recv)
        if layer == last:
            when(not_bottom & ~wraps, seconds[layer].wait_send)
            when(not_top & ~joins, seconds[layer].wait_recv)
        else:
            when(not_bottom, seconds[layer].wait_send)
            when(not_top, seconds[layer].wait_recv)
    arrive(routes, paths, down)
    settle(routes, paths, down)


def send_back(grad_right, grad_lower, grad_probe, probe_wave, scale, rows):
    layers, _, points, cols = grad_lower.shape
    flat = (2 * points, points)
    n_down, n_along = lax.axis_size("ty"), lax.axis_size("tx")
    part = flat[0] // n_along
    copies = 2 * (n_along + n_down - 2) + 4 * layers + 8 * HOPS
    shape = lambda *dims: jax.ShapeDtypeStruct(dims, jnp.float32)
    right_in, lower_in, probe = pl.pallas_call(
        functools.partial(return_kernel, scale),
        out_shape=[shape(layers, 2, rows, points), shape(layers, 2, points, cols), shape(*flat)],
        in_specs=[ANY, ANY, WHOLE, WHOLE],
        out_specs=[ANY, ANY, WHOLE],
        scratch_shapes=[
            pltpu.VMEM((layers, 2, points, points), jnp.float32),
            pltpu.VMEM((layers, 2, points, points), jnp.float32),
            pltpu.VMEM((3, HOPS, 2, points // HOPS, points), jnp.float32),
            pltpu.VMEM((n_along - 1, part, points), jnp.float32),
            pltpu.VMEM((part, points), jnp.float32),
            pltpu.VMEM((n_down - 1, 8, 128), jnp.float32),
            pltpu.SemaphoreType.DMA((layers,)),
            pltpu.SemaphoreType.DMA((copies,)),
            pltpu.SemaphoreType.DMA((copies,)),
        ],
        compiler_params=pltpu.CompilerParams(collective_id=1, has_side_effects=True, vmem_limit_bytes=VMEM_LIMIT),
    )(grad_right, grad_lower, grad_probe.reshape(flat), probe_wave.reshape(flat))
    return right_in, lower_in, probe.reshape(probe_wave.shape)


def local(object_slab, probe_wave, frames, scan_tiles, scan_offsets):
    columns = lax.axis_size("tx")
    row_index = lax.axis_index("ty")
    col_index = lax.axis_index("tx")
    owned = frames.shape[0]
    points = probe_wave.shape[-1]
    layers, _, tile_rows, tile_cols = object_slab.shape
    total_frames = owned * columns
    my_tile = row_index * columns + col_index
    by_owner = scan_tiles.reshape(columns, owned)

    mine = lax.dynamic_index_in_dim(by_owner, col_index, 0, keepdims=False)
    other_row = lax.rem(row_index + lax.axis_size("ty") // 2, lax.axis_size("ty"))
    places = jnp.arange(columns, dtype=jnp.int32)
    wanted = jnp.concatenate([row_index * columns + places, other_row * columns + places])
    source = jnp.sum((mine[None, :] == wanted[:, None]).astype(jnp.int32) * jnp.arange(owned, dtype=jnp.int32)[None, :], axis=1)

    right, lower, corner, arrived = fetch(source, frames, object_slab, points)

    matches = (by_owner == my_tile).astype(jnp.int32)
    present = jnp.sum(matches, axis=1)
    ranks = jnp.cumsum(present) - 1
    slot_pick = present[None, :] * (ranks[None, :] == jnp.arange(TILE_CAP, dtype=jnp.int32)[:, None]).astype(jnp.int32)
    by_slot = lambda values: jnp.sum(slot_pick * values[None, :], axis=1)
    row_offsets, column_offsets = (
        by_slot(jnp.sum(matches * scan_offsets[:, side].reshape(columns, owned), axis=1)) for side in range(2))
    owners = by_slot(places)
    scalars = (row_offsets, column_offsets, jnp.sum(present).reshape(1), owners)

    moved, grad_right, grad_lower, grad_probe = gradients(scalars, object_slab, right, lower, corner, arrived, probe_wave)
    right_back, lower_back, new_probe = send_back(
        grad_right, grad_lower, grad_probe, probe_wave, PROBE_RATE / total_frames, object_slab.shape[2])
    return finish(moved, right_back, lower_back), new_probe


def solution(mesh):
    return jax.shard_map(
        local,
        mesh=mesh,
        in_specs=(P(None, None, "ty", "tx"), P(), P("tx", None, None), P(), P()),
        out_specs=(P(None, None, "ty", "tx"), P()),
        check_vma=False,
    )
```

```python
import functools
import math

import jax
import jax.numpy as jnp
import ml_dtypes
import numpy as np
from jax import lax
from jax.experimental import pallas as pl
from jax.experimental.pallas import tpu as pltpu
from jax.sharding import PartitionSpec as P

MESH = pl.DeviceIdType.MESH
TILE_CAP = 8
HOPS = 4
PAIR = 2
EARLY_FRAMES = (12, 14)
BACKGROUND = 0.5
FRESNEL = 0.25
OBJECT_RATE = 0.25
PROBE_RATE = 4.0
VMEM_LIMIT = 56 * 1024 * 1024


FRAME_STEPS = ((1, 0, 0), (3, 0, 0), (0, 1, 1), (2, 0, 0), (1, 1, 1), (3, 1, 1), (0, 1, 0), (2, 1, 1), (1, 0, 1), (3, 0, 1), (2, 0, 1),
               (1, 1, 0), (3, 1, 0), (2, 1, 0), (0, 0, 1))


def real_form(matrix):
    return np.block([[matrix.real, -matrix.imag], [matrix.imag, matrix.real]])


def split_table(table):
    high = table.astype(ml_dtypes.bfloat16)
    low = (table - high.astype(np.float64)).astype(ml_dtypes.bfloat16)
    return high, low


def left_table(table):
    return np.concatenate(split_table(table), axis=1)


def half_transforms(points):
    half = points // 2
    places = np.arange(half)
    even = np.exp(-2j * np.pi * ((2 * places[:, None]) * places[None, :] % points) / points)
    odd = np.exp(-2j * np.pi * ((2 * places[:, None] + 1) * places[None, :] % points) / points)
    return even / math.sqrt(points), odd / math.sqrt(points)


def build_tables(points):
    even, odd = half_transforms(points)
    places = np.arange(points)
    frequency = (places + points // 2) % points - points // 2
    phase = np.exp(-1j * np.pi * FRESNEL / points * frequency.astype(np.float64) ** 2)
    spread_even = even.conj().T @ (phase[0::2, None] * even)
    spread_odd = odd.conj().T @ (phase[1::2, None] * odd)
    spread = [real_form(spread_even), real_form(spread_odd)]
    fourier = [real_form(even), real_form(odd)]
    order = np.concatenate([places[0::2], places[1::2]])
    shuffle = (places[:, None] == order[None, :]).astype(ml_dtypes.bfloat16)

    groups = [spread, [table.T for table in spread], fourier, [table.T for table in fourier]]
    return np.stack([left_table(table) for group in groups for table in group]), shuffle


def split(value):
    high = value.astype(jnp.bfloat16)
    low = (value - high.astype(jnp.float32)).astype(jnp.bfloat16)
    return high, low


def left_product(table, value):
    high, low = split(value)
    size = value.shape[0]
    table = jnp.concatenate([table[...], table[:, :size]], axis=1)
    return jnp.dot(table, jnp.concatenate([high, high, low], axis=0), preferred_element_type=jnp.float32)


def right_product(value, table):
    high, low = split(value)
    size = value.shape[1]
    table = jnp.concatenate([table[:, :size], table[:, size:], table[:, :size]], axis=0)
    return jnp.dot(jnp.concatenate([high, high, low], axis=1), table, preferred_element_type=jnp.float32)


def halves(value, axis):
    half = value.shape[axis] // 2
    first = lax.slice_in_dim(value, 0, half, axis=axis)
    second = lax.slice_in_dim(value, half, 2 * half, axis=axis)
    return first, second


def apart(real, imag, axis):
    real_a, real_b = halves(real, axis)
    imag_a, imag_b = halves(imag, axis)
    plus = jnp.concatenate([real_a + real_b, imag_a + imag_b], axis=axis)
    minus = jnp.concatenate([real_a - real_b, imag_a - imag_b], axis=axis)
    return plus, minus


def together(plus, minus, axis):
    plus_re, plus_im = halves(plus, axis)
    minus_re, minus_im = halves(minus, axis)
    real = jnp.concatenate([plus_re + minus_re, plus_re - minus_re], axis=axis)
    imag = jnp.concatenate([plus_im + minus_im, plus_im - minus_im], axis=axis)
    return real, imag


def regroup(even, odd, axis):
    even_re, even_im = halves(even, axis)
    odd_re, odd_im = halves(odd, axis)
    return jnp.concatenate([even_re, odd_re], axis=axis), jnp.concatenate([even_im, odd_im], axis=axis)


def spread(real, imag, tables):
    left_even, left_odd, right_even, right_odd = tables
    plus, minus = apart(real, imag, 0)
    real, imag = together(left_product(left_even, plus), left_product(left_odd, minus), 0)
    plus, minus = apart(real, imag, 1)
    return together(right_product(plus, right_even), right_product(minus, right_odd), 1)


def to_frequencies(real, imag, tables):
    left_even, left_odd, right_even, right_odd = tables
    plus, minus = apart(real, imag, 0)
    real, imag = regroup(left_product(left_even, plus), left_product(left_odd, minus), 0)
    plus, minus = apart(real, imag, 1)
    return regroup(right_product(plus, right_even), right_product(minus, right_odd), 1)


def from_frequencies(real, imag, tables):
    left_even, left_odd, right_even, right_odd = tables
    even, odd = regroup(real, imag, 0)
    real, imag = together(left_product(left_even, even), left_product(left_odd, odd), 0)
    even, odd = regroup(real, imag, 1)
    return together(right_product(even, right_even), right_product(odd, right_odd), 1)


def place_of(row, column, points):
    return pl.ds(row, points), column // 128, lax.rem(column, 128)


def window_of(canvas, layer, place, points):
    rows, first, along = place
    before = lax.broadcasted_iota(jnp.int32, (points, 128), 1) < 128 - along
    parts = []
    for part in range(2):
        turned = [
            pltpu.roll(canvas[layer, part, first + step, rows, :], lax.rem(128 - along, 128), 1)
            for step in range(points // 128 + 1)
        ]
        parts.append(jnp.concatenate([jnp.where(before, one, other) for one, other in zip(turned, turned[1:])], axis=1))
    return parts


def add_window(canvas, layer, place, points, parts):
    rows, first, along = place
    inside = lax.broadcasted_iota(jnp.int32, (points, 128), 1) >= along
    for part in range(2):
        turned = [pltpu.roll(parts[part][:, at:at + 128], along, 1) for at in range(0, points, 128)]
        none = jnp.zeros((points, 128), jnp.float32)
        for step, (one, other) in enumerate(zip(turned + [none], [none] + turned)):
            canvas[layer, part, first + step, rows, :] += jnp.where(inside, one, other)


def times(a, b):
    return a[0] * b[0] - a[1] * b[1], a[0] * b[1] + a[1] * b[0]


def times_conjugate(a, b):
    return a[0] * b[0] + a[1] * b[1], a[0] * b[1] - a[1] * b[0]


def gradient_kernel(row_offsets, column_offsets, count, owners, slab, right, lower, corner, arrived, probe, tables_all, shuffle_all, moved,
                    grad_right, grad_lower, grad_probe, canvas, grad, frame, columns, tables, shuffle, load_sems,
                    table_sems, frame_sems, out_sems):
    table_loads = [
        pltpu.make_async_copy(source, target, table_sems.at[at])
        for at, (source, target) in enumerate(((tables_all, tables), (shuffle_all, shuffle)))
    ]
    spread_ahead, spread_back, fourier_ahead, fourier_back = (
        [tables.at[at] for at in order] for order in ((0, 1, 2, 3), (2, 3, 0, 1), (4, 5, 6, 7), (6, 7, 4, 5)))
    layers, rows, cols = slab.shape[0], slab.shape[2], slab.shape[3]
    points = probe.shape[1]
    half = points // 2
    own_lanes, more_lanes = cols // 128, points // 128
    own, beside = pl.ds(0, rows), pl.ds(rows, points)

    def lanes(number):
        return pl.ds(128 * number, 128)

    pairs = (count[0] + PAIR - 1) // PAIR

    def frame_copies(pair):
        side = lax.rem(pair, 2)
        return [
            pltpu.make_async_copy(arrived.at[owners[PAIR * pair + at]], frame.at[side, at], frame_sems.at[side, at])
            for at in range(PAIR)
        ]

    parts = []
    for layer in range(layers):
        for number in range(own_lanes):
            parts.append((slab.at[layer, :, :, lanes(number)], canvas.at[layer, :, number, own, :]))
            parts.append((lower.at[layer, :, :, lanes(number)], canvas.at[layer, :, number, beside, :]))
        for number in range(more_lanes):
            parts.append((right.at[layer, :, :, lanes(number)], canvas.at[layer, :, own_lanes + number, own, :]))
            parts.append((corner.at[layer, :, :, lanes(number)], canvas.at[layer, :, own_lanes + number, beside, :]))
    loads = [pltpu.make_async_copy(source, target, load_sems.at[at]) for at, (source, target) in enumerate(parts)]
    for load in loads + table_loads:
        load.start()

    @pl.when(count[0] > 0)
    def _():
        for copy in frame_copies(0):
            copy.start()

    grad[...] = jnp.zeros_like(grad)
    grad_probe[...] = jnp.zeros_like(grad_probe)
    for load in loads + table_loads:
        load.wait()

    @pl.when(lax.axis_index("ty") == lax.axis_size("ty") - 1)
    def _():
        canvas[:, :, :, beside, :] = jnp.zeros((layers, 2, own_lanes + more_lanes, points, 128), jnp.float32)

    @pl.when(lax.axis_index("tx") == lax.axis_size("tx") - 1)
    def _():
        canvas[:, :, pl.ds(own_lanes, more_lanes)] = jnp.zeros((layers, 2, more_lanes, rows + points, 128), jnp.float32)

    def visit(pair, carry):
        slots = [PAIR * pair + at for at in range(PAIR)]
        places = [place_of(row_offsets[slot], column_offsets[slot], points) for slot in slots]
        for copy in frame_copies(pair):
            copy.wait()

        @pl.when(pair + 1 < pairs)
        def _():
            for copy in frame_copies(pair + 1):
                copy.start()

        probe_wave = (probe[0], probe[1])
        windows = [[window_of(canvas, layer, place, points) for layer in range(layers)] for place in places]
        waves = [spread(*times(probe_wave, window[0]), spread_ahead) for window in windows]
        fars = [to_frequencies(*times(wave, window[1]), fourier_ahead) for wave, window in zip(waves, windows)]
        backs = []
        for at, (real, imag) in enumerate(fars):
            pieces = []
            for side in range(points // 128):
                columns[at, side] = jnp.sqrt(frame[lax.rem(pair, 2), at, :, pl.ds(side * 128, 128)] + BACKGROUND)
                pieces.append(jnp.concatenate([columns[at, side, pl.ds(start, half, stride=2), :] for start in range(2)], axis=0))
            target = jnp.concatenate(pieces, axis=1)
            high = target.astype(jnp.bfloat16)
            rest = target - high.astype(jnp.float32)
            middle = rest.astype(jnp.bfloat16)
            low = (rest - middle.astype(jnp.float32)).astype(jnp.bfloat16)
            target = jnp.dot(
                jnp.concatenate([high, middle, low], axis=1), jnp.concatenate([shuffle[...]] * 3, axis=0),
                preferred_element_type=jnp.float32)
            pull = 2.0 - 2.0 * target * lax.rsqrt(real * real + imag * imag + BACKGROUND)
            pull = pull * (slots[at] < count[0]).astype(jnp.float32)
            backs.append((pull * real, pull * imag))
        backs = [from_frequencies(*back, fourier_back) for back in backs]
        for place, wave, back in zip(places, waves, backs):
            add_window(grad, 1, place, points, times_conjugate(wave, back))
        backs = [spread(*times_conjugate(window[1], back), spread_back) for window, back in zip(windows, backs)]
        for place, back in zip(places, backs):
            add_window(grad, 0, place, points, times_conjugate(probe_wave, back))
        more = [times_conjugate(window[0], back) for window, back in zip(windows, backs)]
        for part in range(2):
            grad_probe[part] += sum(one[part] for one in more)
        return carry

    lax.fori_loop(0, pairs, visit, 0)
    writes = [
        pltpu.make_async_copy(grad.at[:, :, own_lanes + number], grad_right.at[:, :, :, lanes(number)], out_sems.at[number])
        for number in range(more_lanes)
    ]
    writes += [
        pltpu.make_async_copy(grad.at[:, :, number, beside, :], grad_lower.at[:, :, :, lanes(number)], out_sems.at[more_lanes + number])
        for number in range(own_lanes)
    ]
    for write in writes:
        write.start()
    for number in range(own_lanes):
        canvas[:, :, number, :rows, :] -= OBJECT_RATE * grad[:, :, number, :rows, :]
        writes.append(pltpu.make_async_copy(
            canvas.at[:, :, number, own, :], moved.at[:, :, :, lanes(number)], out_sems.at[more_lanes + own_lanes + number]))
        writes[-1].start()
    for write in writes:
        write.wait()


ANY = pl.BlockSpec(memory_space=pl.ANY)
WHOLE = pl.BlockSpec(memory_space=pltpu.VMEM)


def gradients(scalars, object_slab, right, lower, corner, arrived, probe_wave):
    layers, _, rows, cols = object_slab.shape
    points = probe_wave.shape[-1]
    tables = build_tables(points)
    shape = lambda *dims: jax.ShapeDtypeStruct(dims, jnp.float32)
    canvas = pltpu.VMEM((layers, 2, (cols + points) // 128, rows + points, 128), jnp.float32)
    lanes = (cols + points) // 128
    return pl.pallas_call(
        gradient_kernel,
        out_shape=[shape(*object_slab.shape), shape(layers, 2, rows + points, points), shape(layers, 2, points, cols),
                   shape(*probe_wave.shape)],
        grid_spec=pltpu.PrefetchScalarGridSpec(
            num_scalar_prefetch=len(scalars),
            grid=(1,),
            in_specs=[ANY] * 5 + [WHOLE] + [ANY] * len(tables),
            out_specs=[ANY] * 3 + [WHOLE],
            scratch_shapes=[
                canvas, canvas,
                pltpu.VMEM((2, PAIR, points, points), jnp.float32),
                pltpu.VMEM((PAIR, points // 128, points, 128), jnp.float32),
                *[pltpu.VMEM(table.shape, jnp.bfloat16) for table in tables],
                pltpu.SemaphoreType.DMA((2 * layers * lanes,)),
                pltpu.SemaphoreType.DMA((len(tables),)),
                pltpu.SemaphoreType.DMA((2, PAIR)),
                pltpu.SemaphoreType.DMA((lanes + cols // 128,)),
            ]),
        compiler_params=pltpu.CompilerParams(vmem_limit_bytes=VMEM_LIMIT),
        cost_estimate=pl.CostEstimate(flops=TILE_CAP * 96 * points**3, bytes_accessed=32 * 1024 * 1024, transcendentals=0),
    )(*scalars, object_slab, right, lower, corner, arrived, probe_wave, *tables)


def finish_kernel(moved, right, lower, out):
    points = right.shape[3]
    out[...] = moved[...]

    @pl.when(lax.axis_index("tx") > 0)
    def _():
        out[0, 0, :, :points] -= OBJECT_RATE * right[0, 0]

    @pl.when(lax.axis_index("ty") > 0)
    def _():
        out[0, 0, :points, :] -= OBJECT_RATE * lower[0, 0]


def finish(moved, right, lower):
    plane = lambda array: pl.BlockSpec((1, 1) + array.shape[2:], lambda layer, part: (layer, part, 0, 0))
    return pl.pallas_call(
        finish_kernel,
        out_shape=jax.ShapeDtypeStruct(moved.shape, moved.dtype),
        grid=moved.shape[:2],
        in_specs=[plane(moved), plane(right), plane(lower)],
        out_specs=plane(moved),
        compiler_params=pltpu.CompilerParams(vmem_limit_bytes=VMEM_LIMIT),
        cost_estimate=pl.CostEstimate(flops=3 * moved.size, bytes_accessed=12 * moved.size, transcendentals=0),
    )(moved, right, lower)


def remote(source, target, send_sem, recv_sem, peer):
    return pltpu.make_async_remote_copy(
        src_ref=source, dst_ref=target, send_sem=send_sem, recv_sem=recv_sem, device_id=peer, device_id_type=MESH)


def when(condition, action):
    pl.when(condition)(lambda: action())


def greet(peers):
    barrier = pltpu.get_barrier_semaphore()
    for peer in peers:
        pl.semaphore_signal(barrier, inc=1, device_id=peer, device_id_type=MESH)
    pl.semaphore_wait(barrier, len(peers))


def detours(n_down, forward):
    half = n_down // 2
    paths = ((half - 1, n_down - 1, half), (half - 1, n_down - 2, half + 1, half), (half - 1, half - 2, half + 1, half))
    return paths if forward else [tuple(n_down - 1 - place for place in path) for path in paths]


def detour(path, along, sources, targets, relay, send_sems, recv_sems, at):
    hops = len(path) - 1
    route = []
    for number, (source, target) in enumerate(zip(sources, targets)):
        route.append([
            remote(
                source if hop == 0 else relay.at[number], target if hop == hops - 1 else relay.at[number],
                send_sems.at[at + number * hops + hop], recv_sems.at[at + number * hops + hop], (jnp.int32(path[hop + 1]), along))
            for hop in range(hops)
        ])
    return route


def set_off(route, path, down):
    for copies in route:
        when(down == path[0], copies[0].start)


def pass_on(routes, paths, down):
    for number in range(HOPS):
        for route, path in zip(routes, paths):
            for hop in range(1, len(path) - 1 if number < len(route) else 0):
                when(down == path[hop], route[number][hop - 1].wait_recv)
                when(down == path[hop], route[number][hop].start)


def arrive(routes, paths, down):
    for route, path in zip(routes, paths):
        for copies in route:
            when(down == path[-1], copies[-1].wait_recv)


def settle(routes, paths, down):
    for route, path in zip(routes, paths):
        for copies in route:
            for hop, copy in enumerate(copies):
                when(down == path[hop], copy.wait_send)


def around(down, along, n_down, n_along):
    row = [(down, lax.rem(along + step, n_along)) for step in range(1, n_along)]
    column = [(lax.rem(down + step, n_down), along) for step in range(1, n_down)]
    return row, column


def frame_peer(down, along, n_down, n_along, step, ahead):
    step_y, step_z, step_core = step
    if not ahead:
        step_y = -step_y % (n_along // 4)
    place_y, place_z, core = along // 4, lax.rem(along // 2, 2), lax.rem(along, 2)
    other = step_z * jnp.maximum(step_core, core)
    place_y = lax.rem(place_y + step_y, n_along // 4)
    place_z = lax.rem(place_z + step_z, 2)
    core = lax.rem(core + step_core, 2)
    return (lax.rem(down + other * (n_down // 2), n_down), place_y * 4 + place_z * 2 + core), other


def fetch_kernel(source, frames, slab, right, lower, corner, arrived, held, picked, lower_relay, right_relay, held_sem, own_sem,
                 send_sems, recv_sems):
    down, along = lax.axis_index("ty"), lax.axis_index("tx")
    n_down, n_along = lax.axis_size("ty"), lax.axis_size("tx")
    layers, points, rows, cols = right.shape[0], right.shape[3], right.shape[2], lower.shape[3]
    half = n_down // 2
    load = pltpu.make_async_copy(frames, held, held_sem)
    load.start()
    ring = lambda by_down, by_along: (lax.rem(down + by_down + n_down, n_down), lax.rem(along + by_along + n_along, n_along))
    greet([frame_peer(down, along, n_down, n_along, step, False)[0] for step in FRAME_STEPS]
          + [ring(by, 0) for by in (1, -1, half, 3, -3)] + [ring(0, by) for by in (1, -1, 3, -3, 4, -4)])
    above, left = ring(-1, 0), ring(0, -1)
    not_top, not_bottom = down > 0, down < n_down - 1
    not_first, not_last = along > 0, along < n_along - 1
    paths = detours(n_down, False)
    wraps, joins = down == half, down == half - 1
    crosses, carries = lax.rem(along, 4) == 0, lax.rem(along, 4) == 3
    crossed = carries & not_last
    across = crosses & not_first
    base = n_along - 1
    index = iter(range(base, base + 64))

    def copy(source_ref, target, peer, at=None):
        at = next(index) if at is None else at
        return remote(source_ref, target, send_sems.at[at], recv_sems.at[at], peer)

    first, last = 0, layers - 1
    side = [slab.at[layer, :, :, pl.ds(0, points)] for layer in range(layers)]
    edge = [lower.at[layer, :, :, pl.ds(0, points)] for layer in range(layers)]
    rest, start = pl.ds(points, cols - points), pl.ds(0, points)
    lowers, others, rights, corners = [], [], [], []
    for layer in range(layers):
        lowers.append(copy(slab.at[layer, :, pl.ds(0, points), start], lower.at[layer, :, :, start], above))
        others.append(copy(slab.at[layer, :, pl.ds(0, points), rest], lower.at[layer, :, :, rest], above))
        rights.append(copy(side[layer], right.at[layer], left))
        corners.append(copy(edge[layer], corner.at[layer], left))
    at_right, at_corner = base + 4 * last + 2, base + 4 * last + 3
    right_hop = copy(side[last], right_relay.at[:, pl.ds(0, rows), :], ring(0, 3))
    right_forward = copy(right_relay.at[:, pl.ds(0, rows), :], right.at[last], ring(0, -4), at_right)
    corner_hop = copy(edge[last], right_relay.at[:, pl.ds(rows, points), :], ring(0, 3))
    corner_forward = copy(right_relay.at[:, pl.ds(rows, points), :], corner.at[last], ring(0, -4), at_corner)

    chunk = points // HOPS
    routes = []
    at = base + 4 * layers + 2
    for number, (path, layer, lanes) in enumerate(zip(paths, (last, first, last), (start, rest, rest))):
        pieces = [pl.ds(piece * chunk, chunk) for piece in range(HOPS)]
        routes.append(detour(
            path, along, [slab.at[layer, :, piece, lanes] for piece in pieces], [lower.at[layer, :, piece, lanes] for piece in pieces],
            lower_relay.at[number], send_sems, recv_sems, at))
        at += HOPS * (len(path) - 1)
    ahead = (lowers[first], lowers[last], others[first], others[last])
    when(not_top, lowers[first].start)
    for go in ahead[1:]:
        when(not_top & ~wraps, go.start)
    when(across, right_hop.start)
    when(not_first & ~crosses, rights[last].start)
    when(not_first, rights[first].start)
    load.wait()
    sends = []

    def send_frames(steps):
        for step in steps:
            peer, other = frame_peer(down, along, n_down, n_along, FRAME_STEPS[step], True)
            picked[step] = held[source[other * n_along + peer[1]]]
            send = remote(picked.at[step], arrived.at[along], send_sems.at[step], recv_sems.at[step], peer)
            send.start()
            sends.append(send)

    send_frames(range(EARLY_FRAMES[0]))
    for route, path in zip(routes, paths):
        set_off(route, path, down)
    picked[n_along - 1] = held[source[along]]
    own = pltpu.make_async_copy(picked.at[n_along - 1], arrived.at[along], own_sem)
    own.start()
    relays = along >= 4
    when(carries & relays, right_hop.wait_recv)
    when(carries & relays, right_forward.start)
    pass_on(routes, paths, down)
    for layer in range(layers):
        if layer == last:
            arrive(routes[:1], paths[:1], down)
            when(not_bottom & ~joins, lowers[layer].wait_recv)
        else:
            when(not_bottom, lowers[layer].wait_recv)
        if layer == last:
            when(not_bottom & across, corner_hop.start)
            when(not_bottom & not_first & ~crosses, corners[layer].start)
            when(not_bottom & carries & relays, corner_hop.wait_recv)
            when(not_bottom & carries & relays, corner_forward.start)
        else:
            when(not_bottom & not_first, corners[layer].start)
            send_frames(range(EARLY_FRAMES[0], EARLY_FRAMES[1]))
    send_frames(range(EARLY_FRAMES[1], len(FRAME_STEPS)))
    when(not_top, lowers[first].wait_send)
    for go in ahead[1:]:
        when(not_top & ~wraps, go.wait_send)
    for layer in range(layers):
        when(not_bottom & ~joins, others[layer].wait_recv)
        when(not_last, rights[layer].wait_recv)
        when(not_bottom & not_last, corners[layer].wait_recv)
        if layer == last:
            when(across, right_hop.wait_send)
            when(not_first & ~crosses, rights[layer].wait_send)
            when(carries & relays, right_forward.wait_send)
            when(not_bottom & across, corner_hop.wait_send)
            when(not_bottom & not_first & ~crosses, corners[layer].wait_send)
            when(not_bottom & carries & relays, corner_forward.wait_send)
        else:
            when(not_first, rights[layer].wait_send)
            when(not_bottom & not_first, corners[layer].wait_send)
    arrive(routes[1:], paths[1:], down)
    settle(routes, paths, down)
    for send in sends:
        send.wait()
    own.wait()


def fetch(source, frames, object_slab, points):
    layers, _, rows, cols = object_slab.shape
    n_along = lax.axis_size("tx")
    copies = n_along - 1 + 4 * layers + 2 + 8 * HOPS
    shape = lambda *dims: jax.ShapeDtypeStruct(dims, jnp.float32)
    return pl.pallas_call(
        fetch_kernel,
        out_shape=[shape(layers, 2, rows, points), shape(layers, 2, points, cols), shape(layers, 2, points, points),
                   shape(n_along, points, points)],
        in_specs=[pl.BlockSpec(memory_space=pltpu.SMEM), ANY, ANY],
        out_specs=[ANY] * 4,
        scratch_shapes=[
            pltpu.VMEM(frames.shape, jnp.float32),
            pltpu.VMEM((n_along, points, points), jnp.float32),
            pltpu.VMEM((3, HOPS, 2, points // HOPS, points), jnp.float32),
            pltpu.VMEM((2, rows + points, points), jnp.float32),
            pltpu.SemaphoreType.DMA,
            pltpu.SemaphoreType.DMA,
            pltpu.SemaphoreType.DMA((copies,)),
            pltpu.SemaphoreType.DMA((copies,)),
        ],
        compiler_params=pltpu.CompilerParams(collective_id=0, has_side_effects=True, vmem_limit_bytes=VMEM_LIMIT),
    )(source, frames, object_slab)


def return_kernel(scale, all_right, all_lower, grad_probe, probe, right_in, lower_in, probe_out,
                  corner_in, held, relay, from_row, row_sum, from_column, load_sems, send_sems, recv_sems):
    down, along = lax.axis_index("ty"), lax.axis_index("tx")
    n_down, n_along = lax.axis_size("ty"), lax.axis_size("tx")
    rights, lowers = ([ref.at[layer] for layer in range(ref.shape[0])] for ref in (all_right, all_lower))
    layers, points, rows, cols = len(rights), right_in.shape[3], right_in.shape[2], lower_in.shape[3]
    loads = [
        pltpu.make_async_copy(lowers[layer].at[:, :, pl.ds(0, points)], held.at[layer], load_sems.at[layer])
        for layer in range(layers)
    ]
    for load in loads:
        load.start()
    row_peers, column_peers = around(down, along, n_down, n_along)
    greet(row_peers + column_peers)
    part = grad_probe.shape[0] // n_along

    def piece_of(number, start):
        return pl.ds(pl.multiple_of(start + number // 2 * 8, 8), 8), pl.ds(pl.multiple_of(lax.rem(number, 2) * 128, 128), 128)

    below, after = (lax.rem(down + 1, n_down), along), (down, lax.rem(along + 1, n_along))
    not_top, not_bottom = down > 0, down < n_down - 1
    not_first, not_last = along > 0, along < n_along - 1

    def exchange(index, source, target, peer):
        copy = remote(source, target, send_sems.at[index], recv_sems.at[index], peer)
        copy.start()
        return copy

    def aligned(start, size):
        return pl.ds(pl.multiple_of(start, 8), size)

    row_copies = [
        exchange(step, grad_probe.at[aligned(peer[1] * part, part)], from_row.at[step], peer) for step, peer in enumerate(row_peers)
    ]
    base = 2 * (n_along + n_down - 2)
    corners, sides, firsts, seconds = [], [], [], []
    half = n_down // 2
    paths = detours(n_down, True)
    wraps, joins = down == half - 1, down == half
    start, rest = pl.ds(0, points), pl.ds(points, cols - points)
    for layer in range(layers):
        at = base + 4 * layer
        corners.append(remote(rights[layer].at[:, pl.ds(rows, points), :], corner_in.at[layer], send_sems.at[at], recv_sems.at[at], after))
        sides.append(remote(rights[layer].at[:, pl.ds(0, rows), :], right_in.at[layer], send_sems.at[at + 1], recv_sems.at[at + 1], after))
        firsts.append(remote(lowers[layer].at[:, :, rest], lower_in.at[layer, :, :, rest], send_sems.at[at + 2], recv_sems.at[at + 2], below))
        seconds.append(remote(held.at[layer], lower_in.at[layer, :, :, start], send_sems.at[at + 3], recv_sems.at[at + 3], below))
    first, last = 0, layers - 1
    chunk = points // HOPS
    pieces = [pl.ds(piece * chunk, chunk) for piece in range(HOPS)]
    routes = []
    at = base + 4 * layers
    straight = (half - 1, half)
    plan = ((paths[0], last, start, 0, HOPS, 0), (paths[1], first, rest, 0, 3, 1), (straight, first, rest, 3, HOPS, 1),
            (paths[2], last, rest, 0, 3, 2), (straight, last, rest, 3, HOPS, 2))
    paths = [path for path, *_ in plan]
    for path, layer, span, begin, end, number in plan:
        held_rows = held.at[layer] if number == 0 else lowers[layer].at[:, :, span]
        routes.append(detour(
            path, along, [held_rows.at[:, piece, :] for piece in pieces[begin:end]],
            [lower_in.at[layer, :, piece, span] for piece in pieces[begin:end]], relay.at[number], send_sems, recv_sems, at))
        at += (end - begin) * (len(path) - 1)
    for layer in range(layers):
        when(not_bottom & not_last, corners[layer].start)

    when(not_bottom & ~wraps, firsts[0].start)
    total = grad_probe[aligned(along * part, part)]
    for step, copy in enumerate(row_copies):
        copy.wait()
        total = total + from_row[step]
    row_sum[...] = total
    at = n_along - 1
    copies = [
        exchange(at + step, row_sum.at[piece_of(peer[0], 0)], from_column.at[step], peer)
        for step, peer in enumerate(column_peers)
    ]
    total = row_sum[piece_of(down, 0)]
    for step, copy in enumerate(copies):
        copy.wait()
        total = total + from_column[step]
    mine = piece_of(down, along * part)
    probe_out[mine] = probe[mine] - scale * total
    at += n_down - 1
    copies = [exchange(at + step, probe_out.at[mine], probe_out.at[mine], peer) for step, peer in enumerate(column_peers)]
    for layer in range(1, layers):
        when(not_bottom & ~wraps, firsts[layer].start)
    for copy in copies:
        copy.wait()
    at += n_down - 1
    mine = aligned(along * part, part)
    row_copies = [exchange(at + step, probe_out.at[mine], probe_out.at[mine], peer) for step, peer in enumerate(row_peers)]
    for route, path in zip(routes[1:], paths[1:]):
        set_off(route, path, down)
    for layer in range(layers):
        when(not_last, sides[layer].start)

    for layer in range(layers):
        loads[layer].wait()
        when(not_bottom & not_first, corners[layer].wait_recv)

        @pl.when(not_bottom & not_first)
        def _():
            held[layer] += corner_in[layer]

        if layer == last:
            set_off(routes[0], paths[0], down)
            when(not_bottom & ~wraps, seconds[layer].start)
        else:
            when(not_bottom, seconds[layer].start)
    pass_on(routes[1:], paths[1:], down)
    pass_on(routes[:1], paths[:1], down)
    for copy in row_copies:
        copy.wait()
    for layer in range(layers):
        when(not_bottom & not_last, corners[layer].wait_send)
        when(not_last, sides[layer].wait_send)
        when(not_first, sides[layer].wait_recv)
        when(not_bottom & ~wraps, firsts[layer].wait_send)
        when(not_top & ~joins, firsts[layer].wait_recv)
        if layer == last:
            when(not_bottom & ~wraps, seconds[layer].wait_send)
            when(not_top & ~joins, seconds[layer].wait_recv)
        else:
            when(not_bottom, seconds[layer].wait_send)
            when(not_top, seconds[layer].wait_recv)
    arrive(routes, paths, down)
    settle(routes, paths, down)


def send_back(grad_right, grad_lower, grad_probe, probe_wave, scale, rows):
    layers, _, points, cols = grad_lower.shape
    flat = (2 * points, points)
    n_down, n_along = lax.axis_size("ty"), lax.axis_size("tx")
    part = flat[0] // n_along
    copies = 2 * (n_along + n_down - 2) + 4 * layers + 8 * HOPS
    shape = lambda *dims: jax.ShapeDtypeStruct(dims, jnp.float32)
    right_in, lower_in, probe = pl.pallas_call(
        functools.partial(return_kernel, scale),
        out_shape=[shape(layers, 2, rows, points), shape(layers, 2, points, cols), shape(*flat)],
        in_specs=[ANY, ANY, WHOLE, WHOLE],
        out_specs=[ANY, ANY, WHOLE],
        scratch_shapes=[
            pltpu.VMEM((layers, 2, points, points), jnp.float32),
            pltpu.VMEM((layers, 2, points, points), jnp.float32),
            pltpu.VMEM((3, HOPS, 2, points // HOPS, points), jnp.float32),
            pltpu.VMEM((n_along - 1, part, points), jnp.float32),
            pltpu.VMEM((part, points), jnp.float32),
            pltpu.VMEM((n_down - 1, 8, 128), jnp.float32),
            pltpu.SemaphoreType.DMA((layers,)),
            pltpu.SemaphoreType.DMA((copies,)),
            pltpu.SemaphoreType.DMA((copies,)),
        ],
        compiler_params=pltpu.CompilerParams(collective_id=1, has_side_effects=True, vmem_limit_bytes=VMEM_LIMIT),
    )(grad_right, grad_lower, grad_probe.reshape(flat), probe_wave.reshape(flat))
    return right_in, lower_in, probe.reshape(probe_wave.shape)


def local(object_slab, probe_wave, frames, scan_tiles, scan_offsets):
    columns = lax.axis_size("tx")
    row_index = lax.axis_index("ty")
    col_index = lax.axis_index("tx")
    owned = frames.shape[0]
    points = probe_wave.shape[-1]
    layers, _, tile_rows, tile_cols = object_slab.shape
    total_frames = owned * columns
    my_tile = row_index * columns + col_index
    by_owner = scan_tiles.reshape(columns, owned)

    mine = lax.dynamic_index_in_dim(by_owner, col_index, 0, keepdims=False)
    other_row = lax.rem(row_index + lax.axis_size("ty") // 2, lax.axis_size("ty"))
    places = jnp.arange(columns, dtype=jnp.int32)
    wanted = jnp.concatenate([row_index * columns + places, other_row * columns + places])
    source = jnp.sum((mine[None, :] == wanted[:, None]).astype(jnp.int32) * jnp.arange(owned, dtype=jnp.int32)[None, :], axis=1)

    right, lower, corner, arrived = fetch(source, frames, object_slab, points)

    matches = (by_owner == my_tile).astype(jnp.int32)
    present = jnp.sum(matches, axis=1)
    ranks = jnp.cumsum(present) - 1
    slot_pick = present[None, :] * (ranks[None, :] == jnp.arange(TILE_CAP, dtype=jnp.int32)[:, None]).astype(jnp.int32)
    by_slot = lambda values: jnp.sum(slot_pick * values[None, :], axis=1)
    row_offsets, column_offsets = (
        by_slot(jnp.sum(matches * scan_offsets[:, side].reshape(columns, owned), axis=1)) for side in range(2))
    owners = by_slot(places)
    scalars = (row_offsets, column_offsets, jnp.sum(present).reshape(1), owners)

    moved, grad_right, grad_lower, grad_probe = gradients(scalars, object_slab, right, lower, corner, arrived, probe_wave)
    right_back, lower_back, new_probe = send_back(
        grad_right, grad_lower, grad_probe, probe_wave, PROBE_RATE / total_frames, object_slab.shape[2])
    return finish(moved, right_back, lower_back), new_probe


def solution(mesh):
    return jax.shard_map(
        local,
        mesh=mesh,
        in_specs=(P(None, None, "ty", "tx"), P(), P("tx", None, None), P(), P()),
        out_specs=(P(None, None, "ty", "tx"), P()),
        check_vma=False,
    )
```

```python
import functools
import math

import jax
import jax.numpy as jnp
import ml_dtypes
import numpy as np
from jax import lax
from jax.experimental import pallas as pl
from jax.experimental.pallas import tpu as pltpu
from jax.sharding import PartitionSpec as P

MESH = pl.DeviceIdType.MESH
TILE_CAP = 8
HOPS = 8
PAIR = 2
EARLY_FRAMES = (12, 14)
BACKGROUND = 0.5
FRESNEL = 0.25
OBJECT_RATE = 0.25
PROBE_RATE = 4.0
VMEM_LIMIT = 56 * 1024 * 1024


FRAME_STEPS = ((1, 0, 0), (3, 0, 0), (0, 1, 1), (2, 0, 0), (1, 1, 1), (3, 1, 1), (0, 1, 0), (2, 1, 1), (1, 0, 1), (3, 0, 1), (2, 0, 1),
               (1, 1, 0), (3, 1, 0), (2, 1, 0), (0, 0, 1))


def real_form(matrix):
    return np.block([[matrix.real, -matrix.imag], [matrix.imag, matrix.real]])


def split_table(table):
    high = table.astype(ml_dtypes.bfloat16)
    low = (table - high.astype(np.float64)).astype(ml_dtypes.bfloat16)
    return high, low


def left_table(table):
    return np.concatenate(split_table(table), axis=1)


def half_transforms(points):
    half = points // 2
    places = np.arange(half)
    even = np.exp(-2j * np.pi * ((2 * places[:, None]) * places[None, :] % points) / points)
    odd = np.exp(-2j * np.pi * ((2 * places[:, None] + 1) * places[None, :] % points) / points)
    return even / math.sqrt(points), odd / math.sqrt(points)


def build_tables(points):
    even, odd = half_transforms(points)
    places = np.arange(points)
    frequency = (places + points // 2) % points - points // 2
    phase = np.exp(-1j * np.pi * FRESNEL / points * frequency.astype(np.float64) ** 2)
    spread_even = even.conj().T @ (phase[0::2, None] * even)
    spread_odd = odd.conj().T @ (phase[1::2, None] * odd)
    spread = [real_form(spread_even), real_form(spread_odd)]
    fourier = [real_form(even), real_form(odd)]
    order = np.concatenate([places[0::2], places[1::2]])
    shuffle = (places[:, None] == order[None, :]).astype(ml_dtypes.bfloat16)

    groups = [spread, [table.T for table in spread], fourier, [table.T for table in fourier]]
    return np.stack([left_table(table) for group in groups for table in group]), shuffle


def split(value):
    high = value.astype(jnp.bfloat16)
    low = (value - high.astype(jnp.float32)).astype(jnp.bfloat16)
    return high, low


def left_product(table, value):
    high, low = split(value)
    size = value.shape[0]
    table = jnp.concatenate([table[...], table[:, :size]], axis=1)
    return jnp.dot(table, jnp.concatenate([high, high, low], axis=0), preferred_element_type=jnp.float32)


def right_product(value, table):
    high, low = split(value)
    size = value.shape[1]
    table = jnp.concatenate([table[:, :size], table[:, size:], table[:, :size]], axis=0)
    return jnp.dot(jnp.concatenate([high, high, low], axis=1), table, preferred_element_type=jnp.float32)


def halves(value, axis):
    half = value.shape[axis] // 2
    first = lax.slice_in_dim(value, 0, half, axis=axis)
    second = lax.slice_in_dim(value, half, 2 * half, axis=axis)
    return first, second


def apart(real, imag, axis):
    real_a, real_b = halves(real, axis)
    imag_a, imag_b = halves(imag, axis)
    plus = jnp.concatenate([real_a + real_b, imag_a + imag_b], axis=axis)
    minus = jnp.concatenate([real_a - real_b, imag_a - imag_b], axis=axis)
    return plus, minus


def together(plus, minus, axis):
    plus_re, plus_im = halves(plus, axis)
    minus_re, minus_im = halves(minus, axis)
    real = jnp.concatenate([plus_re + minus_re, plus_re - minus_re], axis=axis)
    imag = jnp.concatenate([plus_im + minus_im, plus_im - minus_im], axis=axis)
    return real, imag


def regroup(even, odd, axis):
    even_re, even_im = halves(even, axis)
    odd_re, odd_im = halves(odd, axis)
    return jnp.concatenate([even_re, odd_re], axis=axis), jnp.concatenate([even_im, odd_im], axis=axis)


def spread(real, imag, tables):
    left_even, left_odd, right_even, right_odd = tables
    plus, minus = apart(real, imag, 0)
    real, imag = together(left_product(left_even, plus), left_product(left_odd, minus), 0)
    plus, minus = apart(real, imag, 1)
    return together(right_product(plus, right_even), right_product(minus, right_odd), 1)


def to_frequencies(real, imag, tables):
    left_even, left_odd, right_even, right_odd = tables
    plus, minus = apart(real, imag, 0)
    real, imag = regroup(left_product(left_even, plus), left_product(left_odd, minus), 0)
    plus, minus = apart(real, imag, 1)
    return regroup(right_product(plus, right_even), right_product(minus, right_odd), 1)


def from_frequencies(real, imag, tables):
    left_even, left_odd, right_even, right_odd = tables
    even, odd = regroup(real, imag, 0)
    real, imag = together(left_product(left_even, even), left_product(left_odd, odd), 0)
    even, odd = regroup(real, imag, 1)
    return together(right_product(even, right_even), right_product(odd, right_odd), 1)


def place_of(row, column, points):
    return pl.ds(row, points), column // 128, lax.rem(column, 128)


def window_of(canvas, layer, place, points):
    rows, first, along = place
    before = lax.broadcasted_iota(jnp.int32, (points, 128), 1) < 128 - along
    parts = []
    for part in range(2):
        turned = [
            pltpu.roll(canvas[layer, part, first + step, rows, :], lax.rem(128 - along, 128), 1)
            for step in range(points // 128 + 1)
        ]
        parts.append(jnp.concatenate([jnp.where(before, one, other) for one, other in zip(turned, turned[1:])], axis=1))
    return parts


def add_window(canvas, layer, place, points, parts):
    rows, first, along = place
    inside = lax.broadcasted_iota(jnp.int32, (points, 128), 1) >= along
    for part in range(2):
        turned = [pltpu.roll(parts[part][:, at:at + 128], along, 1) for at in range(0, points, 128)]
        none = jnp.zeros((points, 128), jnp.float32)
        for step, (one, other) in enumerate(zip(turned + [none], [none] + turned)):
            canvas[layer, part, first + step, rows, :] += jnp.where(inside, one, other)


def times(a, b):
    return a[0] * b[0] - a[1] * b[1], a[0] * b[1] + a[1] * b[0]


def times_conjugate(a, b):
    return a[0] * b[0] + a[1] * b[1], a[0] * b[1] - a[1] * b[0]


def gradient_kernel(row_offsets, column_offsets, count, owners, slab, right, lower, corner, arrived, probe, tables_all, shuffle_all, moved,
                    grad_right, grad_lower, grad_probe, canvas, grad, frame, columns, tables, shuffle, load_sems,
                    table_sems, frame_sems, out_sems):
    table_loads = [
        pltpu.make_async_copy(source, target, table_sems.at[at])
        for at, (source, target) in enumerate(((tables_all, tables), (shuffle_all, shuffle)))
    ]
    spread_ahead, spread_back, fourier_ahead, fourier_back = (
        [tables.at[at] for at in order] for order in ((0, 1, 2, 3), (2, 3, 0, 1), (4, 5, 6, 7), (6, 7, 4, 5)))
    layers, rows, cols = slab.shape[0], slab.shape[2], slab.shape[3]
    points = probe.shape[1]
    half = points // 2
    own_lanes, more_lanes = cols // 128, points // 128
    own, beside = pl.ds(0, rows), pl.ds(rows, points)

    def lanes(number):
        return pl.ds(128 * number, 128)

    pairs = (count[0] + PAIR - 1) // PAIR

    def frame_copies(pair):
        side = lax.rem(pair, 2)
        return [
            pltpu.make_async_copy(arrived.at[owners[PAIR * pair + at]], frame.at[side, at], frame_sems.at[side, at])
            for at in range(PAIR)
        ]

    parts = []
    for layer in range(layers):
        for number in range(own_lanes):
            parts.append((slab.at[layer, :, :, lanes(number)], canvas.at[layer, :, number, own, :]))
            parts.append((lower.at[layer, :, :, lanes(number)], canvas.at[layer, :, number, beside, :]))
        for number in range(more_lanes):
            parts.append((right.at[layer, :, :, lanes(number)], canvas.at[layer, :, own_lanes + number, own, :]))
            parts.append((corner.at[layer, :, :, lanes(number)], canvas.at[layer, :, own_lanes + number, beside, :]))
    loads = [pltpu.make_async_copy(source, target, load_sems.at[at]) for at, (source, target) in enumerate(parts)]
    for load in loads + table_loads:
        load.start()

    @pl.when(count[0] > 0)
    def _():
        for copy in frame_copies(0):
            copy.start()

    grad[...] = jnp.zeros_like(grad)
    grad_probe[...] = jnp.zeros_like(grad_probe)
    for load in loads + table_loads:
        load.wait()

    @pl.when(lax.axis_index("ty") == lax.axis_size("ty") - 1)
    def _():
        canvas[:, :, :, beside, :] = jnp.zeros((layers, 2, own_lanes + more_lanes, points, 128), jnp.float32)

    @pl.when(lax.axis_index("tx") == lax.axis_size("tx") - 1)
    def _():
        canvas[:, :, pl.ds(own_lanes, more_lanes)] = jnp.zeros((layers, 2, more_lanes, rows + points, 128), jnp.float32)

    def visit(pair, carry):
        slots = [PAIR * pair + at for at in range(PAIR)]
        places = [place_of(row_offsets[slot], column_offsets[slot], points) for slot in slots]
        for copy in frame_copies(pair):
            copy.wait()

        @pl.when(pair + 1 < pairs)
        def _():
            for copy in frame_copies(pair + 1):
                copy.start()

        probe_wave = (probe[0], probe[1])
        windows = [[window_of(canvas, layer, place, points) for layer in range(layers)] for place in places]
        waves = [spread(*times(probe_wave, window[0]), spread_ahead) for window in windows]
        fars = [to_frequencies(*times(wave, window[1]), fourier_ahead) for wave, window in zip(waves, windows)]
        backs = []
        for at, (real, imag) in enumerate(fars):
            pieces = []
            for side in range(points // 128):
                columns[at, side] = jnp.sqrt(frame[lax.rem(pair, 2), at, :, pl.ds(side * 128, 128)] + BACKGROUND)
                pieces.append(jnp.concatenate([columns[at, side, pl.ds(start, half, stride=2), :] for start in range(2)], axis=0))
            target = jnp.concatenate(pieces, axis=1)
            high = target.astype(jnp.bfloat16)
            rest = target - high.astype(jnp.float32)
            middle = rest.astype(jnp.bfloat16)
            low = (rest - middle.astype(jnp.float32)).astype(jnp.bfloat16)
            target = jnp.dot(
                jnp.concatenate([high, middle, low], axis=1), jnp.concatenate([shuffle[...]] * 3, axis=0),
                preferred_element_type=jnp.float32)
            pull = 2.0 - 2.0 * target * lax.rsqrt(real * real + imag * imag + BACKGROUND)
            pull = pull * (slots[at] < count[0]).astype(jnp.float32)
            backs.append((pull * real, pull * imag))
        backs = [from_frequencies(*back, fourier_back) for back in backs]
        for place, wave, back in zip(places, waves, backs):
            add_window(grad, 1, place, points, times_conjugate(wave, back))
        backs = [spread(*times_conjugate(window[1], back), spread_back) for window, back in zip(windows, backs)]
        for place, back in zip(places, backs):
            add_window(grad, 0, place, points, times_conjugate(probe_wave, back))
        more = [times_conjugate(window[0], back) for window, back in zip(windows, backs)]
        for part in range(2):
            grad_probe[part] += sum(one[part] for one in more)
        return carry

    lax.fori_loop(0, pairs, visit, 0)
    writes = [
        pltpu.make_async_copy(grad.at[:, :, own_lanes + number], grad_right.at[:, :, :, lanes(number)], out_sems.at[number])
        for number in range(more_lanes)
    ]
    writes += [
        pltpu.make_async_copy(grad.at[:, :, number, beside, :], grad_lower.at[:, :, :, lanes(number)], out_sems.at[more_lanes + number])
        for number in range(own_lanes)
    ]
    for write in writes:
        write.start()
    for number in range(own_lanes):
        canvas[:, :, number, :rows, :] -= OBJECT_RATE * grad[:, :, number, :rows, :]
        writes.append(pltpu.make_async_copy(
            canvas.at[:, :, number, own, :], moved.at[:, :, :, lanes(number)], out_sems.at[more_lanes + own_lanes + number]))
        writes[-1].start()
    for write in writes:
        write.wait()


ANY = pl.BlockSpec(memory_space=pl.ANY)
WHOLE = pl.BlockSpec(memory_space=pltpu.VMEM)


def gradients(scalars, object_slab, right, lower, corner, arrived, probe_wave):
    layers, _, rows, cols = object_slab.shape
    points = probe_wave.shape[-1]
    tables = build_tables(points)
    shape = lambda *dims: jax.ShapeDtypeStruct(dims, jnp.float32)
    canvas = pltpu.VMEM((layers, 2, (cols + points) // 128, rows + points, 128), jnp.float32)
    lanes = (cols + points) // 128
    return pl.pallas_call(
        gradient_kernel,
        out_shape=[shape(*object_slab.shape), shape(layers, 2, rows + points, points), shape(layers, 2, points, cols),
                   shape(*probe_wave.shape)],
        grid_spec=pltpu.PrefetchScalarGridSpec(
            num_scalar_prefetch=len(scalars),
            grid=(1,),
            in_specs=[ANY] * 5 + [WHOLE] + [ANY] * len(tables),
            out_specs=[ANY] * 3 + [WHOLE],
            scratch_shapes=[
                canvas, canvas,
                pltpu.VMEM((2, PAIR, points, points), jnp.float32),
                pltpu.VMEM((PAIR, points // 128, points, 128), jnp.float32),
                *[pltpu.VMEM(table.shape, jnp.bfloat16) for table in tables],
                pltpu.SemaphoreType.DMA((2 * layers * lanes,)),
                pltpu.SemaphoreType.DMA((len(tables),)),
                pltpu.SemaphoreType.DMA((2, PAIR)),
                pltpu.SemaphoreType.DMA((lanes + cols // 128,)),
            ]),
        compiler_params=pltpu.CompilerParams(vmem_limit_bytes=VMEM_LIMIT),
        cost_estimate=pl.CostEstimate(flops=TILE_CAP * 96 * points**3, bytes_accessed=32 * 1024 * 1024, transcendentals=0),
    )(*scalars, object_slab, right, lower, corner, arrived, probe_wave, *tables)


def finish_kernel(moved, right, lower, out):
    points = right.shape[3]
    out[...] = moved[...]

    @pl.when(lax.axis_index("tx") > 0)
    def _():
        out[0, 0, :, :points] -= OBJECT_RATE * right[0, 0]

    @pl.when(lax.axis_index("ty") > 0)
    def _():
        out[0, 0, :points, :] -= OBJECT_RATE * lower[0, 0]


def finish(moved, right, lower):
    plane = lambda array: pl.BlockSpec((1, 1) + array.shape[2:], lambda layer, part: (layer, part, 0, 0))
    return pl.pallas_call(
        finish_kernel,
        out_shape=jax.ShapeDtypeStruct(moved.shape, moved.dtype),
        grid=moved.shape[:2],
        in_specs=[plane(moved), plane(right), plane(lower)],
        out_specs=plane(moved),
        compiler_params=pltpu.CompilerParams(vmem_limit_bytes=VMEM_LIMIT),
        cost_estimate=pl.CostEstimate(flops=3 * moved.size, bytes_accessed=12 * moved.size, transcendentals=0),
    )(moved, right, lower)


def remote(source, target, send_sem, recv_sem, peer):
    return pltpu.make_async_remote_copy(
        src_ref=source, dst_ref=target, send_sem=send_sem, recv_sem=recv_sem, device_id=peer, device_id_type=MESH)


def when(condition, action):
    pl.when(condition)(lambda: action())


def greet(peers):
    barrier = pltpu.get_barrier_semaphore()
    for peer in peers:
        pl.semaphore_signal(barrier, inc=1, device_id=peer, device_id_type=MESH)
    pl.semaphore_wait(barrier, len(peers))


def detours(n_down, forward):
    half = n_down // 2
    paths = ((half - 1, n_down - 1, half), (half - 1, n_down - 2, half + 1, half), (half - 1, half - 2, half + 1, half))
    return paths if forward else [tuple(n_down - 1 - place for place in path) for path in paths]


def detour(path, along, sources, targets, relay, send_sems, recv_sems, at):
    hops = len(path) - 1
    route = []
    for number, (source, target) in enumerate(zip(sources, targets)):
        route.append([
            remote(
                source if hop == 0 else relay.at[number], target if hop == hops - 1 else relay.at[number],
                send_sems.at[at + number * hops + hop], recv_sems.at[at + number * hops + hop], (jnp.int32(path[hop + 1]), along))
            for hop in range(hops)
        ])
    return route


def set_off(route, path, down):
    for copies in route:
        when(down == path[0], copies[0].start)


def pass_on(routes, paths, down):
    for number in range(HOPS):
        for route, path in zip(routes, paths):
            for hop in range(1, len(path) - 1 if number < len(route) else 0):
                when(down == path[hop], route[number][hop - 1].wait_recv)
                when(down == path[hop], route[number][hop].start)


def arrive(routes, paths, down):
    for route, path in zip(routes, paths):
        for copies in route:
            when(down == path[-1], copies[-1].wait_recv)


def settle(routes, paths, down):
    for route, path in zip(routes, paths):
        for copies in route:
            for hop, copy in enumerate(copies):
                when(down == path[hop], copy.wait_send)


def around(down, along, n_down, n_along):
    row = [(down, lax.rem(along + step, n_along)) for step in range(1, n_along)]
    column = [(lax.rem(down + step, n_down), along) for step in range(1, n_down)]
    return row, column


def frame_peer(down, along, n_down, n_along, step, ahead):
    step_y, step_z, step_core = step
    if not ahead:
        step_y = -step_y % (n_along // 4)
    place_y, place_z, core = along // 4, lax.rem(along // 2, 2), lax.rem(along, 2)
    other = step_z * jnp.maximum(step_core, core)
    place_y = lax.rem(place_y + step_y, n_along // 4)
    place_z = lax.rem(place_z + step_z, 2)
    core = lax.rem(core + step_core, 2)
    return (lax.rem(down + other * (n_down // 2), n_down), place_y * 4 + place_z * 2 + core), other


def fetch_kernel(source, frames, slab, right, lower, corner, arrived, held, picked, lower_relay, right_relay, held_sem, own_sem,
                 send_sems, recv_sems):
    down, along = lax.axis_index("ty"), lax.axis_index("tx")
    n_down, n_along = lax.axis_size("ty"), lax.axis_size("tx")
    layers, points, rows, cols = right.shape[0], right.shape[3], right.shape[2], lower.shape[3]
    half = n_down // 2
    load = pltpu.make_async_copy(frames, held, held_sem)
    load.start()
    ring = lambda by_down, by_along: (lax.rem(down + by_down + n_down, n_down), lax.rem(along + by_along + n_along, n_along))
    greet([frame_peer(down, along, n_down, n_along, step, False)[0] for step in FRAME_STEPS]
          + [ring(by, 0) for by in (1, -1, half, 3, -3)] + [ring(0, by) for by in (1, -1, 3, -3, 4, -4)])
    above, left = ring(-1, 0), ring(0, -1)
    not_top, not_bottom = down > 0, down < n_down - 1
    not_first, not_last = along > 0, along < n_along - 1
    paths = detours(n_down, False)
    wraps, joins = down == half, down == half - 1
    crosses, carries = lax.rem(along, 4) == 0, lax.rem(along, 4) == 3
    crossed = carries & not_last
    across = crosses & not_first
    base = n_along - 1
    index = iter(range(base, base + 64))

    def copy(source_ref, target, peer, at=None):
        at = next(index) if at is None else at
        return remote(source_ref, target, send_sems.at[at], recv_sems.at[at], peer)

    first, last = 0, layers - 1
    side = [slab.at[layer, :, :, pl.ds(0, points)] for layer in range(layers)]
    edge = [lower.at[layer, :, :, pl.ds(0, points)] for layer in range(layers)]
    rest, start = pl.ds(points, cols - points), pl.ds(0, points)
    lowers, others, rights, corners = [], [], [], []
    for layer in range(layers):
        lowers.append(copy(slab.at[layer, :, pl.ds(0, points), start], lower.at[layer, :, :, start], above))
        others.append(copy(slab.at[layer, :, pl.ds(0, points), rest], lower.at[layer, :, :, rest], above))
        rights.append(copy(side[layer], right.at[layer], left))
        corners.append(copy(edge[layer], corner.at[layer], left))
    at_right, at_corner = base + 4 * last + 2, base + 4 * last + 3
    right_hop = copy(side[last], right_relay.at[:, pl.ds(0, rows), :], ring(0, 3))
    right_forward = copy(right_relay.at[:, pl.ds(0, rows), :], right.at[last], ring(0, -4), at_right)
    corner_hop = copy(edge[last], right_relay.at[:, pl.ds(rows, points), :], ring(0, 3))
    corner_forward = copy(right_relay.at[:, pl.ds(rows, points), :], corner.at[last], ring(0, -4), at_corner)

    chunk = points // HOPS
    routes = []
    at = base + 4 * layers + 2
    for number, (path, layer, lanes) in enumerate(zip(paths, (last, first, last), (start, rest, rest))):
        pieces = [pl.ds(piece * chunk, chunk) for piece in range(HOPS)]
        routes.append(detour(
            path, along, [slab.at[layer, :, piece, lanes] for piece in pieces], [lower.at[layer, :, piece, lanes] for piece in pieces],
            lower_relay.at[number], send_sems, recv_sems, at))
        at += HOPS * (len(path) - 1)
    ahead = (lowers[first], lowers[last], others[first], others[last])
    when(not_top, lowers[first].start)
    for go in ahead[1:]:
        when(not_top & ~wraps, go.start)
    when(across, right_hop.start)
    when(not_first & ~crosses, rights[last].start)
    when(not_first, rights[first].start)
    load.wait()
    sends = []

    def send_frames(steps):
        for step in steps:
            peer, other = frame_peer(down, along, n_down, n_along, FRAME_STEPS[step], True)
            picked[step] = held[source[other * n_along + peer[1]]]
            send = remote(picked.at[step], arrived.at[along], send_sems.at[step], recv_sems.at[step], peer)
            send.start()
            sends.append(send)

    send_frames(range(EARLY_FRAMES[0]))
    for route, path in zip(routes, paths):
        set_off(route, path, down)
    picked[n_along - 1] = held[source[along]]
    own = pltpu.make_async_copy(picked.at[n_along - 1], arrived.at[along], own_sem)
    own.start()
    relays = along >= 4
    when(carries & relays, right_hop.wait_recv)
    when(carries & relays, right_forward.start)
    pass_on(routes, paths, down)
    for layer in range(layers):
        if layer == last:
            arrive(routes[:1], paths[:1], down)
            when(not_bottom & ~joins, lowers[layer].wait_recv)
        else:
            when(not_bottom, lowers[layer].wait_recv)
        if layer == last:
            when(not_bottom & across, corner_hop.start)
            when(not_bottom & not_first & ~crosses, corners[layer].start)
            when(not_bottom & carries & relays, corner_hop.wait_recv)
            when(not_bottom & carries & relays, corner_forward.start)
        else:
            when(not_bottom & not_first, corners[layer].start)
            send_frames(range(EARLY_FRAMES[0], EARLY_FRAMES[1]))
    send_frames(range(EARLY_FRAMES[1], len(FRAME_STEPS)))
    when(not_top, lowers[first].wait_send)
    for go in ahead[1:]:
        when(not_top & ~wraps, go.wait_send)
    for layer in range(layers):
        when(not_bottom & ~joins, others[layer].wait_recv)
        when(not_last, rights[layer].wait_recv)
        when(not_bottom & not_last, corners[layer].wait_recv)
        if layer == last:
            when(across, right_hop.wait_send)
            when(not_first & ~crosses, rights[layer].wait_send)
            when(carries & relays, right_forward.wait_send)
            when(not_bottom & across, corner_hop.wait_send)
            when(not_bottom & not_first & ~crosses, corners[layer].wait_send)
            when(not_bottom & carries & relays, corner_forward.wait_send)
        else:
            when(not_first, rights[layer].wait_send)
            when(not_bottom & not_first, corners[layer].wait_send)
    arrive(routes[1:], paths[1:], down)
    settle(routes, paths, down)
    for send in sends:
        send.wait()
    own.wait()


def fetch(source, frames, object_slab, points):
    layers, _, rows, cols = object_slab.shape
    n_along = lax.axis_size("tx")
    copies = n_along - 1 + 4 * layers + 2 + 8 * HOPS
    shape = lambda *dims: jax.ShapeDtypeStruct(dims, jnp.float32)
    return pl.pallas_call(
        fetch_kernel,
        out_shape=[shape(layers, 2, rows, points), shape(layers, 2, points, cols), shape(layers, 2, points, points),
                   shape(n_along, points, points)],
        in_specs=[pl.BlockSpec(memory_space=pltpu.SMEM), ANY, ANY],
        out_specs=[ANY] * 4,
        scratch_shapes=[
            pltpu.VMEM(frames.shape, jnp.float32),
            pltpu.VMEM((n_along, points, points), jnp.float32),
            pltpu.VMEM((3, HOPS, 2, points // HOPS, points), jnp.float32),
            pltpu.VMEM((2, rows + points, points), jnp.float32),
            pltpu.SemaphoreType.DMA,
            pltpu.SemaphoreType.DMA,
            pltpu.SemaphoreType.DMA((copies,)),
            pltpu.SemaphoreType.DMA((copies,)),
        ],
        compiler_params=pltpu.CompilerParams(collective_id=0, has_side_effects=True, vmem_limit_bytes=VMEM_LIMIT),
    )(source, frames, object_slab)


def return_kernel(scale, all_right, all_lower, grad_probe, probe, right_in, lower_in, probe_out,
                  corner_in, held, relay, from_row, row_sum, from_column, load_sems, send_sems, recv_sems):
    down, along = lax.axis_index("ty"), lax.axis_index("tx")
    n_down, n_along = lax.axis_size("ty"), lax.axis_size("tx")
    rights, lowers = ([ref.at[layer] for layer in range(ref.shape[0])] for ref in (all_right, all_lower))
    layers, points, rows, cols = len(rights), right_in.shape[3], right_in.shape[2], lower_in.shape[3]
    loads = [
        pltpu.make_async_copy(lowers[layer].at[:, :, pl.ds(0, points)], held.at[layer], load_sems.at[layer])
        for layer in range(layers)
    ]
    for load in loads:
        load.start()
    row_peers, column_peers = around(down, along, n_down, n_along)
    greet(row_peers + column_peers)
    part = grad_probe.shape[0] // n_along

    def piece_of(number, start):
        return pl.ds(pl.multiple_of(start + number // 2 * 8, 8), 8), pl.ds(pl.multiple_of(lax.rem(number, 2) * 128, 128), 128)

    below, after = (lax.rem(down + 1, n_down), along), (down, lax.rem(along + 1, n_along))
    not_top, not_bottom = down > 0, down < n_down - 1
    not_first, not_last = along > 0, along < n_along - 1

    def exchange(index, source, target, peer):
        copy = remote(source, target, send_sems.at[index], recv_sems.at[index], peer)
        copy.start()
        return copy

    def aligned(start, size):
        return pl.ds(pl.multiple_of(start, 8), size)

    row_copies = [
        exchange(step, grad_probe.at[aligned(peer[1] * part, part)], from_row.at[step], peer) for step, peer in enumerate(row_peers)
    ]
    base = 2 * (n_along + n_down - 2)
    corners, sides, firsts, seconds = [], [], [], []
    half = n_down // 2
    paths = detours(n_down, True)
    wraps, joins = down == half - 1, down == half
    start, rest = pl.ds(0, points), pl.ds(points, cols - points)
    for layer in range(layers):
        at = base + 4 * layer
        corners.append(remote(rights[layer].at[:, pl.ds(rows, points), :], corner_in.at[layer], send_sems.at[at], recv_sems.at[at], after))
        sides.append(remote(rights[layer].at[:, pl.ds(0, rows), :], right_in.at[layer], send_sems.at[at + 1], recv_sems.at[at + 1], after))
        firsts.append(remote(lowers[layer].at[:, :, rest], lower_in.at[layer, :, :, rest], send_sems.at[at + 2], recv_sems.at[at + 2], below))
        seconds.append(remote(held.at[layer], lower_in.at[layer, :, :, start], send_sems.at[at + 3], recv_sems.at[at + 3], below))
    first, last = 0, layers - 1
    chunk = points // HOPS
    pieces = [pl.ds(piece * chunk, chunk) for piece in range(HOPS)]
    routes = []
    at = base + 4 * layers
    straight = (half - 1, half)
    plan = ((paths[0], last, start, 0, HOPS, 0), (paths[1], first, rest, 0, 6, 1), (straight, first, rest, 6, HOPS, 1),
            (paths[2], last, rest, 0, 6, 2), (straight, last, rest, 6, HOPS, 2))
    paths = [path for path, *_ in plan]
    for path, layer, span, begin, end, number in plan:
        held_rows = held.at[layer] if number == 0 else lowers[layer].at[:, :, span]
        routes.append(detour(
            path, along, [held_rows.at[:, piece, :] for piece in pieces[begin:end]],
            [lower_in.at[layer, :, piece, span] for piece in pieces[begin:end]], relay.at[number], send_sems, recv_sems, at))
        at += (end - begin) * (len(path) - 1)
    for layer in range(layers):
        when(not_bottom & not_last, corners[layer].start)

    when(not_bottom & ~wraps, firsts[0].start)
    total = grad_probe[aligned(along * part, part)]
    for step, copy in enumerate(row_copies):
        copy.wait()
        total = total + from_row[step]
    row_sum[...] = total
    at = n_along - 1
    copies = [
        exchange(at + step, row_sum.at[piece_of(peer[0], 0)], from_column.at[step], peer)
        for step, peer in enumerate(column_peers)
    ]
    total = row_sum[piece_of(down, 0)]
    for step, copy in enumerate(copies):
        copy.wait()
        total = total + from_column[step]
    mine = piece_of(down, along * part)
    probe_out[mine] = probe[mine] - scale * total
    at += n_down - 1
    copies = [exchange(at + step, probe_out.at[mine], probe_out.at[mine], peer) for step, peer in enumerate(column_peers)]
    for layer in range(1, layers):
        when(not_bottom & ~wraps, firsts[layer].start)
    for copy in copies:
        copy.wait()
    at += n_down - 1
    mine = aligned(along * part, part)
    row_copies = [exchange(at + step, probe_out.at[mine], probe_out.at[mine], peer) for step, peer in enumerate(row_peers)]
    for route, path in zip(routes[1:], paths[1:]):
        set_off(route, path, down)
    for layer in range(layers):
        when(not_last, sides[layer].start)

    for layer in range(layers):
        loads[layer].wait()
        when(not_bottom & not_first, corners[layer].wait_recv)

        @pl.when(not_bottom & not_first)
        def _():
            held[layer] += corner_in[layer]

        if layer == last:
            set_off(routes[0], paths[0], down)
            when(not_bottom & ~wraps, seconds[layer].start)
        else:
            when(not_bottom, seconds[layer].start)
    pass_on(routes[1:], paths[1:], down)
    pass_on(routes[:1], paths[:1], down)
    for copy in row_copies:
        copy.wait()
    for layer in range(layers):
        when(not_bottom & not_last, corners[layer].wait_send)
        when(not_last, sides[layer].wait_send)
        when(not_first, sides[layer].wait_recv)
        when(not_bottom & ~wraps, firsts[layer].wait_send)
        when(not_top & ~joins, firsts[layer].wait_recv)
        if layer == last:
            when(not_bottom & ~wraps, seconds[layer].wait_send)
            when(not_top & ~joins, seconds[layer].wait_recv)
        else:
            when(not_bottom, seconds[layer].wait_send)
            when(not_top, seconds[layer].wait_recv)
    arrive(routes, paths, down)
    settle(routes, paths, down)


def send_back(grad_right, grad_lower, grad_probe, probe_wave, scale, rows):
    layers, _, points, cols = grad_lower.shape
    flat = (2 * points, points)
    n_down, n_along = lax.axis_size("ty"), lax.axis_size("tx")
    part = flat[0] // n_along
    copies = 2 * (n_along + n_down - 2) + 4 * layers + 8 * HOPS
    shape = lambda *dims: jax.ShapeDtypeStruct(dims, jnp.float32)
    right_in, lower_in, probe = pl.pallas_call(
        functools.partial(return_kernel, scale),
        out_shape=[shape(layers, 2, rows, points), shape(layers, 2, points, cols), shape(*flat)],
        in_specs=[ANY, ANY, WHOLE, WHOLE],
        out_specs=[ANY, ANY, WHOLE],
        scratch_shapes=[
            pltpu.VMEM((layers, 2, points, points), jnp.float32),
            pltpu.VMEM((layers, 2, points, points), jnp.float32),
            pltpu.VMEM((3, HOPS, 2, points // HOPS, points), jnp.float32),
            pltpu.VMEM((n_along - 1, part, points), jnp.float32),
            pltpu.VMEM((part, points), jnp.float32),
            pltpu.VMEM((n_down - 1, 8, 128), jnp.float32),
            pltpu.SemaphoreType.DMA((layers,)),
            pltpu.SemaphoreType.DMA((copies,)),
            pltpu.SemaphoreType.DMA((copies,)),
        ],
        compiler_params=pltpu.CompilerParams(collective_id=1, has_side_effects=True, vmem_limit_bytes=VMEM_LIMIT),
    )(grad_right, grad_lower, grad_probe.reshape(flat), probe_wave.reshape(flat))
    return right_in, lower_in, probe.reshape(probe_wave.shape)


def local(object_slab, probe_wave, frames, scan_tiles, scan_offsets):
    columns = lax.axis_size("tx")
    row_index = lax.axis_index("ty")
    col_index = lax.axis_index("tx")
    owned = frames.shape[0]
    points = probe_wave.shape[-1]
    layers, _, tile_rows, tile_cols = object_slab.shape
    total_frames = owned * columns
    my_tile = row_index * columns + col_index
    by_owner = scan_tiles.reshape(columns, owned)

    mine = lax.dynamic_index_in_dim(by_owner, col_index, 0, keepdims=False)
    other_row = lax.rem(row_index + lax.axis_size("ty") // 2, lax.axis_size("ty"))
    places = jnp.arange(columns, dtype=jnp.int32)
    wanted = jnp.concatenate([row_index * columns + places, other_row * columns + places])
    source = jnp.sum((mine[None, :] == wanted[:, None]).astype(jnp.int32) * jnp.arange(owned, dtype=jnp.int32)[None, :], axis=1)

    right, lower, corner, arrived = fetch(source, frames, object_slab, points)

    matches = (by_owner == my_tile).astype(jnp.int32)
    present = jnp.sum(matches, axis=1)
    ranks = jnp.cumsum(present) - 1
    slot_pick = present[None, :] * (ranks[None, :] == jnp.arange(TILE_CAP, dtype=jnp.int32)[:, None]).astype(jnp.int32)
    by_slot = lambda values: jnp.sum(slot_pick * values[None, :], axis=1)
    row_offsets, column_offsets = (
        by_slot(jnp.sum(matches * scan_offsets[:, side].reshape(columns, owned), axis=1)) for side in range(2))
    owners = by_slot(places)
    scalars = (row_offsets, column_offsets, jnp.sum(present).reshape(1), owners)

    moved, grad_right, grad_lower, grad_probe = gradients(scalars, object_slab, right, lower, corner, arrived, probe_wave)
    right_back, lower_back, new_probe = send_back(
        grad_right, grad_lower, grad_probe, probe_wave, PROBE_RATE / total_frames, object_slab.shape[2])
    return finish(moved, right_back, lower_back), new_probe


def solution(mesh):
    return jax.shard_map(
        local,
        mesh=mesh,
        in_specs=(P(None, None, "ty", "tx"), P(), P("tx", None, None), P(), P()),
        out_specs=(P(None, None, "ty", "tx"), P()),
        check_vma=False,
    )
```
